256 devices in a mesh: dp: 32 (over y, x, core), mp: 8 (over z).
Axes of the slice: x: 4, y: 4, z: 8, core: 2. Of those that a mesh axis runs over, the one named last changes fastest.
Arguments:
- hidden: bfloat16 [16384, 28672], P('dp', 'mp'), may hold values from -6 to 6
- grad_out: bfloat16 [16384, 8192], P('dp', 'mp'), may hold values from -6 to 6
- basis: bfloat16 [28672, 512], P('mp'), may hold values from -0.03125 to 0.03125
- owners: int32 [256, 1], P('mp'), may hold values from 0 to 31; in each aligned block of 32 rows (0 to 31, 32 to 63, ...) at most 4 rows name the same one
- first_moment: float32 [32768, 512], P(('dp', 'mp')), may hold values from -6 to 6
- second_moment: float32 [32768, 512], P(('dp', 'mp')), may hold values from 0.25 to 4
Outputs:
- update: bfloat16 [28672, 8192], P('mp', 'dp')
- new_first: float32 [32768, 512], P(('dp', 'mp'))
- new_second: float32 [32768, 512], P(('dp', 'mp'))
The draws below stay inside these ranges and needn't reach their ends.
Inputs may be any that keep to these rules, and one draw needn't show every extreme that they name: `owners`: among the 32 fragments of one index of mp no owner is named more than 4 times; in some of them an owner is named exactly 4 times; every owner is named somewhere.
All inputs are finite; a program needn't handle non-finite values.
Results may differ from the reference program's by a relative error of at most 0.0049.
Values may be sent and summed in bfloat16 or wider, within the bound.
No kernel may reach another device: no remote copies, remote signals or barrier semaphores. Data moves between devices by JAX's collectives and lax.ppermute only.
A program may use at most 64 MiB of HBM per device.

```python
import math
import jax
import jax.numpy as jnp
import numpy as np
from jax import lax

D = 8192
FF = 28672
RANK = 512
FC = 32
TOKENS = 16384
FRAGS_MP = 32
FRAGS = 256
SLOTS = 4
STATE_ROWS = 32768
N_DP = 32
N_MP = 8


def levels(rng, extent, split, least, high):
    def one(dim, shards_of):
        heights = jax.random.uniform(jax.random.fold_in(jax.random.fold_in(rng, 6), dim), (shards_of,), jnp.float32, least / len(split), high / len(split))
        return jnp.repeat(jnp.exp(heights), extent[dim] // shards_of).reshape((-1,) + (1,) * (len(extent) - dim - 1))

    factor_of = one(*split[0])
    for cut in split[1:]:
        factor_of = factor_of * one(*cut)
    return factor_of


def routed_block(own_key, own, number, rows, number_of, top, bound, lean):
    sequence = jax.random.permutation(own_key, number_of)
    crowded, usual = load_shares(number_of, rows * top, bound, lean, True), load_shares(number_of, rows * top, bound, lean, False)
    places = jnp.arange(number_of)

    def named(lengths, offset_by):
        used = int((lengths > 0).sum())
        fixed = max(1, used // 4)
        moved = fixed + (places - fixed + offset_by * (used - fixed)) % max(1, number_of - fixed)
        return jnp.zeros((number_of,), jnp.int32).at[sequence[jnp.where(places < fixed, places, moved)]].set(jnp.asarray(lengths, jnp.int32))

    lengths = jnp.where(number % 4 == 0, named(crowded, number // 4), named(usual, number - number // 4 - 1))
    mixed = jax.random.permutation(jax.random.fold_in(own, 3), number_of)
    giver, receiver = mixed[0:number_of // 2 * 2:2], mixed[1:number_of // 2 * 2:2]
    slack = jnp.minimum(lengths[giver] - 1, bound - lengths[receiver]) // 2
    slack = jnp.where((giver == sequence[0]) | (receiver == sequence[0]) | (lengths[receiver] == 0), 0, jnp.maximum(slack, 0))
    moved = jax.random.randint(jax.random.fold_in(own, 4), (number_of // 2,), 0, 1 << 20) % (slack + 1)
    lengths = lengths.at[giver].add(-moved).at[receiver].add(moved)
    members = jnp.searchsorted(jnp.cumsum(lengths), jnp.arange(rows * top), side="right").astype(jnp.int32)
    table = members.reshape(top, rows).T
    table = table[jax.random.permutation(jax.random.fold_in(own, 1), rows)]
    offset_by = jax.random.randint(jax.random.fold_in(own, 2), (rows, 1), 0, top)
    return jnp.take_along_axis(table, (jnp.arange(top)[None, :] + offset_by) % top, axis=1)


def load_shares(amount, total, reach, skew, full):
    portions = [(1 << 20) // math.isqrt(grade ** skew) + 1 for grade in range(1, amount + 1)]
    largest = reach if full else min(reach, max(-(-total // amount), total * portions[0] // sum(portions)))
    least = 1 if total - largest >= amount - 1 else 0
    given, rest = [largest] + [least] * (amount - 1), total - largest - least * (amount - 1)
    while rest > 0:
        free = [i for i in range(1, amount) if given[i] < largest] or [i for i in range(1, amount) if given[i] < reach]
        pool, budget = sum([portions[i] for i in free]), rest
        for i in free:
            more = min(reach - given[i], max(1, budget * portions[i] // pool), rest)
            given[i] = given[i] + more
            rest = rest - more
    return np.array(given)


def gaussian(rng, extent, width, most, shards=(), held_as=jnp.bfloat16):
    result = width * jax.random.normal(rng, extent, jnp.float32)
    if shards:
        result = result * levels(rng, extent, shards, -0.22, 0.18)
    return jnp.clip(result, -most, most).astype(held_as)


def setup_inputs(seed: int = 0) -> dict:
    arg_keys = jax.random.split(jax.random.key(seed), 7)
    hidden = gaussian(arg_keys[0], (TOKENS, FF), 1.0, 6.0, ((0, 32), (1, 8)))
    grad_out = gaussian(arg_keys[1], (TOKENS, D), 1.0, 6.0, ((0, 32), (1, 8)))
    basis = gaussian(arg_keys[2], (FF, RANK), FF ** -0.5, 0.03125, ((0, 8),))
    owners_keys = jax.random.split(jax.random.fold_in(arg_keys[3], 1), FRAGS // FRAGS_MP)
    owners_turns = jax.random.permutation(jax.random.fold_in(arg_keys[3], 3), FRAGS // FRAGS_MP)
    owners = jax.vmap(lambda own, number: routed_block(jax.random.fold_in(arg_keys[3], 2), own, number, FRAGS_MP, N_DP, 1, SLOTS, 3))(owners_keys, owners_turns).reshape((FRAGS, 1))
    first_moment = gaussian(arg_keys[4], (STATE_ROWS, RANK), 1.0, 6.0, ((0, 256),), jnp.float32)
    second_moment = jnp.clip(jnp.exp(math.log(4.0) - 2.7725887 * jax.random.uniform(arg_keys[5], (STATE_ROWS, RANK), jnp.float32) ** levels(arg_keys[5], (STATE_ROWS, RANK), ((0, 256),), -0.2, 0.2)), 0.25, 4.0)
    return {"hidden": hidden, "grad_out": grad_out, "basis": basis, "owners": owners, "first_moment": first_moment, "second_moment": second_moment}


first_keep = 0.9
first_take = 0.1
second_keep = 0.95
second_take = 0.05
adam_eps = 1e-08

def reference(hidden, grad_out, basis, owners, first_moment, second_moment):
    coeffs = jnp.dot(hidden, basis, preferred_element_type=jnp.float32).astype(jnp.bfloat16)
    projected = jnp.dot(grad_out.T, coeffs, preferred_element_type=jnp.float32) * (1.0 / math.sqrt(TOKENS))
    owner_ids = owners[:, 0].reshape(N_MP, FRAGS_MP).astype(jnp.int32)
    frag_index = jnp.arange(FRAGS_MP, dtype=jnp.int32)
    same = owner_ids[:, None, :] == owner_ids[:, :, None]
    before = frag_index[None, None, :] < frag_index[None, :, None]
    slot = lax.optimization_barrier(jnp.sum((same & before).astype(jnp.int32), axis=2)).astype(jnp.int32)
    shard = jnp.broadcast_to(jnp.arange(N_MP, dtype=jnp.int32)[:, None], (N_MP, FRAGS_MP))
    first_view = first_moment.reshape(N_DP, N_MP, SLOTS, FC, RANK)
    second_view = second_moment.reshape(N_DP, N_MP, SLOTS, FC, RANK)
    grads = projected.reshape(N_MP, FRAGS_MP, FC, RANK)
    old_first = first_view[owner_ids, shard, slot]
    old_second = second_view[owner_ids, shard, slot]
    blend_first = first_keep * old_first + first_take * grads
    blend_second = second_keep * old_second + second_take * grads * grads
    new_first = first_view.at[owner_ids, shard, slot].set(blend_first).reshape(STATE_ROWS, RANK)
    new_second = second_view.at[owner_ids, shard, slot].set(blend_second).reshape(STATE_ROWS, RANK)
    factor = (blend_first / (jnp.sqrt(blend_second) + adam_eps)).astype(jnp.bfloat16).reshape(D, RANK)
    update = jnp.dot(basis, factor.T, preferred_element_type=jnp.float32) * math.sqrt(FF / RANK)
    return (update.astype(jnp.bfloat16), new_first, new_second)
```

```python
import math

import jax
import jax.numpy as jnp
from jax import lax
from jax.sharding import PartitionSpec as P

FF = 28672
RANK = 512
FC = 32

first_keep = 0.9
first_take = 0.1
second_keep = 0.95
second_take = 0.05
adam_eps = 1e-08

bf16 = jnp.bfloat16
f32 = jnp.float32


def body(hidden, grad_out, basis, owners, first_moment, second_moment):
    owner_count = lax.axis_size("dp")
    planes = lax.axis_size("mp")
    chips = owner_count // 2
    tok, col = grad_out.shape
    slots = first_moment.shape[0] // FC
    frags = owners.shape[0]
    block = col * planes // owner_count
    per_block = block // FC
    piece = block // chips
    pairs = col // block // 2
    scale = 1.0 / math.sqrt(tok * owner_count)
    same_core = [[2 * k + c for k in range(chips)] for c in range(2)]
    swap = [(i, i ^ 1) for i in range(owner_count)]

    def other_core(x):
        return lax.ppermute(x, "dp", swap)

    def over_chips(x):
        return lax.all_to_all(x, "dp", 0, 0, axis_index_groups=same_core, tiled=True)

    def over_planes(x):
        return lax.all_to_all(x, "mp", 0, 0, tiled=True)

    me = lax.axis_index("dp")
    core = me % 2
    chip = me // 2

    raw = jnp.concatenate([first_moment.astype(bf16), second_moment.astype(bf16)], axis=1)
    raw = jnp.concatenate([raw, other_core(raw)], axis=0)

    go = grad_out.reshape(tok, pairs, 2, block)
    go_mine = lax.dynamic_slice_in_dim(go, core, 1, 2).reshape(tok, pairs * block)
    go_theirs = lax.dynamic_slice_in_dim(go, 1 - core, 1, 2).reshape(tok, pairs * block)
    go_both = jnp.concatenate([go_mine, other_core(go_theirs)], axis=0)

    ids = owners[:, 0]
    order = jnp.arange(frags, dtype=jnp.int32)
    same = ids[None, :] == ids[:, None]
    slot_of = jnp.sum((same & (order[None, :] < order[:, None])).astype(jnp.int32), axis=1)

    k_of = jnp.arange(chips, dtype=jnp.int32)[:, None]
    p_of = jnp.arange(pairs, dtype=jnp.int32)[None, :]
    parts = FC // piece
    half = chips // per_block
    frag = (core + 2 * p_of) * per_block + k_of // half
    base = (ids % 2 != core).astype(jnp.int32) * slots * FC + slot_of * FC
    pick = (frag.reshape(-1)[:, None] == order[None, :]).astype(jnp.int32)
    start = jnp.sum(pick * base[None, :], axis=1).reshape(chips, pairs) + (k_of % half) * piece
    rows = (start[:, :, None] + jnp.arange(piece, dtype=jnp.int32)).reshape(-1)
    hot = (rows[:, None] == jnp.arange(raw.shape[0], dtype=jnp.int32)[None, :]).astype(bf16)
    moments = jnp.dot(hot, raw, preferred_element_type=f32).astype(bf16)
    moments = moments.reshape(chips, pairs * piece, 2 * RANK)

    part = jnp.dot(hidden, basis, preferred_element_type=f32).astype(bf16)
    part = over_planes(part).reshape(planes, tok // planes, RANK)
    mine = jnp.sum(part.astype(f32), axis=0).astype(bf16)
    coeffs = over_planes(jnp.broadcast_to(mine[None], part.shape).reshape(tok, RANK))
    both = jnp.concatenate([coeffs, other_core(coeffs)], axis=0)

    proj = lax.dot_general(go_both, both, (((0,), (0,)), ((), ())), preferred_element_type=f32)
    proj = (proj * scale).astype(bf16).reshape(pairs, chips, piece, RANK)
    proj = proj.transpose(1, 0, 2, 3).reshape(chips, pairs * piece, RANK)
    got = over_chips(jnp.concatenate([proj, moments], axis=2))
    grad = jnp.sum(got[:, :, :RANK].astype(f32), axis=0)
    old = []
    for p in range(pairs):
        q = (core + 2 * p) * per_block + chip // half
        from_chip = jnp.sum(jnp.where(order == q, ids, 0)) // 2
        old.append(
            lax.dynamic_slice(
                got, (from_chip, p * piece, RANK), (1, piece, 2 * RANK)
            )[0]
        )
    old = jnp.concatenate(old, axis=0).astype(f32)
    blend_first = first_keep * old[:, :RANK] + first_take * grad
    blend_second = second_keep * old[:, RANK:] + second_take * grad * grad
    factor = (blend_first / (jnp.sqrt(blend_second) + adam_eps)).astype(bf16)

    spread = over_planes(jnp.broadcast_to(factor[None], (planes, pairs * piece, RANK)))
    spread = spread.reshape(chips, piece, RANK)
    grad_bf = jnp.broadcast_to(grad.astype(bf16)[None], (chips, pairs * piece, RANK))
    last = over_chips(jnp.concatenate([spread, grad_bf], axis=1))
    chosen = last[:, :piece].reshape(block, RANK)
    update = lax.dot_general(basis, chosen, (((1,), (1,)), ((), ())), preferred_element_type=f32)
    update = (update * math.sqrt(FF / RANK)).astype(bf16)

    sums = last[:, piece:].reshape(chips * pairs * piece, RANK)
    sums = jnp.concatenate([sums, other_core(sums)], axis=0)
    key = jnp.arange(slots, dtype=jnp.int32)
    mine_slot = (ids[None, :] == me) & (slot_of[None, :] == key[:, None])
    filled = jnp.any(mine_slot, axis=1)
    source = jnp.sum(jnp.where(mine_slot, order[None, :], 0), axis=1)
    b = source // per_block
    within = jnp.arange(FC, dtype=jnp.int32)
    k = ((source % per_block) * half)[:, None] + (within // piece)[None, :]
    row = k * (pairs * piece) + ((b // 2) * piece)[:, None] + (within % piece)[None, :]
    row = row + ((b % 2 != core).astype(jnp.int32) * chips * pairs * piece)[:, None]
    row = jnp.where(filled[:, None], row, -1).reshape(-1)
    hot2 = (row[:, None] == jnp.arange(sums.shape[0], dtype=jnp.int32)[None, :]).astype(bf16)
    totals = jnp.dot(hot2, sums, preferred_element_type=f32)
    live = jnp.repeat(filled, FC)[:, None]
    new_first = jnp.where(live, first_keep * first_moment + first_take * totals, first_moment)
    new_second = jnp.where(
        live, second_keep * second_moment + second_take * totals * totals, second_moment
    )
    return (update, new_first, new_second)


def solution(mesh):
    placed = (
        P("dp", "mp"),
        P("dp", "mp"),
        P("mp", None),
        P("mp", None),
        P(("dp", "mp"), None),
        P(("dp", "mp"), None),
    )
    return jax.shard_map(
        body,
        mesh=mesh,
        in_specs=placed,
        out_specs=(P("mp", "dp"), P(("dp", "mp"), None), P(("dp", "mp"), None)),
        check_vma=False,
    )
```

```python
import math

import jax
import jax.numpy as jnp
from jax import lax
from jax.sharding import PartitionSpec as P

FF = 28672
RANK = 512
FC = 32

first_keep = 0.9
first_take = 0.1
second_keep = 0.95
second_take = 0.05
adam_eps = 1e-08

bf16 = jnp.bfloat16
f32 = jnp.float32


def over(exchange, x, *rest):
    x, rest = lax.optimization_barrier((x, rest))
    return lax.optimization_barrier((exchange(x), rest))


def body(hidden, grad_out, basis, owners, first_moment, second_moment):
    owner_count = lax.axis_size("dp")
    planes = lax.axis_size("mp")
    chips = owner_count // 2
    tok, col = grad_out.shape
    slots = first_moment.shape[0] // FC
    frags = owners.shape[0]
    block = col * planes // owner_count
    per_block = block // FC
    piece = block // chips
    pairs = col // block // 2
    half = chips // per_block
    share = pairs * piece
    scale = 1.0 / math.sqrt(tok * owner_count)
    same_core = [[2 * k + c for k in range(chips)] for c in range(2)]
    swap = [(i, i ^ 1) for i in range(owner_count)]

    def other_core(x):
        return lax.ppermute(x, "dp", swap)

    def over_chips(x):
        return lax.all_to_all(x, "dp", 0, 0, axis_index_groups=same_core, tiled=True)

    def over_planes(x):
        return lax.all_to_all(x, "mp", 0, 0, tiled=True)

    def iota(shape, dim):
        return lax.broadcasted_iota(jnp.int32, shape, dim)

    me = lax.axis_index("dp")
    core = me & 1

    raw = jnp.concatenate([first_moment.astype(bf16), second_moment.astype(bf16)], axis=1)
    raw_other = other_core(raw)

    go = grad_out.reshape(tok, pairs, 2, block)
    go_even, go_odd = (go[:, :, c].reshape(tok, pairs * block) for c in range(2))
    go_mine = jnp.where(core == 0, go_even, go_odd)
    go_other = other_core(jnp.where(core == 0, go_odd, go_even))

    part = jnp.dot(hidden, basis, preferred_element_type=f32).astype(bf16)
    part, (raw, raw_other, go_mine, go_other, owners, first_moment, second_moment, me) = over(
        over_planes, part, raw, raw_other, go_mine, go_other, owners, first_moment, second_moment, me
    )
    part = part.reshape(planes, tok // planes, RANK)
    mine = jnp.sum(part.astype(f32), axis=0).astype(bf16)
    mine = jnp.broadcast_to(mine[None], part.shape).reshape(tok, RANK)
    coeffs, (raw, raw_other, go_mine, go_other, owners, first_moment, second_moment, me) = over(
        over_planes, mine, raw, raw_other, go_mine, go_other, owners, first_moment, second_moment, me
    )
    coeffs_other = other_core(coeffs)

    core = me & 1
    chip = me >> 1
    ids = owners[:, 0]
    order = iota((frags,), 0)
    same = ids[None, :] == ids[:, None]
    slot_of = jnp.sum((same & (order[None, :] < order[:, None])).astype(jnp.int32), axis=1)

    at = iota((chips * share, 1), 0) + (me & owner_count)
    k_of, p_of, r_of = at // share, (at // piece) % pairs, at % piece
    frag = (core + 2 * p_of) * per_block + k_of // half
    base = ((ids & 1) != core).astype(jnp.int32) * (slots * FC) + slot_of * FC
    rows = jnp.sum(jnp.where(frag == order[None, :], base[None, :], 0), axis=1, keepdims=True)
    rows = rows + (k_of % half) * piece + r_of
    held = slots * FC
    hot = (rows == iota((1, 2 * held), 1)).astype(bf16)
    moments = (
        jnp.dot(hot[:, :held], raw, preferred_element_type=f32)
        + jnp.dot(hot[:, held:], raw_other, preferred_element_type=f32)
    ).astype(bf16)
    moments = moments.reshape(chips, share, 2 * RANK)

    over_tokens = (((0,), (0,)), ((), ()))
    proj = lax.dot_general(go_mine, coeffs, over_tokens, preferred_element_type=f32)
    proj = proj + lax.dot_general(go_other, coeffs_other, over_tokens, preferred_element_type=f32)
    proj = (proj * scale).astype(bf16).reshape(pairs, chips, piece, RANK)
    proj = proj.transpose(1, 0, 2, 3).reshape(chips, share, RANK)
    got, (owners, first_moment, second_moment, me) = over(
        over_chips,
        jnp.concatenate([proj, moments], axis=2),
        owners,
        first_moment,
        second_moment,
        me,
    )
    core = me & 1
    chip = me >> 1
    ids = owners[:, 0]
    order = iota((frags,), 0)
    grad = jnp.sum(got[:, :, :RANK].astype(f32), axis=0)
    at = iota((share, 1), 0) + (me & owner_count)
    frag = (core + 2 * (at // piece)) * per_block + chip // half
    sender = jnp.sum(jnp.where(frag == order[None, :], ids[None, :], 0), axis=1) >> 1
    sent = iota((chips, share, 1), 0) == sender[None, :, None]
    old = jnp.sum(jnp.where(sent, got[:, :, RANK:].astype(f32), 0.0), axis=0)
    blend_first = first_keep * old[:, :RANK] + first_take * grad
    blend_second = second_keep * old[:, RANK:] + second_take * grad * grad
    factor = (blend_first / (jnp.sqrt(blend_second) + adam_eps)).astype(bf16)

    spread, (grad, owners, first_moment, second_moment, me) = over(
        over_planes,
        jnp.broadcast_to(factor[None], (planes, share, RANK)),
        grad.astype(bf16),
        owners,
        first_moment,
        second_moment,
        me,
    )
    spread = spread.reshape(chips, piece, RANK)
    grad = jnp.broadcast_to(grad[None], (chips, share, RANK))
    last, (owners, first_moment, second_moment, me) = over(
        over_chips,
        jnp.concatenate([spread, grad], axis=1),
        owners,
        first_moment,
        second_moment,
        me,
    )
    sums = last[:, piece:].reshape(chips * share, RANK)
    sums_other = other_core(sums)
    chosen = last[:, :piece].reshape(block, RANK)
    update = lax.dot_general(basis, chosen, (((1,), (1,)), ((), ())), preferred_element_type=f32)
    update = (update * math.sqrt(FF / RANK)).astype(bf16)

    core = me & 1
    ids = owners[:, 0]
    order = iota((frags,), 0)
    same = ids[None, :] == ids[:, None]
    slot_of = jnp.sum((same & (order[None, :] < order[:, None])).astype(jnp.int32), axis=1)
    at = iota((held, 1), 0) + (me & owner_count)
    within = at % FC
    own = (ids[None, :] == me) & (slot_of[None, :] == at // FC)
    live = jnp.any(own, axis=1, keepdims=True)
    source = jnp.sum(jnp.where(own, order[None, :], 0), axis=1, keepdims=True)
    b = source // per_block
    row = ((source % per_block) * half + within // piece) * share + (b // 2) * piece + within % piece
    row = row + (b % 2 != core).astype(jnp.int32) * (chips * share)
    row = jnp.where(live, row, -1)
    hot = (row == iota((1, 2 * chips * share), 1)).astype(bf16)
    totals = jnp.dot(hot[:, : chips * share], sums, preferred_element_type=f32)
    totals = totals + jnp.dot(hot[:, chips * share :], sums_other, preferred_element_type=f32)
    new_first = jnp.where(live, first_keep * first_moment + first_take * totals, first_moment)
    new_second = jnp.where(
        live, second_keep * second_moment + second_take * totals * totals, second_moment
    )
    return (update, new_first, new_second)


def solution(mesh):
    placed = (
        P("dp", "mp"),
        P("dp", "mp"),
        P("mp", None),
        P("mp", None),
        P(("dp", "mp"), None),
        P(("dp", "mp"), None),
    )
    return jax.shard_map(
        body,
        mesh=mesh,
        in_specs=placed,
        out_specs=(P("mp", "dp"), P(("dp", "mp"), None), P(("dp", "mp"), None)),
        check_vma=False,
    )
```

```python
import functools
import math

import jax
import jax.numpy as jnp
from jax import lax
from jax.experimental import pallas as pl
from jax.experimental.pallas import tpu as pltpu
from jax.sharding import PartitionSpec as P

FF = 28672
RANK = 512
FC = 32
STEPS = 7

first_keep = 0.9
first_take = 0.1
second_keep = 0.95
second_take = 0.05
adam_eps = 1e-08

bf16 = jnp.bfloat16
f32 = jnp.float32
VMEM = pl.BlockSpec(memory_space=pltpu.VMEM)
SMEM = pl.BlockSpec(memory_space=pltpu.SMEM)


def iota(shape, dim):
    return lax.broadcasted_iota(jnp.int32, shape, dim)


def kernel_params(mib=16):
    return pltpu.CompilerParams(vmem_limit_bytes=mib * 2**20)


def plane_slots(ids_row):
    n = ids_row.shape[1]
    f0, f1 = iota((n, n), 0), iota((n, n), 1)
    ids_col = jnp.sum(jnp.where(f0 == f1, ids_row, 0), axis=1, keepdims=True)
    same = ids_col == ids_row
    return jnp.sum((same & (f0 < f1)).astype(jnp.int32), axis=0, keepdims=True)


def coeffs_kernel(
    me_ref, hidden_ref, basis_ref, go_ref, first_ref, second_ref,
    part_ref, mine_ref, other_ref, raw_ref, total,
):
    step = pl.program_id(0)

    @pl.when(step == 0)
    def _():
        total[...] = jnp.zeros_like(total)
        raw_ref[:, :RANK] = first_ref[...].astype(bf16)
        raw_ref[:, RANK:] = second_ref[...].astype(bf16)
        even = (me_ref[0] & 1) == 0
        width = go_ref.shape[1] // 4
        for p in range(2):
            low = go_ref[:, (2 * p) * width : (2 * p + 1) * width]
            high = go_ref[:, (2 * p + 1) * width : (2 * p + 2) * width]
            mine_ref[:, p * width : (p + 1) * width] = jnp.where(even, low, high)
            other_ref[:, p * width : (p + 1) * width] = jnp.where(even, high, low)

    total[...] += jnp.dot(hidden_ref[...], basis_ref[...], preferred_element_type=f32)

    @pl.when(step == STEPS - 1)
    def _():
        part_ref[...] = total[...].astype(bf16)


def coeffs_call(me, hidden, basis, go, first, second):
    tok, ff = hidden.shape
    step = ff // STEPS
    held = first.shape[0]
    whole = lambda shape: pl.BlockSpec(shape, lambda i: (0, 0))
    return pl.pallas_call(
        coeffs_kernel,
        grid=(STEPS,),
        in_specs=[
            SMEM,
            pl.BlockSpec((tok, step), lambda i: (0, i)),
            pl.BlockSpec((step, RANK), lambda i: (i, 0)),
            whole(go.shape),
            whole(first.shape),
            whole(second.shape),
        ],
        out_specs=[
            whole((tok, RANK)),
            whole((tok, go.shape[1] // 2)),
            whole((tok, go.shape[1] // 2)),
            whole((held, 2 * RANK)),
        ],
        out_shape=[
            jax.ShapeDtypeStruct((tok, RANK), bf16),
            jax.ShapeDtypeStruct((tok, go.shape[1] // 2), bf16),
            jax.ShapeDtypeStruct((tok, go.shape[1] // 2), bf16),
            jax.ShapeDtypeStruct((held, 2 * RANK), bf16),
        ],
        scratch_shapes=[pltpu.VMEM((tok, RANK), f32)],
        compiler_params=kernel_params(56),
    )(me, hidden, basis, go, first, second)


OVER_TOKENS = (((0,), (0,)), ((), ()))


def payload_kernel(
    dims, me_ref, owners_ref, raw_ref, raw_other_ref, mine_ref, co_ref, out_ref, proj_ref
):
    chips, pairs, piece, per_block, slots, _ = dims
    share = pairs * piece
    half = chips // per_block
    held = slots * FC
    core = me_ref[0] & 1
    ids_row = owners_ref[...]
    slot_row = plane_slots(ids_row)
    frags = ids_row.shape[1]
    at = iota((chips * share, 1), 0)
    k_of, p_of, r_of = at // share, (at // piece) % pairs, at % piece
    frag = (core + 2 * p_of) * per_block + k_of // half
    base = ((ids_row & 1) != core).astype(jnp.int32) * held + slot_row * FC
    rows = jnp.sum(jnp.where(frag == iota((1, frags), 1), base, 0), axis=1, keepdims=True)
    rows = rows + (k_of % half) * piece + r_of
    cols = iota((1, held), 1)
    hot = jnp.where(rows == cols, 1.0, 0.0).astype(bf16)
    hot_other = jnp.where(rows == cols + held, 1.0, 0.0).astype(bf16)
    for n in range(2):
        at_n = slice(n * RANK, (n + 1) * RANK)
        old = jnp.dot(hot, raw_ref[:, at_n], preferred_element_type=f32)
        old += jnp.dot(hot_other, raw_other_ref[:, at_n], preferred_element_type=f32)
        old = old.astype(bf16).reshape(chips, share, RANK)
        out_ref[:, (n + 1) * share : (n + 2) * share, :] = old
    proj_ref[...] = lax.dot_general(
        mine_ref[...], co_ref[...], OVER_TOKENS, preferred_element_type=f32
    )


def project_kernel(dims, other_ref, co_other_ref, proj_ref, part_ref, out_ref):
    chips, pairs, piece, _, _, scale = dims
    proj = proj_ref[...] + lax.dot_general(
        other_ref[...], co_other_ref[...], OVER_TOKENS, preferred_element_type=f32
    )
    proj = (proj * scale).astype(bf16).reshape(pairs, chips, piece, RANK)
    for p in range(pairs):
        out_ref[:, p * piece : (p + 1) * piece, :] = proj[p]


def factor_kernel(dims, me_ref, owners_ref, got_ref, factor_ref, grad_ref):
    chips, pairs, piece, per_block, _, _ = dims
    share = pairs * piece
    core = me_ref[0] & 1
    chip = me_ref[0] >> 1
    ids_row = owners_ref[...]
    at = iota((share, 1), 0)
    frag = (core + 2 * (at // piece)) * per_block + chip // (chips // per_block)
    sender = jnp.where(frag == iota((1, ids_row.shape[1]), 1), ids_row, 0)
    sender = jnp.sum(sender, axis=1, keepdims=True) >> 1
    grad = jnp.zeros((share, RANK), f32)
    first = jnp.zeros((share, RANK), f32)
    second = jnp.zeros((share, RANK), f32)
    for k in range(chips):
        sent = sender == k
        grad += got_ref[k, :share, :].astype(f32)
        first = jnp.where(sent, got_ref[k, share : 2 * share, :].astype(f32), first)
        second = jnp.where(sent, got_ref[k, 2 * share :, :].astype(f32), second)
    first = first_keep * first + first_take * grad
    second = second_keep * second + second_take * grad * grad
    factor = (first / (jnp.sqrt(second) + adam_eps)).astype(bf16)
    for m in range(factor_ref.shape[0]):
        factor_ref[m] = factor
    grad_ref[...] = grad.astype(bf16)


def update_kernel(block, piece, basis_ref, last_ref, out_ref):
    chosen = last_ref[:, :piece, :].reshape(block, RANK)
    update = lax.dot_general(
        basis_ref[...], chosen, (((1,), (1,)), ((), ())), preferred_element_type=f32
    )
    out_ref[...] = (update * math.sqrt(FF / RANK)).astype(bf16)


def update_call(basis, last, block, piece):
    rows = basis.shape[0]
    step = rows // STEPS
    return pl.pallas_call(
        functools.partial(update_kernel, block, piece),
        grid=(STEPS,),
        in_specs=[
            pl.BlockSpec((step, RANK), lambda i: (i, 0)),
            pl.BlockSpec(last.shape, lambda i: (0, 0, 0)),
        ],
        out_specs=pl.BlockSpec((step, block), lambda i: (i, 0)),
        out_shape=jax.ShapeDtypeStruct((rows, block), bf16),
        compiler_params=kernel_params(),
    )(basis, last)


def owner_kernel(
    dims, me_ref, owners_ref, first_ref, second_ref, sums_ref, sums_other_ref, first_out, second_out
):
    chips, pairs, piece, per_block, slots = dims
    share = pairs * piece
    half = chips // per_block
    me = me_ref[0]
    ids_row = owners_ref[...]
    slot_row = plane_slots(ids_row)
    frags = ids_row.shape[1]
    at = iota((slots * FC, 1), 0)
    within = at % FC
    own = (ids_row == me) & (slot_row == at // FC)
    live = jnp.sum(own.astype(jnp.int32), axis=1, keepdims=True) > 0
    source = jnp.sum(jnp.where(own, iota((1, frags), 1), 0), axis=1, keepdims=True)
    b = source // per_block
    row = ((source % per_block) * half + within // piece) * share + (b // 2) * piece + within % piece
    row = jnp.where(live, row + (b % 2 != (me & 1)).astype(jnp.int32) * (chips * share), -1)
    cols = iota((1, chips * share), 1)
    hot = jnp.where(row == cols, 1.0, 0.0).astype(bf16)
    hot_other = jnp.where(row == cols + chips * share, 1.0, 0.0).astype(bf16)
    g = jnp.dot(hot, sums_ref[...], preferred_element_type=f32)
    g += jnp.dot(hot_other, sums_other_ref[...], preferred_element_type=f32)
    first, second = first_ref[...], second_ref[...]
    first_out[...] = jnp.where(live, first_keep * first + first_take * g, first)
    second_out[...] = jnp.where(live, second_keep * second + second_take * g * g, second)


def over(exchange, x, *rest):
    x, rest = lax.optimization_barrier((x, rest))
    return lax.optimization_barrier((exchange(x), rest))


def body(hidden, grad_out, basis, owners, first_moment, second_moment):
    owner_count = lax.axis_size("dp")
    planes = lax.axis_size("mp")
    chips = owner_count // 2
    tok, col = grad_out.shape
    slots = first_moment.shape[0] // FC
    frags = owners.shape[0]
    block = col * planes // owner_count
    per_block = block // FC
    piece = block // chips
    pairs = col // block // 2
    share = pairs * piece
    scale = 1.0 / math.sqrt(tok * owner_count)
    same_core = [[2 * k + c for k in range(chips)] for c in range(2)]
    swap = [(i, i ^ 1) for i in range(owner_count)]

    def other_core(x):
        return lax.ppermute(x, "dp", swap)

    def over_chips(x):
        return lax.all_to_all(x, "dp", 0, 0, axis_index_groups=same_core, tiled=True)

    def over_planes(x):
        return lax.all_to_all(x, "mp", 0, 0, tiled=True)

    me = lax.axis_index("dp").reshape(1)
    owners = owners.reshape(1, frags)

    part, go_mine, go_theirs, raw = coeffs_call(
        me, hidden, basis, grad_out, first_moment, second_moment
    )
    raw_other = other_core(raw)
    go_other = other_core(go_theirs)

    part, (raw_other, go_other) = over(over_planes, part, raw_other, go_other)
    part = part.reshape(planes, tok // planes, RANK)
    mine = jnp.sum(part.astype(f32), axis=0).astype(bf16)
    mine = jnp.broadcast_to(mine[None], part.shape).reshape(tok, RANK)
    coeffs, (me, owners) = over(over_planes, mine, me, owners)
    coeffs_other = other_core(coeffs)

    dims = (chips, pairs, piece, per_block, slots, scale)
    payload_shape = jax.ShapeDtypeStruct((chips, 3 * share, RANK), bf16)
    payload, proj = pl.pallas_call(
        functools.partial(payload_kernel, dims),
        in_specs=[SMEM] + [VMEM] * 5,
        out_specs=[VMEM, VMEM],
        out_shape=[payload_shape, jax.ShapeDtypeStruct((pairs * block, RANK), f32)],
        compiler_params=kernel_params(),
    )(me, owners, raw, raw_other, go_mine, coeffs)
    payload = pl.pallas_call(
        functools.partial(project_kernel, dims),
        in_specs=[VMEM] * 4,
        out_specs=VMEM,
        out_shape=payload_shape,
        input_output_aliases={3: 0},
        compiler_params=kernel_params(),
    )(go_other, coeffs_other, proj, payload)
    got, (me, owners) = over(over_chips, payload, me, owners)
    factor, grad = pl.pallas_call(
        functools.partial(factor_kernel, dims),
        in_specs=[SMEM] + [VMEM] * 2,
        out_specs=[VMEM, VMEM],
        out_shape=[
            jax.ShapeDtypeStruct((planes, share, RANK), bf16),
            jax.ShapeDtypeStruct((share, RANK), bf16),
        ],
        compiler_params=kernel_params(),
    )(me, owners, got)

    spread, (grad,) = over(over_planes, factor, grad)
    spread = spread.reshape(chips, piece, RANK)
    grad = jnp.broadcast_to(grad[None], (chips, share, RANK))
    last, (me, owners, first_moment, second_moment) = over(
        over_chips,
        jnp.concatenate([spread, grad], axis=1),
        me,
        owners,
        first_moment,
        second_moment,
    )
    sums = last[:, piece:].reshape(chips * share, RANK)
    sums_other = other_core(sums)
    update = update_call(basis, last, block, piece)

    like = jax.ShapeDtypeStruct(first_moment.shape, f32)
    new_first, new_second = pl.pallas_call(
        functools.partial(owner_kernel, dims[:5]),
        in_specs=[SMEM] + [VMEM] * 5,
        out_specs=[VMEM, VMEM],
        out_shape=[like, like],
        compiler_params=kernel_params(),
    )(me, owners, first_moment, second_moment, sums, sums_other)
    return (update, new_first, new_second)


def solution(mesh):
    placed = (
        P("dp", "mp"),
        P("dp", "mp"),
        P("mp", None),
        P("mp", None),
        P(("dp", "mp"), None),
        P(("dp", "mp"), None),
    )
    return jax.shard_map(
        body,
        mesh=mesh,
        in_specs=placed,
        out_specs=(P("mp", "dp"), P(("dp", "mp"), None), P(("dp", "mp"), None)),
        check_vma=False,
    )
```

```python
import functools
import math

import jax
import jax.numpy as jnp
from jax import lax
from jax.experimental import pallas as pl
from jax.experimental.pallas import tpu as pltpu
from jax.sharding import PartitionSpec as P

FF = 28672
RANK = 512
FC = 32
STEPS = 7

first_keep = 0.9
first_take = 0.1
second_keep = 0.95
second_take = 0.05
adam_eps = 1e-08

bf16 = jnp.bfloat16
f32 = jnp.float32
VMEM = pl.BlockSpec(memory_space=pltpu.VMEM)
SMEM = pl.BlockSpec(memory_space=pltpu.SMEM)


def iota(shape, dim):
    return lax.broadcasted_iota(jnp.int32, shape, dim)


def kernel_params(mib=16):
    return pltpu.CompilerParams(vmem_limit_bytes=mib * 2**20)


def plane_slots(ids_row):
    n = ids_row.shape[1]
    f0, f1 = iota((n, n), 0), iota((n, n), 1)
    ids_col = jnp.sum(jnp.where(f0 == f1, ids_row, 0), axis=1, keepdims=True)
    same = ids_col == ids_row
    return jnp.sum((same & (f0 < f1)).astype(jnp.int32), axis=0, keepdims=True)


def coeffs_kernel(
    me_ref, hidden_ref, basis_ref, go_ref, first_ref, second_ref,
    part_ref, mine_ref, other_ref, raw_ref,
    hidden, basis, go, first, second, total, sems,
):
    step = hidden.shape[2]

    def chunk(j):
        at = slice(j * step, (j + 1) * step)
        return (
            pltpu.make_async_copy(hidden_ref.at[:, at], hidden.at[j], sems.at[2 * j]),
            pltpu.make_async_copy(basis_ref.at[at, :], basis.at[j], sems.at[2 * j + 1]),
        )

    chunks = [chunk(j) for j in range(STEPS)]
    extra = [
        pltpu.make_async_copy(first_ref, first, sems.at[2 * STEPS]),
        pltpu.make_async_copy(second_ref, second, sems.at[2 * STEPS + 1]),
        pltpu.make_async_copy(go_ref, go, sems.at[2 * STEPS + 2]),
    ]
    for copy in [c for pair in chunks for c in pair] + extra:
        copy.start()
    for j in range(STEPS):
        for copy in chunks[j]:
            copy.wait()
        term = jnp.dot(hidden[j], basis[j], preferred_element_type=f32)
        if j == 0:
            total[...] = term
        elif j < STEPS - 1:
            total[...] += term
        else:
            part_ref[...] = (total[...] + term).astype(bf16)
    for copy in extra:
        copy.wait()
    raw_ref[:, :RANK] = first[...].astype(bf16)
    raw_ref[:, RANK:] = second[...].astype(bf16)
    even = (me_ref[0] & 1) == 0
    width = go.shape[1] // 4
    for p in range(2):
        low = go[:, (2 * p) * width : (2 * p + 1) * width]
        high = go[:, (2 * p + 1) * width : (2 * p + 2) * width]
        mine_ref[:, p * width : (p + 1) * width] = jnp.where(even, low, high)
        other_ref[:, p * width : (p + 1) * width] = jnp.where(even, high, low)


def coeffs_call(me, hidden, basis, go, first, second):
    tok, ff = hidden.shape
    step = ff // STEPS
    held = first.shape[0]
    like = lambda *shape: jax.ShapeDtypeStruct(shape, bf16)
    return pl.pallas_call(
        coeffs_kernel,
        in_specs=[SMEM] + [pl.BlockSpec(memory_space=pl.ANY)] * 5,
        out_specs=[VMEM] * 4,
        out_shape=[
            like(tok, RANK),
            like(tok, go.shape[1] // 2),
            like(tok, go.shape[1] // 2),
            like(held, 2 * RANK),
        ],
        scratch_shapes=[
            pltpu.VMEM((STEPS, tok, step), bf16),
            pltpu.VMEM((STEPS, step, RANK), bf16),
            pltpu.VMEM(go.shape, bf16),
            pltpu.VMEM(first.shape, f32),
            pltpu.VMEM(second.shape, f32),
            pltpu.VMEM((tok, RANK), f32),
            pltpu.SemaphoreType.DMA((2 * STEPS + 3,)),
        ],
        compiler_params=kernel_params(56),
    )(me, hidden, basis, go, first, second)


OVER_TOKENS = (((0,), (0,)), ((), ()))


def payload_kernel(
    dims, me_ref, owners_ref, near_ref, far_ref, mine_ref, co_ref, out_ref, proj_ref
):
    chips, pairs, piece, per_block, slots, _ = dims
    share = pairs * piece
    half = chips // per_block
    held = slots * FC
    core = me_ref[0] & 1
    chip = me_ref[0] >> 1
    ids_row = owners_ref[...]
    slot_row = plane_slots(ids_row)
    frags = ids_row.shape[1]
    at = iota((chips * share, 1), 0)
    k_of, p_of, r_of = at // share, (at // piece) % pairs, at % piece
    frag = (core + 2 * p_of) * per_block + k_of // half
    base = ((ids_row & 1) != core).astype(jnp.int32) * (2 * held) + slot_row * FC
    base += ((ids_row >> 1) != chip).astype(jnp.int32) * held
    rows = jnp.sum(jnp.where(frag == iota((1, frags), 1), base, 0), axis=1, keepdims=True)
    rows = rows + (k_of % half) * piece + r_of
    cols = iota((1, 2 * held), 1)
    hot = jnp.where(rows == cols, 1.0, 0.0).astype(bf16)
    hot_far = jnp.where(rows == cols + 2 * held, 1.0, 0.0).astype(bf16)
    width = RANK // 2
    low = (chip & 1) == 0
    for n in range(2):
        near, far = (
            jnp.where(
                low,
                ref[:, 2 * n * width : (2 * n + 1) * width],
                ref[:, (2 * n + 1) * width : (2 * n + 2) * width],
            )
            for ref in (near_ref, far_ref)
        )
        old = jnp.dot(hot, near, preferred_element_type=f32)
        old += jnp.dot(hot_far, far, preferred_element_type=f32)
        old = old.astype(bf16).reshape(chips, share, width)
        out_ref[:, share:, n * width : (n + 1) * width] = old
    proj_ref[...] = lax.dot_general(
        mine_ref[...], co_ref[...], OVER_TOKENS, preferred_element_type=f32
    )


def project_kernel(dims, other_ref, co_other_ref, proj_ref, part_ref, out_ref):
    chips, pairs, piece, _, _, scale = dims
    proj = proj_ref[...] + lax.dot_general(
        other_ref[...], co_other_ref[...], OVER_TOKENS, preferred_element_type=f32
    )
    proj = (proj * scale).astype(bf16).reshape(pairs, chips, piece, RANK)
    for p in range(pairs):
        out_ref[:, p * piece : (p + 1) * piece, :] = proj[p]


def factor_kernel(dims, me_ref, owners_ref, got_ref, factor_ref, grad_ref):
    chips, pairs, piece, per_block, _, _ = dims
    share = pairs * piece
    core = me_ref[0] & 1
    chip = me_ref[0] >> 1
    ids_row = owners_ref[...]
    at = iota((share, 1), 0)
    frag = (core + 2 * (at // piece)) * per_block + chip // (chips // per_block)
    sender = jnp.where(frag == iota((1, ids_row.shape[1]), 1), ids_row, 0)
    sender = jnp.sum(sender, axis=1, keepdims=True) >> 1
    width = RANK // 2
    grad = jnp.zeros((share, RANK), f32)
    old = [jnp.zeros((share, 2 * width), f32) for _ in range(2)]
    for k in range(chips):
        grad += got_ref[k, :share, :].astype(f32)
        sent = (sender >> 1) == (k >> 1)
        old[k & 1] = jnp.where(sent, got_ref[k, share:, :].astype(f32), old[k & 1])
    first = jnp.concatenate([old[0][:, :width], old[1][:, :width]], axis=1)
    second = jnp.concatenate([old[0][:, width:], old[1][:, width:]], axis=1)
    first = first_keep * first + first_take * grad
    second = second_keep * second + second_take * grad * grad
    factor = (first / (jnp.sqrt(second) + adam_eps)).astype(bf16)
    for m in range(factor_ref.shape[0]):
        factor_ref[m] = factor
    grad_ref[...] = grad.astype(bf16)


def update_kernel(piece, basis_ref, last_ref, out_ref, done, sems):
    step, block = done.shape[1:]
    chosen = last_ref[:, :piece, :].reshape(block, RANK)
    copies = []
    for j in range(STEPS):
        at = slice(j * step, (j + 1) * step)
        update = lax.dot_general(
            basis_ref[at, :], chosen, (((1,), (1,)), ((), ())), preferred_element_type=f32
        )
        done[j] = (update * math.sqrt(FF / RANK)).astype(bf16)
        copies.append(pltpu.make_async_copy(done.at[j], out_ref.at[at, :], sems.at[j]))
        copies[-1].start()
    for copy in copies:
        copy.wait()


def update_call(basis, last, block, piece):
    rows = basis.shape[0]
    return pl.pallas_call(
        functools.partial(update_kernel, piece),
        in_specs=[VMEM, VMEM],
        out_specs=pl.BlockSpec(memory_space=pl.ANY),
        out_shape=jax.ShapeDtypeStruct((rows, block), bf16),
        scratch_shapes=[
            pltpu.VMEM((STEPS, rows // STEPS, block), bf16),
            pltpu.SemaphoreType.DMA((STEPS,)),
        ],
        compiler_params=kernel_params(),
    )(basis, last)


def owner_kernel(
    dims, me_ref, owners_ref, first_ref, second_ref, sums_ref, sums_other_ref, first_out, second_out
):
    chips, pairs, piece, per_block, slots = dims
    share = pairs * piece
    half = chips // per_block
    me = me_ref[0]
    ids_row = owners_ref[...]
    slot_row = plane_slots(ids_row)
    frags = ids_row.shape[1]
    at = iota((slots * FC, 1), 0)
    within = at % FC
    own = (ids_row == me) & (slot_row == at // FC)
    live = jnp.sum(own.astype(jnp.int32), axis=1, keepdims=True) > 0
    source = jnp.sum(jnp.where(own, iota((1, frags), 1), 0), axis=1, keepdims=True)
    b = source // per_block
    row = ((source % per_block) * half + within // piece) * share + (b // 2) * piece + within % piece
    row = jnp.where(live, row + (b % 2 != (me & 1)).astype(jnp.int32) * (chips * share), -1)
    cols = iota((1, chips * share), 1)
    hot = jnp.where(row == cols, 1.0, 0.0).astype(bf16)
    hot_other = jnp.where(row == cols + chips * share, 1.0, 0.0).astype(bf16)
    g = jnp.dot(hot, sums_ref[...], preferred_element_type=f32)
    g += jnp.dot(hot_other, sums_other_ref[...], preferred_element_type=f32)
    first, second = first_ref[...], second_ref[...]
    first_out[...] = jnp.where(live, first_keep * first + first_take * g, first)
    second_out[...] = jnp.where(live, second_keep * second + second_take * g * g, second)


def over(exchange, x, *rest):
    x, rest = lax.optimization_barrier((x, rest))
    return lax.optimization_barrier((exchange(x), rest))


def body(hidden, grad_out, basis, owners, first_moment, second_moment):
    owner_count = lax.axis_size("dp")
    planes = lax.axis_size("mp")
    chips = owner_count // 2
    tok, col = grad_out.shape
    slots = first_moment.shape[0] // FC
    frags = owners.shape[0]
    block = col * planes // owner_count
    per_block = block // FC
    piece = block // chips
    pairs = col // block // 2
    share = pairs * piece
    scale = 1.0 / math.sqrt(tok * owner_count)
    same_core = [[2 * k + c for k in range(chips)] for c in range(2)]
    swap = [(i, i ^ 1) for i in range(owner_count)]
    next_chip = [(i, i ^ 2) for i in range(owner_count)]

    def other_core(x):
        return lax.ppermute(x, "dp", swap)

    def over_chips(x):
        return lax.all_to_all(x, "dp", 0, 0, axis_index_groups=same_core, tiled=True)

    def over_planes(x):
        return lax.all_to_all(x, "mp", 0, 0, tiled=True)

    me = lax.axis_index("dp").reshape(1)
    owners = owners.reshape(1, frags)

    part, go_mine, go_theirs, raw = coeffs_call(
        me, hidden, basis, grad_out, first_moment, second_moment
    )
    go_other = other_core(go_theirs)
    near = jnp.concatenate([raw, lax.ppermute(raw, "dp", next_chip)], axis=0)

    part, _ = over(over_planes, part)
    part = part.reshape(planes, tok // planes, RANK)
    mine = jnp.sum(part.astype(f32), axis=0).astype(bf16)
    far = other_core(near)
    mine = jnp.broadcast_to(mine[None], part.shape).reshape(tok, RANK)
    coeffs, (me, owners) = over(over_planes, mine, me, owners)
    coeffs_other = other_core(coeffs)

    dims = (chips, pairs, piece, per_block, slots, scale)
    payload_shape = jax.ShapeDtypeStruct((chips, 2 * share, RANK), bf16)
    payload, proj = pl.pallas_call(
        functools.partial(payload_kernel, dims),
        in_specs=[SMEM] + [VMEM] * 5,
        out_specs=[VMEM, VMEM],
        out_shape=[payload_shape, jax.ShapeDtypeStruct((pairs * block, RANK), f32)],
        compiler_params=kernel_params(),
    )(me, owners, near, far, go_mine, coeffs)
    payload = pl.pallas_call(
        functools.partial(project_kernel, dims),
        in_specs=[VMEM] * 4,
        out_specs=VMEM,
        out_shape=payload_shape,
        input_output_aliases={3: 0},
        compiler_params=kernel_params(),
    )(go_other, coeffs_other, proj, payload)
    got, (me, owners) = over(over_chips, payload, me, owners)
    factor, grad = pl.pallas_call(
        functools.partial(factor_kernel, dims),
        in_specs=[SMEM] + [VMEM] * 2,
        out_specs=[VMEM, VMEM],
        out_shape=[
            jax.ShapeDtypeStruct((planes, share, RANK), bf16),
            jax.ShapeDtypeStruct((share, RANK), bf16),
        ],
        compiler_params=kernel_params(),
    )(me, owners, got)

    spread, (grad,) = over(over_planes, factor, grad)
    spread = spread.reshape(chips, piece, RANK)
    grad = jnp.broadcast_to(grad[None], (chips, share, RANK))
    last, (me, owners, first_moment, second_moment) = over(
        over_chips,
        jnp.concatenate([spread, grad], axis=1),
        me,
        owners,
        first_moment,
        second_moment,
    )
    sums = last[:, piece:].reshape(chips * share, RANK)
    sums_other = other_core(sums)
    update = update_call(basis, last, block, piece)

    like = jax.ShapeDtypeStruct(first_moment.shape, f32)
    new_first, new_second = pl.pallas_call(
        functools.partial(owner_kernel, dims[:5]),
        in_specs=[SMEM] + [VMEM] * 5,
        out_specs=[VMEM, VMEM],
        out_shape=[like, like],
        compiler_params=kernel_params(),
    )(me, owners, first_moment, second_moment, sums, sums_other)
    return (update, new_first, new_second)


def solution(mesh):
    placed = (
        P("dp", "mp"),
        P("dp", "mp"),
        P("mp", None),
        P("mp", None),
        P(("dp", "mp"), None),
        P(("dp", "mp"), None),
    )
    return jax.shard_map(
        body,
        mesh=mesh,
        in_specs=placed,
        out_specs=(P("mp", "dp"), P(("dp", "mp"), None), P(("dp", "mp"), None)),
        check_vma=False,
    )
```

```python
import functools
import math

import jax
import jax.numpy as jnp
from jax import lax
from jax.experimental import pallas as pl
from jax.experimental.pallas import tpu as pltpu
from jax.sharding import PartitionSpec as P

FF = 28672
RANK = 512
FC = 32
STEPS = 7
SQUARE = 4

first_keep = 0.9
first_take = 0.1
second_keep = 0.95
second_take = 0.05
adam_eps = 1e-08

bf16 = jnp.bfloat16
f32 = jnp.float32
VMEM = pl.BlockSpec(memory_space=pltpu.VMEM)
SMEM = pl.BlockSpec(memory_space=pltpu.SMEM)


def iota(shape, dim):
    return lax.broadcasted_iota(jnp.int32, shape, dim)


def kernel_params(mib=16):
    return pltpu.CompilerParams(vmem_limit_bytes=mib * 2**20)


def plane_slots(ids_row):
    n = ids_row.shape[1]
    f0, f1 = iota((n, n), 0), iota((n, n), 1)
    ids_col = jnp.sum(jnp.where(f0 == f1, ids_row, 0), axis=1, keepdims=True)
    same = ids_col == ids_row
    return jnp.sum((same & (f0 < f1)).astype(jnp.int32), axis=0, keepdims=True)


def coeffs_kernel(
    me_ref, hidden_ref, basis_ref, go_ref, first_ref, second_ref,
    part_ref, mine_ref, other_ref, raw_ref,
    hidden, basis, go, first, second, total, sems,
):
    step = hidden.shape[2]

    def chunk(j):
        at = slice(j * step, (j + 1) * step)
        return (
            pltpu.make_async_copy(hidden_ref.at[:, at], hidden.at[j], sems.at[2 * j]),
            pltpu.make_async_copy(basis_ref.at[at, :], basis.at[j], sems.at[2 * j + 1]),
        )

    chunks = [chunk(j) for j in range(STEPS)]
    extra = [
        pltpu.make_async_copy(first_ref, first, sems.at[2 * STEPS]),
        pltpu.make_async_copy(second_ref, second, sems.at[2 * STEPS + 1]),
        pltpu.make_async_copy(go_ref, go, sems.at[2 * STEPS + 2]),
    ]
    for copy in [c for pair in chunks[:2] for c in pair] + extra:
        copy.start()
    for copy in [c for pair in chunks[2:] for c in pair]:
        copy.start()
    for j in range(STEPS):
        for copy in chunks[j]:
            copy.wait()
        term = jnp.dot(hidden[j], basis[j], preferred_element_type=f32)
        if j == 0:
            total[...] = term
        elif j < STEPS - 1:
            total[...] += term
        else:
            part_ref[...] = (total[...] + term).astype(bf16)
        if j == 2:
            for copy in extra:
                copy.wait()
            raw_ref[:, :RANK] = first[...].astype(bf16)
            raw_ref[:, RANK:] = second[...].astype(bf16)
            even = (me_ref[0] & 1) == 0
            width = go.shape[1] // 4
            for p in range(2):
                low = go[:, (2 * p) * width : (2 * p + 1) * width]
                high = go[:, (2 * p + 1) * width : (2 * p + 2) * width]
                mine_ref[:, p * width : (p + 1) * width] = jnp.where(even, low, high)
                other_ref[:, p * width : (p + 1) * width] = jnp.where(even, high, low)


def coeffs_call(me, hidden, basis, go, first, second):
    tok, ff = hidden.shape
    step = ff // STEPS
    held = first.shape[0]
    like = lambda *shape: jax.ShapeDtypeStruct(shape, bf16)
    return pl.pallas_call(
        coeffs_kernel,
        in_specs=[SMEM] + [pl.BlockSpec(memory_space=pltpu.HBM)] * 5,
        out_specs=[VMEM] * 4,
        out_shape=[
            like(tok, RANK),
            like(tok, go.shape[1] // 2),
            like(tok, go.shape[1] // 2),
            like(held, 2 * RANK),
        ],
        scratch_shapes=[
            pltpu.VMEM((STEPS, tok, step), bf16),
            pltpu.VMEM((STEPS, step, RANK), bf16),
            pltpu.VMEM(go.shape, bf16),
            pltpu.VMEM(first.shape, f32),
            pltpu.VMEM(second.shape, f32),
            pltpu.VMEM((tok, RANK), f32),
            pltpu.SemaphoreType.DMA((2 * STEPS + 3,)),
        ],
        compiler_params=kernel_params(56),
    )(me, hidden, basis, go, first, second)


OVER_TOKENS = (((0,), (0,)), ((), ()))


def in_square(chip):
    return (chip & 1) + 2 * ((chip >> 2) & 1), ((chip >> 1) & 1) + 2 * (chip >> 3)


def payload_kernel(
    dims, me_ref, owners_ref, near_ref, far_ref, mine_ref, co_ref, out_ref, proj_ref
):
    chips, pairs, piece, per_block, slots, _ = dims
    share = pairs * piece
    half = chips // per_block
    held = slots * FC
    core = me_ref[0] & 1
    chip = me_ref[0] >> 1
    ids_row = owners_ref[...]
    slot_row = plane_slots(ids_row)
    frags = ids_row.shape[1]
    at = iota((chips * share, 1), 0)
    k_of, p_of, r_of = at // share, (at // piece) % pairs, at % piece
    frag = (core + 2 * p_of) * per_block + k_of // half
    base = ((ids_row & 1) != core).astype(jnp.int32) * (SQUARE * held) + slot_row * FC
    base += (in_square(ids_row >> 1)[0] ^ in_square(chip)[0]) * held
    rows = jnp.sum(jnp.where(frag == iota((1, frags), 1), base, 0), axis=1, keepdims=True)
    rows = rows + (k_of % half) * piece + r_of
    cols = iota((1, SQUARE * held), 1)
    hot = jnp.where(rows == cols, 1.0, 0.0).astype(bf16)
    hot_far = jnp.where(rows == cols + SQUARE * held, 1.0, 0.0).astype(bf16)
    width = RANK // SQUARE
    for n in range(2):
        at_n = pl.ds(pl.multiple_of(n * RANK + in_square(chip)[0] * width, 128), width)
        old = jnp.dot(hot, near_ref[:, at_n], preferred_element_type=f32)
        old += jnp.dot(hot_far, far_ref[:, at_n], preferred_element_type=f32)
        old = old.astype(bf16).reshape(chips, pairs, piece, width)
        for p in range(pairs):
            out_ref[:, share:, (2 * p + n) * width : (2 * p + n + 1) * width] = old[:, p]
    proj_ref[...] = lax.dot_general(
        mine_ref[...], co_ref[...], OVER_TOKENS, preferred_element_type=f32
    )


def project_kernel(dims, other_ref, co_other_ref, proj_ref, part_ref, out_ref):
    chips, pairs, piece, _, _, scale = dims
    proj = proj_ref[...] + lax.dot_general(
        other_ref[...], co_other_ref[...], OVER_TOKENS, preferred_element_type=f32
    )
    proj = (proj * scale).astype(bf16).reshape(pairs, chips, piece, RANK)
    for p in range(pairs):
        out_ref[:, p * piece : (p + 1) * piece, :] = proj[p]


def factor_kernel(dims, me_ref, owners_ref, got_ref, factor_ref, grad_ref):
    chips, pairs, piece, per_block, _, _ = dims
    share = pairs * piece
    core = me_ref[0] & 1
    chip = me_ref[0] >> 1
    ids_row = owners_ref[...]
    grad = jnp.zeros((share, RANK), f32)
    for k in range(chips):
        grad += got_ref[k, :share, :].astype(f32)
    width = RANK // SQUARE
    parts = []
    for p in range(pairs):
        frag = (core + 2 * p) * per_block + chip // (chips // per_block)
        sender = jnp.where(iota(ids_row.shape, 1) == frag, ids_row, 0)
        square = in_square(jnp.sum(sender, axis=1, keepdims=True) >> 1)[1]
        old = [jnp.zeros((piece, 2 * width), f32) for _ in range(SQUARE)]
        for k in range(chips):
            place, number = in_square(k)
            sent = got_ref[k, share:, 2 * p * width : (2 * p + 2) * width].astype(f32)
            old[place] = jnp.where(square == number, sent, old[place])
        parts.append(old)
    first, second = (
        jnp.concatenate(
            [
                jnp.concatenate([o[:, n * width : (n + 1) * width] for o in old], axis=1)
                for old in parts
            ],
            axis=0,
        )
        for n in range(2)
    )
    first = first_keep * first + first_take * grad
    second = second_keep * second + second_take * grad * grad
    factor = (first / (jnp.sqrt(second) + adam_eps)).astype(bf16)
    for m in range(factor_ref.shape[0]):
        factor_ref[m] = factor
    grad_ref[...] = grad.astype(bf16)


def update_kernel(piece, basis_ref, last_ref, out_ref, done, sems):
    step, block = done.shape[1:]
    chosen = last_ref[:, :piece, :].reshape(block, RANK)
    copies = []
    for j in range(STEPS):
        at = slice(j * step, (j + 1) * step)
        update = lax.dot_general(
            basis_ref[at, :], chosen, (((1,), (1,)), ((), ())), preferred_element_type=f32
        )
        done[j] = (update * math.sqrt(FF / RANK)).astype(bf16)
        copies.append(pltpu.make_async_copy(done.at[j], out_ref.at[at, :], sems.at[j]))
        copies[-1].start()
    for copy in copies:
        copy.wait()


def update_call(basis, last, block, piece):
    rows = basis.shape[0]
    return pl.pallas_call(
        functools.partial(update_kernel, piece),
        in_specs=[VMEM, VMEM],
        out_specs=pl.BlockSpec(memory_space=pl.ANY),
        out_shape=jax.ShapeDtypeStruct((rows, block), bf16),
        scratch_shapes=[
            pltpu.VMEM((STEPS, rows // STEPS, block), bf16),
            pltpu.SemaphoreType.DMA((STEPS,)),
        ],
        compiler_params=kernel_params(),
    )(basis, last)


def owner_kernel(
    dims, me_ref, owners_ref, first_ref, second_ref, sums_ref, sums_other_ref, first_out, second_out
):
    chips, pairs, piece, per_block, slots = dims
    share = pairs * piece
    half = chips // per_block
    me = me_ref[0]
    ids_row = owners_ref[...]
    slot_row = plane_slots(ids_row)
    frags = ids_row.shape[1]
    at = iota((slots * FC, 1), 0)
    within = at % FC
    own = (ids_row == me) & (slot_row == at // FC)
    live = jnp.sum(own.astype(jnp.int32), axis=1, keepdims=True) > 0
    source = jnp.sum(jnp.where(own, iota((1, frags), 1), 0), axis=1, keepdims=True)
    b = source // per_block
    row = ((source % per_block) * half + within // piece) * share + (b // 2) * piece + within % piece
    row = jnp.where(live, row + (b % 2 != (me & 1)).astype(jnp.int32) * (chips * share), -1)
    cols = iota((1, chips * share), 1)
    hot = jnp.where(row == cols, 1.0, 0.0).astype(bf16)
    hot_other = jnp.where(row == cols + chips * share, 1.0, 0.0).astype(bf16)
    g = jnp.dot(hot, sums_ref[...], preferred_element_type=f32)
    g += jnp.dot(hot_other, sums_other_ref[...], preferred_element_type=f32)
    first, second = first_ref[...], second_ref[...]
    first_out[...] = jnp.where(live, first_keep * first + first_take * g, first)
    second_out[...] = jnp.where(live, second_keep * second + second_take * g * g, second)


def over(exchange, x, *rest):
    x, rest = lax.optimization_barrier((x, rest))
    return lax.optimization_barrier((exchange(x), rest))


def body(hidden, grad_out, basis, owners, first_moment, second_moment):
    owner_count = lax.axis_size("dp")
    planes = lax.axis_size("mp")
    chips = owner_count // 2
    tok, col = grad_out.shape
    slots = first_moment.shape[0] // FC
    frags = owners.shape[0]
    block = col * planes // owner_count
    per_block = block // FC
    piece = block // chips
    pairs = col // block // 2
    share = pairs * piece
    scale = 1.0 / math.sqrt(tok * owner_count)
    same_core = [[2 * k + c for k in range(chips)] for c in range(2)]
    swap = [(i, i ^ 1) for i in range(owner_count)]
    next_x = [(i, i ^ 2) for i in range(owner_count)]
    next_y = [(i, i ^ 8) for i in range(owner_count)]

    def other_core(x):
        return lax.ppermute(x, "dp", swap)

    def over_chips(x):
        return lax.all_to_all(x, "dp", 0, 0, axis_index_groups=same_core, tiled=True)

    def over_planes(x):
        return lax.all_to_all(x, "mp", 0, 0, tiled=True)

    me = lax.axis_index("dp").reshape(1)
    owners = owners.reshape(1, frags)

    part, go_mine, go_theirs, raw = coeffs_call(
        me, hidden, basis, grad_out, first_moment, second_moment
    )
    part, go_theirs, raw = lax.optimization_barrier((part, go_theirs, raw))

    part = over_planes(part)
    near = jnp.concatenate([raw, lax.ppermute(raw, "dp", next_x)], axis=0)
    near = jnp.concatenate([near, lax.ppermute(near, "dp", next_y)], axis=0)
    go_other = other_core(go_theirs)
    part, near, go_other = lax.optimization_barrier((part, near, go_other))
    part = part.reshape(planes, tok // planes, RANK)
    mine = jnp.sum(part.astype(f32), axis=0).astype(bf16)
    mine = jnp.broadcast_to(mine[None], part.shape).reshape(tok, RANK)
    mine, near, me, owners = lax.optimization_barrier((mine, near, me, owners))
    coeffs = over_planes(mine)
    far = other_core(near)
    coeffs, near, far, me, owners = lax.optimization_barrier((coeffs, near, far, me, owners))
    coeffs_other = other_core(coeffs)

    dims = (chips, pairs, piece, per_block, slots, scale)
    payload_shape = jax.ShapeDtypeStruct((chips, share + piece, RANK), bf16)
    payload, proj = pl.pallas_call(
        functools.partial(payload_kernel, dims),
        in_specs=[SMEM] + [VMEM] * 5,
        out_specs=[VMEM, VMEM],
        out_shape=[payload_shape, jax.ShapeDtypeStruct((pairs * block, RANK), f32)],
        compiler_params=kernel_params(),
    )(me, owners, near, far, go_mine, coeffs)
    payload = pl.pallas_call(
        functools.partial(project_kernel, dims),
        in_specs=[VMEM] * 4,
        out_specs=VMEM,
        out_shape=payload_shape,
        input_output_aliases={3: 0},
        compiler_params=kernel_params(),
    )(go_other, coeffs_other, proj, payload)
    got, (me, owners) = over(over_chips, payload, me, owners)
    factor, grad = pl.pallas_call(
        functools.partial(factor_kernel, dims),
        in_specs=[SMEM] + [VMEM] * 2,
        out_specs=[VMEM, VMEM],
        out_shape=[
            jax.ShapeDtypeStruct((planes, share, RANK), bf16),
            jax.ShapeDtypeStruct((share, RANK), bf16),
        ],
        compiler_params=kernel_params(),
    )(me, owners, got)

    spread, (grad,) = over(over_planes, factor, grad)
    spread = spread.reshape(chips, piece, RANK)
    grad = jnp.broadcast_to(grad[None], (chips, share, RANK))
    last, (me, owners, first_moment, second_moment) = over(
        over_chips,
        jnp.concatenate([spread, grad], axis=1),
        me,
        owners,
        first_moment,
        second_moment,
    )
    sums = last[:, piece:].reshape(chips * share, RANK)
    sums_other = other_core(sums)
    update = update_call(basis, last, block, piece)

    like = jax.ShapeDtypeStruct(first_moment.shape, f32)
    new_first, new_second = pl.pallas_call(
        functools.partial(owner_kernel, dims[:5]),
        in_specs=[SMEM] + [VMEM] * 5,
        out_specs=[VMEM, VMEM],
        out_shape=[like, like],
        compiler_params=kernel_params(),
    )(me, owners, first_moment, second_moment, sums, sums_other)
    return (update, new_first, new_second)


def solution(mesh):
    placed = (
        P("dp", "mp"),
        P("dp", "mp"),
        P("mp", None),
        P("mp", None),
        P(("dp", "mp"), None),
        P(("dp", "mp"), None),
    )
    return jax.shard_map(
        body,
        mesh=mesh,
        in_specs=placed,
        out_specs=(P("mp", "dp"), P(("dp", "mp"), None), P(("dp", "mp"), None)),
        check_vma=False,
    )
```

```python
import functools
import math

import jax
import jax.numpy as jnp
from jax import lax
from jax.experimental import pallas as pl
from jax.experimental.pallas import tpu as pltpu
from jax.sharding import PartitionSpec as P

FF = 28672
RANK = 512
FC = 32
STEPS = 7
SQUARE = 4

first_keep = 0.9
first_take = 0.1
second_keep = 0.95
second_take = 0.05
adam_eps = 1e-08

bf16 = jnp.bfloat16
f32 = jnp.float32
VMEM = pl.BlockSpec(memory_space=pltpu.VMEM)
SMEM = pl.BlockSpec(memory_space=pltpu.SMEM)


def iota(shape, dim):
    return lax.broadcasted_iota(jnp.int32, shape, dim)


def kernel_params(mib=16):
    return pltpu.CompilerParams(vmem_limit_bytes=mib * 2**20)


def plane_slots(ids_row):
    n = ids_row.shape[1]
    f0, f1 = iota((n, n), 0), iota((n, n), 1)
    ids_col = jnp.sum(jnp.where(f0 == f1, ids_row, 0), axis=1, keepdims=True)
    same = ids_col == ids_row
    return jnp.sum((same & (f0 < f1)).astype(jnp.int32), axis=0, keepdims=True)


def in_square(chip):
    return (chip & 1) + 2 * ((chip >> 2) & 1), ((chip >> 1) & 1) + 2 * (chip >> 3)


def coeffs_kernel(
    me_ref, hidden_ref, basis_ref, go_ref, first_ref, second_ref,
    part_ref, mine_ref, other_ref, keep_ref, send_ref,
    hidden, basis, go, first, second, total, sems,
):
    step = hidden.shape[2]

    def chunk(j):
        at = slice(j * step, (j + 1) * step)
        return (
            pltpu.make_async_copy(hidden_ref.at[:, at], hidden.at[j], sems.at[2 * j]),
            pltpu.make_async_copy(basis_ref.at[at, :], basis.at[j], sems.at[2 * j + 1]),
        )

    chunks = [chunk(j) for j in range(STEPS)]
    extra = [
        pltpu.make_async_copy(first_ref, first, sems.at[2 * STEPS]),
        pltpu.make_async_copy(second_ref, second, sems.at[2 * STEPS + 1]),
        pltpu.make_async_copy(go_ref, go, sems.at[2 * STEPS + 2]),
    ]
    for copy in [c for pair in chunks[:2] for c in pair] + extra:
        copy.start()
    for copy in [c for pair in chunks[2:] for c in pair]:
        copy.start()
    for j in range(STEPS):
        for copy in chunks[j]:
            copy.wait()
        term = jnp.dot(hidden[j], basis[j], preferred_element_type=f32)
        if j == 0:
            total[...] = term
        elif j < STEPS - 1:
            total[...] += term
        else:
            part_ref[...] = (total[...] + term).astype(bf16)
        if j == 2:
            for copy in extra:
                copy.wait()
            place = in_square(me_ref[0] >> 1)[0]
            quarter = RANK // SQUARE
            for n, ref in enumerate((first, second)):
                old = [ref[:, q * quarter : (q + 1) * quarter].astype(bf16) for q in range(SQUARE)]
                for d, out in enumerate((keep_ref, send_ref)):
                    for e in range(2):
                        at = slice((2 * e + n) * quarter, (2 * e + n + 1) * quarter)
                        q = place ^ (d + 2 * e)
                        low = jnp.where((q & 1) == 0, old[0], old[1])
                        high = jnp.where((q & 1) == 0, old[2], old[3])
                        out[:, at] = jnp.where(q < 2, low, high)
            even = (me_ref[0] & 1) == 0
            width = go.shape[1] // 4
            for p in range(2):
                low = go[:, (2 * p) * width : (2 * p + 1) * width]
                high = go[:, (2 * p + 1) * width : (2 * p + 2) * width]
                mine_ref[:, p * width : (p + 1) * width] = jnp.where(even, low, high)
                other_ref[:, p * width : (p + 1) * width] = jnp.where(even, high, low)


def coeffs_call(me, hidden, basis, go, first, second):
    tok, ff = hidden.shape
    step = ff // STEPS
    held = first.shape[0]
    like = lambda *shape: jax.ShapeDtypeStruct(shape, bf16)
    return pl.pallas_call(
        coeffs_kernel,
        in_specs=[SMEM] + [pl.BlockSpec(memory_space=pltpu.HBM)] * 5,
        out_specs=[VMEM] * 5,
        out_shape=[
            like(tok, RANK),
            like(tok, go.shape[1] // 2),
            like(tok, go.shape[1] // 2),
            like(held, RANK),
            like(held, RANK),
        ],
        scratch_shapes=[
            pltpu.VMEM((STEPS, tok, step), bf16),
            pltpu.VMEM((STEPS, step, RANK), bf16),
            pltpu.VMEM(go.shape, bf16),
            pltpu.VMEM(first.shape, f32),
            pltpu.VMEM(second.shape, f32),
            pltpu.VMEM((tok, RANK), f32),
            pltpu.SemaphoreType.DMA((2 * STEPS + 3,)),
        ],
        compiler_params=kernel_params(56),
    )(me, hidden, basis, go, first, second)


OVER_TOKENS = (((0,), (0,)), ((), ()))


def payload_kernel(
    dims, me_ref, owners_ref, near_ref, far_ref, mine_ref, co_ref, out_ref, proj_ref
):
    chips, pairs, piece, per_block, slots, _ = dims
    share = pairs * piece
    half = chips // per_block
    held = slots * FC
    core = me_ref[0] & 1
    chip = me_ref[0] >> 1
    ids_row = owners_ref[...]
    slot_row = plane_slots(ids_row)
    frags = ids_row.shape[1]
    at = iota((chips * share, 1), 0)
    k_of, p_of, r_of = at // share, (at // piece) % pairs, at % piece
    frag = (core + 2 * p_of) * per_block + k_of // half
    base = ((ids_row & 1) != core).astype(jnp.int32) * (SQUARE * held) + slot_row * FC
    base += (in_square(ids_row >> 1)[0] ^ in_square(chip)[0]) * held
    rows = jnp.sum(jnp.where(frag == iota((1, frags), 1), base, 0), axis=1, keepdims=True)
    rows = rows + (k_of % half) * piece + r_of
    cols = iota((1, SQUARE * held), 1)
    hot = jnp.where(rows == cols, 1.0, 0.0).astype(bf16)
    hot_far = jnp.where(rows == cols + SQUARE * held, 1.0, 0.0).astype(bf16)
    old = jnp.dot(hot, near_ref[...], preferred_element_type=f32)
    old += jnp.dot(hot_far, far_ref[...], preferred_element_type=f32)
    old = old.astype(bf16).reshape(chips, pairs, piece, near_ref.shape[1])
    for p in range(pairs):
        out_ref[:, share:, p * old.shape[3] : (p + 1) * old.shape[3]] = old[:, p]
    proj_ref[...] = lax.dot_general(
        mine_ref[...], co_ref[...], OVER_TOKENS, preferred_element_type=f32
    )


def project_kernel(dims, other_ref, co_other_ref, proj_ref, part_ref, out_ref):
    chips, pairs, piece, _, _, scale = dims
    proj = proj_ref[...] + lax.dot_general(
        other_ref[...], co_other_ref[...], OVER_TOKENS, preferred_element_type=f32
    )
    proj = (proj * scale).astype(bf16).reshape(pairs, chips, piece, RANK)
    for p in range(pairs):
        out_ref[:, p * piece : (p + 1) * piece, :] = proj[p]


def factor_kernel(dims, me_ref, owners_ref, got_ref, factor_ref, grad_ref):
    chips, pairs, piece, per_block, _, _ = dims
    share = pairs * piece
    core = me_ref[0] & 1
    chip = me_ref[0] >> 1
    ids_row = owners_ref[...]
    grad = jnp.zeros((share, RANK), f32)
    for k in range(chips):
        grad += got_ref[k, :share, :].astype(f32)
    width = RANK // SQUARE
    parts = []
    for p in range(pairs):
        frag = (core + 2 * p) * per_block + chip // (chips // per_block)
        sender = jnp.where(iota(ids_row.shape, 1) == frag, ids_row, 0)
        square = in_square(jnp.sum(sender, axis=1, keepdims=True) >> 1)[1]
        old = [jnp.zeros((piece, 2 * width), f32) for _ in range(SQUARE)]
        for k in range(chips):
            place, number = in_square(k)
            sent = got_ref[k, share:, 2 * p * width : (2 * p + 2) * width].astype(f32)
            old[place] = jnp.where(square == number, sent, old[place])
        parts.append(old)
    first, second = (
        jnp.concatenate(
            [
                jnp.concatenate([o[:, n * width : (n + 1) * width] for o in old], axis=1)
                for old in parts
            ],
            axis=0,
        )
        for n in range(2)
    )
    first = first_keep * first + first_take * grad
    second = second_keep * second + second_take * grad * grad
    factor = (first / (jnp.sqrt(second) + adam_eps)).astype(bf16)
    for m in range(factor_ref.shape[0]):
        factor_ref[m] = factor
    grad_ref[...] = grad.astype(bf16)


def update_kernel(piece, basis_ref, last_ref, out_ref, done, sems):
    step, block = done.shape[1:]
    chosen = last_ref[:, :piece, :].reshape(block, RANK)
    copies = []
    for j in range(STEPS):
        at = slice(j * step, (j + 1) * step)
        update = lax.dot_general(
            basis_ref[at, :], chosen, (((1,), (1,)), ((), ())), preferred_element_type=f32
        )
        done[j] = (update * math.sqrt(FF / RANK)).astype(bf16)
        copies.append(pltpu.make_async_copy(done.at[j], out_ref.at[at, :], sems.at[j]))
        copies[-1].start()
    for copy in copies:
        copy.wait()


def update_call(basis, last, block, piece):
    rows = basis.shape[0]
    return pl.pallas_call(
        functools.partial(update_kernel, piece),
        in_specs=[VMEM, VMEM],
        out_specs=pl.BlockSpec(memory_space=pl.ANY),
        out_shape=jax.ShapeDtypeStruct((rows, block), bf16),
        scratch_shapes=[
            pltpu.VMEM((STEPS, rows // STEPS, block), bf16),
            pltpu.SemaphoreType.DMA((STEPS,)),
        ],
        compiler_params=kernel_params(),
    )(basis, last)


def owner_kernel(
    dims, me_ref, owners_ref, first_ref, second_ref, sums_ref, sums_other_ref, first_out, second_out
):
    chips, pairs, piece, per_block, slots = dims
    share = pairs * piece
    half = chips // per_block
    me = me_ref[0]
    ids_row = owners_ref[...]
    slot_row = plane_slots(ids_row)
    frags = ids_row.shape[1]
    at = iota((slots * FC, 1), 0)
    within = at % FC
    own = (ids_row == me) & (slot_row == at // FC)
    live = jnp.sum(own.astype(jnp.int32), axis=1, keepdims=True) > 0
    source = jnp.sum(jnp.where(own, iota((1, frags), 1), 0), axis=1, keepdims=True)
    b = source // per_block
    row = ((source % per_block) * half + within // piece) * share + (b // 2) * piece + within % piece
    row = jnp.where(live, row + (b % 2 != (me & 1)).astype(jnp.int32) * (chips * share), -1)
    cols = iota((1, chips * share), 1)
    hot = jnp.where(row == cols, 1.0, 0.0).astype(bf16)
    hot_other = jnp.where(row == cols + chips * share, 1.0, 0.0).astype(bf16)
    g = jnp.dot(hot, sums_ref[...], preferred_element_type=f32)
    g += jnp.dot(hot_other, sums_other_ref[...], preferred_element_type=f32)
    first, second = first_ref[...], second_ref[...]
    first_out[...] = jnp.where(live, first_keep * first + first_take * g, first)
    second_out[...] = jnp.where(live, second_keep * second + second_take * g * g, second)


def over(exchange, x, *rest):
    x, rest = lax.optimization_barrier((x, rest))
    return lax.optimization_barrier((exchange(x), rest))


def body(hidden, grad_out, basis, owners, first_moment, second_moment):
    owner_count = lax.axis_size("dp")
    planes = lax.axis_size("mp")
    chips = owner_count // 2
    tok, col = grad_out.shape
    slots = first_moment.shape[0] // FC
    frags = owners.shape[0]
    block = col * planes // owner_count
    per_block = block // FC
    piece = block // chips
    pairs = col // block // 2
    share = pairs * piece
    scale = 1.0 / math.sqrt(tok * owner_count)
    same_core = [[2 * k + c for k in range(chips)] for c in range(2)]
    swap = [(i, i ^ 1) for i in range(owner_count)]
    next_x = [(i, i ^ 2) for i in range(owner_count)]
    next_y = [(i, i ^ 8) for i in range(owner_count)]

    def other_core(x):
        return lax.ppermute(x, "dp", swap)

    def over_chips(x):
        return lax.all_to_all(x, "dp", 0, 0, axis_index_groups=same_core, tiled=True)

    def over_planes(x):
        return lax.all_to_all(x, "mp", 0, 0, tiled=True)

    me = lax.axis_index("dp").reshape(1)
    owners = owners.reshape(1, frags)

    part, go_mine, go_theirs, keep, send = coeffs_call(
        me, hidden, basis, grad_out, first_moment, second_moment
    )
    part, go_theirs, keep, send = lax.optimization_barrier((part, go_theirs, keep, send))

    part = over_planes(part)
    near = jnp.concatenate([keep, lax.ppermute(send, "dp", next_x)], axis=0)
    keep, send = near[:, : RANK // 2], near[:, RANK // 2 :]
    near = jnp.concatenate([keep, lax.ppermute(send, "dp", next_y)], axis=0)
    go_other = other_core(go_theirs)
    part, near, go_other = lax.optimization_barrier((part, near, go_other))
    part = part.reshape(planes, tok // planes, RANK)
    mine = jnp.sum(part.astype(f32), axis=0).astype(bf16)
    mine = jnp.broadcast_to(mine[None], part.shape).reshape(tok, RANK)
    mine, near, me, owners = lax.optimization_barrier((mine, near, me, owners))
    coeffs = over_planes(mine)
    far = other_core(near)
    coeffs, near, far, me, owners = lax.optimization_barrier((coeffs, near, far, me, owners))
    coeffs_other = other_core(coeffs)

    dims = (chips, pairs, piece, per_block, slots, scale)
    payload_shape = jax.ShapeDtypeStruct((chips, share + piece, RANK), bf16)
    payload, proj = pl.pallas_call(
        functools.partial(payload_kernel, dims),
        in_specs=[SMEM] + [VMEM] * 5,
        out_specs=[VMEM, VMEM],
        out_shape=[payload_shape, jax.ShapeDtypeStruct((pairs * block, RANK), f32)],
        compiler_params=kernel_params(),
    )(me, owners, near, far, go_mine, coeffs)
    payload = pl.pallas_call(
        functools.partial(project_kernel, dims),
        in_specs=[VMEM] * 4,
        out_specs=VMEM,
        out_shape=payload_shape,
        input_output_aliases={3: 0},
        compiler_params=kernel_params(),
    )(go_other, coeffs_other, proj, payload)
    got, (me, owners) = over(over_chips, payload, me, owners)
    factor, grad = pl.pallas_call(
        functools.partial(factor_kernel, dims),
        in_specs=[SMEM] + [VMEM] * 2,
        out_specs=[VMEM, VMEM],
        out_shape=[
            jax.ShapeDtypeStruct((planes, share, RANK), bf16),
            jax.ShapeDtypeStruct((share, RANK), bf16),
        ],
        compiler_params=kernel_params(),
    )(me, owners, got)

    spread, (grad,) = over(over_planes, factor, grad)
    spread = spread.reshape(chips, piece, RANK)
    grad = jnp.broadcast_to(grad[None], (chips, share, RANK))
    last, (me, owners, first_moment, second_moment) = over(
        over_chips,
        jnp.concatenate([spread, grad], axis=1),
        me,
        owners,
        first_moment,
        second_moment,
    )
    sums = last[:, piece:].reshape(chips * share, RANK)
    sums_other = other_core(sums)
    update = update_call(basis, last, block, piece)

    like = jax.ShapeDtypeStruct(first_moment.shape, f32)
    new_first, new_second = pl.pallas_call(
        functools.partial(owner_kernel, dims[:5]),
        in_specs=[SMEM] + [VMEM] * 5,
        out_specs=[VMEM, VMEM],
        out_shape=[like, like],
        compiler_params=kernel_params(),
    )(me, owners, first_moment, second_moment, sums, sums_other)
    return (update, new_first, new_second)


def solution(mesh):
    placed = (
        P("dp", "mp"),
        P("dp", "mp"),
        P("mp", None),
        P("mp", None),
        P(("dp", "mp"), None),
        P(("dp", "mp"), None),
    )
    return jax.shard_map(
        body,
        mesh=mesh,
        in_specs=placed,
        out_specs=(P("mp", "dp"), P(("dp", "mp"), None), P(("dp", "mp"), None)),
        check_vma=False,
    )
```

```python
import functools
import math

import jax
import jax.numpy as jnp
from jax import lax
from jax.experimental import pallas as pl
from jax.experimental.pallas import tpu as pltpu
from jax.sharding import PartitionSpec as P

FF = 28672
RANK = 512
FC = 32
STEPS = 7
SQUARE = 4

first_keep = 0.9
first_take = 0.1
second_keep = 0.95
second_take = 0.05
adam_eps = 1e-08

bf16 = jnp.bfloat16
f32 = jnp.float32
VMEM = pl.BlockSpec(memory_space=pltpu.VMEM)
SMEM = pl.BlockSpec(memory_space=pltpu.SMEM)


def iota(shape, dim):
    return lax.broadcasted_iota(jnp.int32, shape, dim)


def kernel_params(mib=16):
    return pltpu.CompilerParams(vmem_limit_bytes=mib * 2**20)


def plane_slots(ids_row):
    n = ids_row.shape[1]
    f0, f1 = iota((n, n), 0), iota((n, n), 1)
    ids_col = jnp.sum(jnp.where(f0 == f1, ids_row, 0), axis=1, keepdims=True)
    same = ids_col == ids_row
    return jnp.sum((same & (f0 < f1)).astype(jnp.int32), axis=0, keepdims=True)


def in_square(chip):
    return (chip & 1) + 2 * ((chip >> 2) & 1), ((chip >> 1) & 1) + 2 * (chip >> 3)


def coeffs_kernel(hidden_ref, basis_ref, part_ref, hidden, basis, total, sems):
    step = hidden.shape[2]

    def chunk(j):
        at = slice(j * step, (j + 1) * step)
        return (
            pltpu.make_async_copy(hidden_ref.at[:, at], hidden.at[j], sems.at[2 * j]),
            pltpu.make_async_copy(basis_ref.at[at, :], basis.at[j], sems.at[2 * j + 1]),
        )

    chunks = [chunk(j) for j in range(STEPS)]
    for pair in chunks:
        for copy in pair:
            copy.start()
    for j in range(STEPS):
        for copy in chunks[j]:
            copy.wait()
        term = jnp.dot(hidden[j], basis[j], preferred_element_type=f32)
        if j == 0:
            total[...] = term
        elif j < STEPS - 1:
            total[...] += term
        else:
            part_ref[...] = (total[...] + term).astype(bf16)


def coeffs_call(hidden, basis):
    tok, ff = hidden.shape
    step = ff // STEPS
    return pl.pallas_call(
        coeffs_kernel,
        in_specs=[pl.BlockSpec(memory_space=pl.ANY)] * 2,
        out_specs=VMEM,
        out_shape=jax.ShapeDtypeStruct((tok, RANK), bf16),
        scratch_shapes=[
            pltpu.VMEM((STEPS, tok, step), bf16),
            pltpu.VMEM((STEPS, step, RANK), bf16),
            pltpu.VMEM((tok, RANK), f32),
            pltpu.SemaphoreType.DMA((2 * STEPS,)),
        ],
        compiler_params=kernel_params(56),
    )(hidden, basis)


def sort_kernel(me_ref, go_ref, first_ref, second_ref, mine_ref, other_ref, keep_ref, send_ref):
    even = (me_ref[0] & 1) == 0
    width = go_ref.shape[1] // 4
    for p in range(2):
        low = go_ref[:, (2 * p) * width : (2 * p + 1) * width]
        high = go_ref[:, (2 * p + 1) * width : (2 * p + 2) * width]
        mine_ref[:, p * width : (p + 1) * width] = jnp.where(even, low, high)
        other_ref[:, p * width : (p + 1) * width] = jnp.where(even, high, low)
    place = in_square(me_ref[0] >> 1)[0]
    width = RANK // SQUARE
    for n, ref in enumerate((first_ref, second_ref)):
        old = [ref[:, q * width : (q + 1) * width].astype(bf16) for q in range(SQUARE)]
        for d, out in enumerate((keep_ref, send_ref)):
            for e in range(2):
                at = slice((2 * e + n) * width, (2 * e + n + 1) * width)
                q = place ^ (d + 2 * e)
                low = jnp.where((q & 1) == 0, old[0], old[1])
                high = jnp.where((q & 1) == 0, old[2], old[3])
                out[:, at] = jnp.where(q < 2, low, high)


def sort_call(me, go, first, second):
    tok, col = go.shape
    like = lambda *shape: jax.ShapeDtypeStruct(shape, bf16)
    return pl.pallas_call(
        sort_kernel,
        in_specs=[SMEM] + [VMEM] * 3,
        out_specs=[VMEM] * 4,
        out_shape=[
            like(tok, col // 2),
            like(tok, col // 2),
            like(first.shape[0], RANK),
            like(first.shape[0], RANK),
        ],
        compiler_params=kernel_params(),
        cost_estimate=pl.CostEstimate(flops=2**28, bytes_accessed=2**24, transcendentals=0),
    )(me, go, first, second)


OVER_TOKENS = (((0,), (0,)), ((), ()))


def payload_kernel(
    dims, me_ref, owners_ref, near_ref, far_ref, mine_ref, co_ref, out_ref, proj_ref
):
    chips, pairs, piece, per_block, slots, _ = dims
    share = pairs * piece
    half = chips // per_block
    held = slots * FC
    core = me_ref[0] & 1
    chip = me_ref[0] >> 1
    ids_row = owners_ref[...]
    slot_row = plane_slots(ids_row)
    frags = ids_row.shape[1]
    at = iota((chips * share, 1), 0)
    k_of, p_of, r_of = at // share, (at // piece) % pairs, at % piece
    frag = (core + 2 * p_of) * per_block + k_of // half
    base = ((ids_row & 1) != core).astype(jnp.int32) * (SQUARE * held) + slot_row * FC
    base += (in_square(ids_row >> 1)[0] ^ in_square(chip)[0]) * held
    rows = jnp.sum(jnp.where(frag == iota((1, frags), 1), base, 0), axis=1, keepdims=True)
    rows = rows + (k_of % half) * piece + r_of
    cols = iota((1, SQUARE * held), 1)
    hot = jnp.where(rows == cols, 1.0, 0.0).astype(bf16)
    hot_far = jnp.where(rows == cols + SQUARE * held, 1.0, 0.0).astype(bf16)
    old = jnp.dot(hot, near_ref[...], preferred_element_type=f32)
    old += jnp.dot(hot_far, far_ref[...], preferred_element_type=f32)
    old = old.astype(bf16).reshape(chips, pairs, piece, near_ref.shape[1])
    for p in range(pairs):
        out_ref[:, share:, p * old.shape[3] : (p + 1) * old.shape[3]] = old[:, p]
    proj_ref[...] = lax.dot_general(
        mine_ref[...], co_ref[...], OVER_TOKENS, preferred_element_type=f32
    )


def project_kernel(dims, other_ref, co_other_ref, proj_ref, part_ref, out_ref):
    chips, pairs, piece, _, _, scale = dims
    proj = proj_ref[...] + lax.dot_general(
        other_ref[...], co_other_ref[...], OVER_TOKENS, preferred_element_type=f32
    )
    proj = (proj * scale).astype(bf16).reshape(pairs, chips, piece, RANK)
    for p in range(pairs):
        out_ref[:, p * piece : (p + 1) * piece, :] = proj[p]


def factor_kernel(dims, me_ref, owners_ref, got_ref, factor_ref, grad_ref):
    chips, pairs, piece, per_block, _, _ = dims
    share = pairs * piece
    core = me_ref[0] & 1
    chip = me_ref[0] >> 1
    ids_row = owners_ref[...]
    grad = jnp.zeros((share, RANK), f32)
    for k in range(chips):
        grad += got_ref[k, :share, :].astype(f32)
    width = RANK // SQUARE
    parts = []
    for p in range(pairs):
        frag = (core + 2 * p) * per_block + chip // (chips // per_block)
        sender = jnp.where(iota(ids_row.shape, 1) == frag, ids_row, 0)
        square = in_square(jnp.sum(sender, axis=1, keepdims=True) >> 1)[1]
        old = [jnp.zeros((piece, 2 * width), f32) for _ in range(SQUARE)]
        for k in range(chips):
            place, number = in_square(k)
            sent = got_ref[k, share:, 2 * p * width : (2 * p + 2) * width].astype(f32)
            old[place] = jnp.where(square == number, sent, old[place])
        parts.append(old)
    first, second = (
        jnp.concatenate(
            [
                jnp.concatenate([o[:, n * width : (n + 1) * width] for o in old], axis=1)
                for old in parts
            ],
            axis=0,
        )
        for n in range(2)
    )
    first = first_keep * first + first_take * grad
    second = second_keep * second + second_take * grad * grad
    factor = (first / (jnp.sqrt(second) + adam_eps)).astype(bf16)
    for m in range(factor_ref.shape[0]):
        factor_ref[m] = factor
    grad_ref[...] = grad.astype(bf16)


def update_kernel(piece, basis_ref, last_ref, out_ref, done, sems):
    step, block = done.shape[1:]
    chosen = last_ref[:, :piece, :].reshape(block, RANK)
    copies = []
    for j in range(STEPS):
        at = slice(j * step, (j + 1) * step)
        update = lax.dot_general(
            basis_ref[at, :], chosen, (((1,), (1,)), ((), ())), preferred_element_type=f32
        )
        done[j] = (update * math.sqrt(FF / RANK)).astype(bf16)
        copies.append(pltpu.make_async_copy(done.at[j], out_ref.at[at, :], sems.at[j]))
        copies[-1].start()
    for copy in copies:
        copy.wait()


def update_call(basis, last, block, piece):
    rows = basis.shape[0]
    return pl.pallas_call(
        functools.partial(update_kernel, piece),
        in_specs=[VMEM, VMEM],
        out_specs=pl.BlockSpec(memory_space=pl.ANY),
        out_shape=jax.ShapeDtypeStruct((rows, block), bf16),
        scratch_shapes=[
            pltpu.VMEM((STEPS, rows // STEPS, block), bf16),
            pltpu.SemaphoreType.DMA((STEPS,)),
        ],
        compiler_params=kernel_params(),
    )(basis, last)


def owner_kernel(
    dims, me_ref, owners_ref, first_ref, second_ref, sums_ref, sums_other_ref, first_out, second_out
):
    chips, pairs, piece, per_block, slots = dims
    share = pairs * piece
    half = chips // per_block
    me = me_ref[0]
    ids_row = owners_ref[...]
    slot_row = plane_slots(ids_row)
    frags = ids_row.shape[1]
    at = iota((slots * FC, 1), 0)
    within = at % FC
    own = (ids_row == me) & (slot_row == at // FC)
    live = jnp.sum(own.astype(jnp.int32), axis=1, keepdims=True) > 0
    source = jnp.sum(jnp.where(own, iota((1, frags), 1), 0), axis=1, keepdims=True)
    b = source // per_block
    row = ((source % per_block) * half + within // piece) * share + (b // 2) * piece + within % piece
    row = jnp.where(live, row + (b % 2 != (me & 1)).astype(jnp.int32) * (chips * share), -1)
    cols = iota((1, chips * share), 1)
    hot = jnp.where(row == cols, 1.0, 0.0).astype(bf16)
    hot_other = jnp.where(row == cols + chips * share, 1.0, 0.0).astype(bf16)
    g = jnp.dot(hot, sums_ref[...], preferred_element_type=f32)
    g += jnp.dot(hot_other, sums_other_ref[...], preferred_element_type=f32)
    first, second = first_ref[...], second_ref[...]
    first_out[...] = jnp.where(live, first_keep * first + first_take * g, first)
    second_out[...] = jnp.where(live, second_keep * second + second_take * g * g, second)


def over(exchange, x, *rest):
    x, rest = lax.optimization_barrier((x, rest))
    return lax.optimization_barrier((exchange(x), rest))


def body(hidden, grad_out, basis, owners, first_moment, second_moment):
    owner_count = lax.axis_size("dp")
    planes = lax.axis_size("mp")
    chips = owner_count // 2
    tok, col = grad_out.shape
    slots = first_moment.shape[0] // FC
    frags = owners.shape[0]
    block = col * planes // owner_count
    per_block = block // FC
    piece = block // chips
    pairs = col // block // 2
    share = pairs * piece
    scale = 1.0 / math.sqrt(tok * owner_count)
    same_core = [[2 * k + c for k in range(chips)] for c in range(2)]
    swap = [(i, i ^ 1) for i in range(owner_count)]
    next_x = [(i, i ^ 2) for i in range(owner_count)]
    next_y = [(i, i ^ 8) for i in range(owner_count)]

    def other_core(x):
        return lax.ppermute(x, "dp", swap)

    def over_chips(x):
        return lax.all_to_all(x, "dp", 0, 0, axis_index_groups=same_core, tiled=True)

    def over_planes(x):
        return lax.all_to_all(x, "mp", 0, 0, tiled=True)

    me = lax.axis_index("dp").reshape(1)
    owners = owners.reshape(1, frags)

    part = coeffs_call(hidden, basis)
    part, grad_out, first, second = lax.optimization_barrier(
        (part, grad_out, first_moment, second_moment)
    )
    part = over_planes(part)
    go_mine, go_theirs, keep, send = sort_call(me, grad_out, first, second)
    go_other = other_core(go_theirs)
    near = jnp.concatenate([keep, lax.ppermute(send, "dp", next_x)], axis=0)
    keep, send = near[:, : RANK // 2], near[:, RANK // 2 :]
    near = jnp.concatenate([keep, lax.ppermute(send, "dp", next_y)], axis=0)
    far = other_core(near)
    part, near, far, go_mine, go_other = lax.optimization_barrier(
        (part, near, far, go_mine, go_other)
    )
    part = part.reshape(planes, tok // planes, RANK)
    mine = jnp.sum(part.astype(f32), axis=0).astype(bf16)
    mine = jnp.broadcast_to(mine[None], part.shape).reshape(tok, RANK)
    coeffs, (near, far, go_mine, go_other, me, owners) = over(
        over_planes, mine, near, far, go_mine, go_other, me, owners
    )
    coeffs_other = other_core(coeffs)

    dims = (chips, pairs, piece, per_block, slots, scale)
    payload_shape = jax.ShapeDtypeStruct((chips, share + piece, RANK), bf16)
    payload, proj = pl.pallas_call(
        functools.partial(payload_kernel, dims),
        in_specs=[SMEM] + [VMEM] * 5,
        out_specs=[VMEM, VMEM],
        out_shape=[payload_shape, jax.ShapeDtypeStruct((pairs * block, RANK), f32)],
        compiler_params=kernel_params(),
    )(me, owners, near, far, go_mine, coeffs)
    payload = pl.pallas_call(
        functools.partial(project_kernel, dims),
        in_specs=[VMEM] * 4,
        out_specs=VMEM,
        out_shape=payload_shape,
        input_output_aliases={3: 0},
        compiler_params=kernel_params(),
    )(go_other, coeffs_other, proj, payload)
    got, (me, owners) = over(over_chips, payload, me, owners)
    factor, grad = pl.pallas_call(
        functools.partial(factor_kernel, dims),
        in_specs=[SMEM] + [VMEM] * 2,
        out_specs=[VMEM, VMEM],
        out_shape=[
            jax.ShapeDtypeStruct((planes, share, RANK), bf16),
            jax.ShapeDtypeStruct((share, RANK), bf16),
        ],
        compiler_params=kernel_params(),
    )(me, owners, got)

    spread, (grad,) = over(over_planes, factor, grad)
    spread = spread.reshape(chips, piece, RANK)
    grad = jnp.broadcast_to(grad[None], (chips, share, RANK))
    last, (me, owners, first_moment, second_moment) = over(
        over_chips,
        jnp.concatenate([spread, grad], axis=1),
        me,
        owners,
        first_moment,
        second_moment,
    )
    sums = last[:, piece:].reshape(chips * share, RANK)
    sums_other = other_core(sums)
    update = update_call(basis, last, block, piece)

    like = jax.ShapeDtypeStruct(first_moment.shape, f32)
    new_first, new_second = pl.pallas_call(
        functools.partial(owner_kernel, dims[:5]),
        in_specs=[SMEM] + [VMEM] * 5,
        out_specs=[VMEM, VMEM],
        out_shape=[like, like],
        compiler_params=kernel_params(),
    )(me, owners, first_moment, second_moment, sums, sums_other)
    return (update, new_first, new_second)


def solution(mesh):
    placed = (
        P("dp", "mp"),
        P("dp", "mp"),
        P("mp", None),
        P("mp", None),
        P(("dp", "mp"), None),
        P(("dp", "mp"), None),
    )
    return jax.shard_map(
        body,
        mesh=mesh,
        in_specs=placed,
        out_specs=(P("mp", "dp"), P(("dp", "mp"), None), P(("dp", "mp"), None)),
        check_vma=False,
    )
```

```python
import functools
import math

import jax
import jax.numpy as jnp
from jax import lax
from jax.experimental import pallas as pl
from jax.experimental.pallas import tpu as pltpu
from jax.sharding import PartitionSpec as P

FF = 28672
RANK = 512
FC = 32
STEPS = 7
SQUARE = 4

first_keep = 0.9
first_take = 0.1
second_keep = 0.95
second_take = 0.05
adam_eps = 1e-08

bf16 = jnp.bfloat16
f32 = jnp.float32
VMEM = pl.BlockSpec(memory_space=pltpu.VMEM)
SMEM = pl.BlockSpec(memory_space=pltpu.SMEM)


def iota(shape, dim):
    return lax.broadcasted_iota(jnp.int32, shape, dim)


def kernel_params(mib=16):
    return pltpu.CompilerParams(vmem_limit_bytes=mib * 2**20)


def plane_slots(ids_row):
    n = ids_row.shape[1]
    f0, f1 = iota((n, n), 0), iota((n, n), 1)
    ids_col = jnp.sum(jnp.where(f0 == f1, ids_row, 0), axis=1, keepdims=True)
    same = ids_col == ids_row
    return jnp.sum((same & (f0 < f1)).astype(jnp.int32), axis=0, keepdims=True)


def in_square(chip):
    return (chip & 1) + 2 * ((chip >> 2) & 1), ((chip >> 1) & 1) + 2 * (chip >> 3)


def coeffs_kernel(hidden_ref, basis_ref, part_ref, hidden, basis, total, sems):
    step = hidden.shape[2]

    def chunk(j):
        at = slice(j * step, (j + 1) * step)
        return (
            pltpu.make_async_copy(hidden_ref.at[:, at], hidden.at[j], sems.at[2 * j]),
            pltpu.make_async_copy(basis_ref.at[at, :], basis.at[j], sems.at[2 * j + 1]),
        )

    chunks = [chunk(j) for j in range(STEPS)]
    for pair in chunks:
        for copy in pair:
            copy.start()
    for j in range(STEPS):
        for copy in chunks[j]:
            copy.wait()
        term = jnp.dot(hidden[j], basis[j], preferred_element_type=f32)
        if j == 0:
            total[...] = term
        elif j < STEPS - 1:
            total[...] += term
        else:
            part_ref[...] = (total[...] + term).astype(bf16)


def coeffs_call(hidden, basis):
    tok, ff = hidden.shape
    step = ff // STEPS
    return pl.pallas_call(
        coeffs_kernel,
        in_specs=[pl.BlockSpec(memory_space=pl.ANY)] * 2,
        out_specs=VMEM,
        out_shape=jax.ShapeDtypeStruct((tok, RANK), bf16),
        scratch_shapes=[
            pltpu.VMEM((STEPS, tok, step), bf16),
            pltpu.VMEM((STEPS, step, RANK), bf16),
            pltpu.VMEM((tok, RANK), f32),
            pltpu.SemaphoreType.DMA((2 * STEPS,)),
        ],
        compiler_params=kernel_params(56),
    )(hidden, basis)


def sort_kernel(me_ref, go_ref, first_ref, second_ref, mine_ref, other_ref, keep_ref, send_ref):
    even = (me_ref[0] & 1) == 0
    width = go_ref.shape[1] // 4
    for p in range(2):
        low = go_ref[:, (2 * p) * width : (2 * p + 1) * width]
        high = go_ref[:, (2 * p + 1) * width : (2 * p + 2) * width]
        mine_ref[:, p * width : (p + 1) * width] = jnp.where(even, low, high)
        other_ref[:, p * width : (p + 1) * width] = jnp.where(even, high, low)
    place = in_square(me_ref[0] >> 1)[0]
    width = RANK // SQUARE
    for n, ref in enumerate((first_ref, second_ref)):
        old = [ref[:, q * width : (q + 1) * width].astype(bf16) for q in range(SQUARE)]
        for d, out in enumerate((keep_ref, send_ref)):
            for e in range(2):
                at = slice((2 * e + n) * width, (2 * e + n + 1) * width)
                q = place ^ (d + 2 * e)
                low = jnp.where((q & 1) == 0, old[0], old[1])
                high = jnp.where((q & 1) == 0, old[2], old[3])
                out[:, at] = jnp.where(q < 2, low, high)


def sort_call(me, go, first, second):
    tok, col = go.shape
    like = lambda *shape: jax.ShapeDtypeStruct(shape, bf16)
    return pl.pallas_call(
        sort_kernel,
        in_specs=[SMEM] + [VMEM] * 3,
        out_specs=[VMEM] * 4,
        out_shape=[
            like(tok, col // 2),
            like(tok, col // 2),
            like(first.shape[0], RANK),
            like(first.shape[0], RANK),
        ],
        compiler_params=kernel_params(),
        cost_estimate=pl.CostEstimate(flops=2**28, bytes_accessed=2**24, transcendentals=0),
    )(me, go, first, second)


OVER_TOKENS = (((0,), (0,)), ((), ()))


def payload_kernel(
    dims, me_ref, owners_ref, near_ref, far_ref, mine_ref, co_ref, out_ref, proj_ref
):
    chips, pairs, piece, per_block, slots, _ = dims
    share = pairs * piece
    half = chips // per_block
    held = slots * FC
    core = me_ref[0] & 1
    chip = me_ref[0] >> 1
    ids_row = owners_ref[...]
    slot_row = plane_slots(ids_row)
    frags = ids_row.shape[1]
    at = iota((chips * share, 1), 0)
    k_of, p_of, r_of = at // share, (at // piece) % pairs, at % piece
    frag = (core + 2 * p_of) * per_block + k_of // half
    base = ((ids_row & 1) != core).astype(jnp.int32) * (SQUARE * held) + slot_row * FC
    base += (in_square(ids_row >> 1)[0] ^ in_square(chip)[0]) * held
    rows = jnp.sum(jnp.where(frag == iota((1, frags), 1), base, 0), axis=1, keepdims=True)
    rows = rows + (k_of % half) * piece + r_of
    cols = iota((1, SQUARE * held), 1)
    hot = jnp.where(rows == cols, 1.0, 0.0).astype(bf16)
    hot_far = jnp.where(rows == cols + SQUARE * held, 1.0, 0.0).astype(bf16)
    old = jnp.dot(hot, near_ref[...], preferred_element_type=f32)
    old += jnp.dot(hot_far, far_ref[...], preferred_element_type=f32)
    old = old.astype(bf16).reshape(chips, pairs, piece, near_ref.shape[1])
    for p in range(pairs):
        out_ref[:, share:, p * old.shape[3] : (p + 1) * old.shape[3]] = old[:, p]
    proj_ref[...] = lax.dot_general(
        mine_ref[...], co_ref[...], OVER_TOKENS, preferred_element_type=f32
    )


def project_kernel(dims, other_ref, co_other_ref, proj_ref, part_ref, out_ref):
    chips, pairs, piece, _, _, scale = dims
    proj = proj_ref[...] + lax.dot_general(
        other_ref[...], co_other_ref[...], OVER_TOKENS, preferred_element_type=f32
    )
    proj = (proj * scale).astype(bf16).reshape(pairs, chips, piece, RANK)
    for p in range(pairs):
        out_ref[:, p * piece : (p + 1) * piece, :] = proj[p]


def factor_kernel(dims, me_ref, owners_ref, got_ref, factor_ref, grad_ref):
    chips, pairs, piece, per_block, _, _ = dims
    share = pairs * piece
    core = me_ref[0] & 1
    chip = me_ref[0] >> 1
    ids_row = owners_ref[...]
    grad = jnp.zeros((share, RANK), f32)
    for k in range(chips):
        grad += got_ref[k, :share, :].astype(f32)
    width = RANK // SQUARE
    parts = []
    for p in range(pairs):
        frag = (core + 2 * p) * per_block + chip // (chips // per_block)
        sender = jnp.where(iota(ids_row.shape, 1) == frag, ids_row, 0)
        square = in_square(jnp.sum(sender, axis=1, keepdims=True) >> 1)[1]
        old = [jnp.zeros((piece, 2 * width), f32) for _ in range(SQUARE)]
        for k in range(chips):
            place, number = in_square(k)
            sent = got_ref[k, share:, 2 * p * width : (2 * p + 2) * width].astype(f32)
            old[place] = jnp.where(square == number, sent, old[place])
        parts.append(old)
    first, second = (
        jnp.concatenate(
            [
                jnp.concatenate([o[:, n * width : (n + 1) * width] for o in old], axis=1)
                for old in parts
            ],
            axis=0,
        )
        for n in range(2)
    )
    first = first_keep * first + first_take * grad
    second = second_keep * second + second_take * grad * grad
    factor = (first / (jnp.sqrt(second) + adam_eps)).astype(bf16)
    for m in range(factor_ref.shape[0]):
        factor_ref[m] = factor
    grad_ref[...] = grad.astype(bf16)


def update_kernel(piece, basis_ref, last_ref, out_ref, done, sems):
    step, block = done.shape[1:]
    chosen = last_ref[:, :piece, :].reshape(block, RANK)
    copies = []
    for j in range(STEPS):
        at = slice(j * step, (j + 1) * step)
        update = lax.dot_general(
            basis_ref[at, :], chosen, (((1,), (1,)), ((), ())), preferred_element_type=f32
        )
        done[j] = (update * math.sqrt(FF / RANK)).astype(bf16)
        copies.append(pltpu.make_async_copy(done.at[j], out_ref.at[at, :], sems.at[j]))
        copies[-1].start()
    for copy in copies:
        copy.wait()


def update_call(basis, last, block, piece):
    rows = basis.shape[0]
    return pl.pallas_call(
        functools.partial(update_kernel, piece),
        in_specs=[VMEM, VMEM],
        out_specs=pl.BlockSpec(memory_space=pl.ANY),
        out_shape=jax.ShapeDtypeStruct((rows, block), bf16),
        scratch_shapes=[
            pltpu.VMEM((STEPS, rows // STEPS, block), bf16),
            pltpu.SemaphoreType.DMA((STEPS,)),
        ],
        compiler_params=kernel_params(),
    )(basis, last)


def owner_kernel(
    dims, me_ref, owners_ref, first_ref, second_ref, sums_ref, sums_other_ref, first_out, second_out
):
    chips, pairs, piece, per_block, slots = dims
    share = pairs * piece
    half = chips // per_block
    me = me_ref[0]
    ids_row = owners_ref[...]
    slot_row = plane_slots(ids_row)
    frags = ids_row.shape[1]
    at = iota((slots * FC, 1), 0)
    within = at % FC
    own = (ids_row == me) & (slot_row == at // FC)
    live = jnp.sum(own.astype(jnp.int32), axis=1, keepdims=True) > 0
    source = jnp.sum(jnp.where(own, iota((1, frags), 1), 0), axis=1, keepdims=True)
    b = source // per_block
    row = ((source % per_block) * half + within // piece) * share + (b // 2) * piece + within % piece
    row = jnp.where(live, row + (b % 2 != (me & 1)).astype(jnp.int32) * (chips * share), -1)
    cols = iota((1, chips * share), 1)
    hot = jnp.where(row == cols, 1.0, 0.0).astype(bf16)
    hot_other = jnp.where(row == cols + chips * share, 1.0, 0.0).astype(bf16)
    g = jnp.dot(hot, sums_ref[...], preferred_element_type=f32)
    g += jnp.dot(hot_other, sums_other_ref[...], preferred_element_type=f32)
    first, second = first_ref[...], second_ref[...]
    first_out[...] = jnp.where(live, first_keep * first + first_take * g, first)
    second_out[...] = jnp.where(live, second_keep * second + second_take * g * g, second)


def over(exchange, x, *rest):
    x, rest = lax.optimization_barrier((x, rest))
    return lax.optimization_barrier((exchange(x), rest))


def body(hidden, grad_out, basis, owners, first_moment, second_moment):
    owner_count = lax.axis_size("dp")
    planes = lax.axis_size("mp")
    chips = owner_count // 2
    tok, col = grad_out.shape
    slots = first_moment.shape[0] // FC
    frags = owners.shape[0]
    block = col * planes // owner_count
    per_block = block // FC
    piece = block // chips
    pairs = col // block // 2
    share = pairs * piece
    scale = 1.0 / math.sqrt(tok * owner_count)
    same_core = [[2 * k + c for k in range(chips)] for c in range(2)]
    swap = [(i, i ^ 1) for i in range(owner_count)]
    next_x = [(i, i ^ 2) for i in range(owner_count)]
    next_y = [(i, i ^ 8) for i in range(owner_count)]

    def other_core(x):
        return lax.ppermute(x, "dp", swap)

    def over_chips(x):
        return lax.all_to_all(x, "dp", 0, 0, axis_index_groups=same_core, tiled=True)

    def over_planes(x):
        return lax.all_to_all(x, "mp", 0, 0, tiled=True)

    me = lax.axis_index("dp").reshape(1)
    owners = owners.reshape(1, frags)

    part = coeffs_call(hidden, basis)
    part, (me, owners, grad_out, first, second) = over(
        over_planes, part, me, owners, grad_out, first_moment, second_moment
    )
    part = part.reshape(planes, tok // planes, RANK)
    mine = jnp.sum(part.astype(f32), axis=0).astype(bf16)
    mine = jnp.broadcast_to(mine[None], part.shape).reshape(tok, RANK)
    coeffs = over_planes(mine)
    go_mine, go_theirs, keep, send = sort_call(me, grad_out, first, second)
    near = jnp.concatenate([keep, lax.ppermute(send, "dp", next_x)], axis=0)
    keep, send = near[:, : RANK // 2], near[:, RANK // 2 :]
    near = jnp.concatenate([keep, lax.ppermute(send, "dp", next_y)], axis=0)
    far = other_core(near)
    go_other = other_core(go_theirs)
    coeffs, near, far, go_mine, go_other, me, owners = lax.optimization_barrier(
        (coeffs, near, far, go_mine, go_other, me, owners)
    )
    coeffs_other = other_core(coeffs)

    dims = (chips, pairs, piece, per_block, slots, scale)
    payload_shape = jax.ShapeDtypeStruct((chips, share + piece, RANK), bf16)
    payload, proj = pl.pallas_call(
        functools.partial(payload_kernel, dims),
        in_specs=[SMEM] + [VMEM] * 5,
        out_specs=[VMEM, VMEM],
        out_shape=[payload_shape, jax.ShapeDtypeStruct((pairs * block, RANK), f32)],
        compiler_params=kernel_params(),
    )(me, owners, near, far, go_mine, coeffs)
    payload = pl.pallas_call(
        functools.partial(project_kernel, dims),
        in_specs=[VMEM] * 4,
        out_specs=VMEM,
        out_shape=payload_shape,
        input_output_aliases={3: 0},
        compiler_params=kernel_params(),
    )(go_other, coeffs_other, proj, payload)
    got, (me, owners) = over(over_chips, payload, me, owners)
    factor, grad = pl.pallas_call(
        functools.partial(factor_kernel, dims),
        in_specs=[SMEM] + [VMEM] * 2,
        out_specs=[VMEM, VMEM],
        out_shape=[
            jax.ShapeDtypeStruct((planes, share, RANK), bf16),
            jax.ShapeDtypeStruct((share, RANK), bf16),
        ],
        compiler_params=kernel_params(),
    )(me, owners, got)

    spread, (grad,) = over(over_planes, factor, grad)
    spread = spread.reshape(chips, piece, RANK)
    grad = jnp.broadcast_to(grad[None], (chips, share, RANK))
    last, (me, owners, first_moment, second_moment) = over(
        over_chips,
        jnp.concatenate([spread, grad], axis=1),
        me,
        owners,
        first_moment,
        second_moment,
    )
    sums = last[:, piece:].reshape(chips * share, RANK)
    sums_other = other_core(sums)
    update = update_call(basis, last, block, piece)

    like = jax.ShapeDtypeStruct(first_moment.shape, f32)
    new_first, new_second = pl.pallas_call(
        functools.partial(owner_kernel, dims[:5]),
        in_specs=[SMEM] + [VMEM] * 5,
        out_specs=[VMEM, VMEM],
        out_shape=[like, like],
        compiler_params=kernel_params(),
    )(me, owners, first_moment, second_moment, sums, sums_other)
    return (update, new_first, new_second)


def solution(mesh):
    placed = (
        P("dp", "mp"),
        P("dp", "mp"),
        P("mp", None),
        P("mp", None),
        P(("dp", "mp"), None),
        P(("dp", "mp"), None),
    )
    return jax.shard_map(
        body,
        mesh=mesh,
        in_specs=placed,
        out_specs=(P("mp", "dp"), P(("dp", "mp"), None), P(("dp", "mp"), None)),
        check_vma=False,
    )
```

```python
import functools
import math

import jax
import jax.numpy as jnp
from jax import lax
from jax.experimental import pallas as pl
from jax.experimental.pallas import tpu as pltpu
from jax.sharding import PartitionSpec as P

FF = 28672
RANK = 512
FC = 32
STEPS = 7
SQUARE = 4

first_keep = 0.9
first_take = 0.1
second_keep = 0.95
second_take = 0.05
adam_eps = 1e-08

bf16 = jnp.bfloat16
f32 = jnp.float32
VMEM = pl.BlockSpec(memory_space=pltpu.VMEM)
SMEM = pl.BlockSpec(memory_space=pltpu.SMEM)


def iota(shape, dim):
    return lax.broadcasted_iota(jnp.int32, shape, dim)


def kernel_params(mib=16):
    return pltpu.CompilerParams(vmem_limit_bytes=mib * 2**20)


def plane_slots(ids_row):
    n = ids_row.shape[1]
    f0, f1 = iota((n, n), 0), iota((n, n), 1)
    ids_col = jnp.sum(jnp.where(f0 == f1, ids_row, 0), axis=1, keepdims=True)
    same = ids_col == ids_row
    return jnp.sum((same & (f0 < f1)).astype(jnp.int32), axis=0, keepdims=True)


def in_square(chip):
    return (chip & 1) + 2 * ((chip >> 2) & 1), ((chip >> 1) & 1) + 2 * (chip >> 3)


def coeffs_kernel(hidden_ref, basis_ref, part_ref, hidden, basis, total, sems):
    step = hidden.shape[2]

    def chunk(j):
        at = slice(j * step, (j + 1) * step)
        return (
            pltpu.make_async_copy(hidden_ref.at[:, at], hidden.at[j], sems.at[2 * j]),
            pltpu.make_async_copy(basis_ref.at[at, :], basis.at[j], sems.at[2 * j + 1]),
        )

    chunks = [chunk(j) for j in range(STEPS)]
    for pair in chunks:
        for copy in pair:
            copy.start()
    for j in range(STEPS):
        for copy in chunks[j]:
            copy.wait()
        term = jnp.dot(hidden[j], basis[j], preferred_element_type=f32)
        if j == 0:
            total[...] = term
        elif j < STEPS - 1:
            total[...] += term
        else:
            part_ref[...] = (total[...] + term).astype(bf16)


def coeffs_call(hidden, basis):
    tok, ff = hidden.shape
    step = ff // STEPS
    return pl.pallas_call(
        coeffs_kernel,
        in_specs=[pl.BlockSpec(memory_space=pl.ANY)] * 2,
        out_specs=VMEM,
        out_shape=jax.ShapeDtypeStruct((tok, RANK), bf16),
        scratch_shapes=[
            pltpu.VMEM((STEPS, tok, step), bf16),
            pltpu.VMEM((STEPS, step, RANK), bf16),
            pltpu.VMEM((tok, RANK), f32),
            pltpu.SemaphoreType.DMA((2 * STEPS,)),
        ],
        compiler_params=kernel_params(56),
    )(hidden, basis)


def sort_kernel(me_ref, go_ref, first_ref, second_ref, mine_ref, other_ref, keep_ref, send_ref):
    even = (me_ref[0] & 1) == 0
    width = go_ref.shape[1] // 4
    for p in range(2):
        low = go_ref[:, (2 * p) * width : (2 * p + 1) * width]
        high = go_ref[:, (2 * p + 1) * width : (2 * p + 2) * width]
        mine_ref[:, p * width : (p + 1) * width] = jnp.where(even, low, high)
        other_ref[:, p * width : (p + 1) * width] = jnp.where(even, high, low)
    place = in_square(me_ref[0] >> 1)[0]
    width = RANK // SQUARE
    for n, ref in enumerate((first_ref, second_ref)):
        old = [ref[:, q * width : (q + 1) * width].astype(bf16) for q in range(SQUARE)]
        for d, out in enumerate((keep_ref, send_ref)):
            for e in range(2):
                at = slice((2 * e + n) * width, (2 * e + n + 1) * width)
                q = place ^ (d + 2 * e)
                low = jnp.where((q & 1) == 0, old[0], old[1])
                high = jnp.where((q & 1) == 0, old[2], old[3])
                out[:, at] = jnp.where(q < 2, low, high)


def sort_call(me, go, first, second):
    tok, col = go.shape
    like = lambda *shape: jax.ShapeDtypeStruct(shape, bf16)
    return pl.pallas_call(
        sort_kernel,
        in_specs=[SMEM] + [VMEM] * 3,
        out_specs=[VMEM] * 4,
        out_shape=[
            like(tok, col // 2),
            like(tok, col // 2),
            like(first.shape[0], RANK),
            like(first.shape[0], RANK),
        ],
        compiler_params=kernel_params(),
        cost_estimate=pl.CostEstimate(flops=2**28, bytes_accessed=2**24, transcendentals=0),
    )(me, go, first, second)


OVER_TOKENS = (((0,), (0,)), ((), ()))


def payload_kernel(
    dims, me_ref, owners_ref, near_ref, far_ref, mine_ref, co_ref, out_ref, proj_ref
):
    chips, pairs, piece, per_block, slots, _ = dims
    share = pairs * piece
    half = chips // per_block
    held = slots * FC
    core = me_ref[0] & 1
    chip = me_ref[0] >> 1
    ids_row = owners_ref[...]
    slot_row = plane_slots(ids_row)
    frags = ids_row.shape[1]
    at = iota((chips * share, 1), 0)
    k_of, p_of, r_of = at // share, (at // piece) % pairs, at % piece
    frag = (core + 2 * p_of) * per_block + k_of // half
    base = ((ids_row & 1) != core).astype(jnp.int32) * (SQUARE * held) + slot_row * FC
    base += (in_square(ids_row >> 1)[0] ^ in_square(chip)[0]) * held
    rows = jnp.sum(jnp.where(frag == iota((1, frags), 1), base, 0), axis=1, keepdims=True)
    rows = rows + (k_of % half) * piece + r_of
    cols = iota((1, SQUARE * held), 1)
    hot = jnp.where(rows == cols, 1.0, 0.0).astype(bf16)
    hot_far = jnp.where(rows == cols + SQUARE * held, 1.0, 0.0).astype(bf16)
    old = jnp.dot(hot, near_ref[...], preferred_element_type=f32)
    old += jnp.dot(hot_far, far_ref[...], preferred_element_type=f32)
    old = old.astype(bf16).reshape(chips, pairs, piece, near_ref.shape[1])
    for p in range(pairs):
        out_ref[:, share:, p * old.shape[3] : (p + 1) * old.shape[3]] = old[:, p]
    proj_ref[...] = lax.dot_general(
        mine_ref[...], co_ref[...], OVER_TOKENS, preferred_element_type=f32
    )


def project_kernel(dims, other_ref, co_other_ref, proj_ref, part_ref, out_ref):
    chips, pairs, piece, _, _, scale = dims
    proj = proj_ref[...] + lax.dot_general(
        other_ref[...], co_other_ref[...], OVER_TOKENS, preferred_element_type=f32
    )
    proj = (proj * scale).astype(bf16).reshape(pairs, chips, piece, RANK)
    for p in range(pairs):
        out_ref[:, p * piece : (p + 1) * piece, :] = proj[p]


def factor_kernel(dims, me_ref, owners_ref, got_ref, factor_ref, grad_ref):
    chips, pairs, piece, per_block, _, _ = dims
    share = pairs * piece
    core = me_ref[0] & 1
    chip = me_ref[0] >> 1
    ids_row = owners_ref[...]
    grad = jnp.zeros((share, RANK), f32)
    for k in range(chips):
        grad += got_ref[k, :share, :].astype(f32)
    width = RANK // SQUARE
    parts = []
    for p in range(pairs):
        frag = (core + 2 * p) * per_block + chip // (chips // per_block)
        sender = jnp.where(iota(ids_row.shape, 1) == frag, ids_row, 0)
        square = in_square(jnp.sum(sender, axis=1, keepdims=True) >> 1)[1]
        old = [jnp.zeros((piece, 2 * width), f32) for _ in range(SQUARE)]
        for k in range(chips):
            place, number = in_square(k)
            sent = got_ref[k, share:, 2 * p * width : (2 * p + 2) * width].astype(f32)
            old[place] = jnp.where(square == number, sent, old[place])
        parts.append(old)
    first, second = (
        jnp.concatenate(
            [
                jnp.concatenate([o[:, n * width : (n + 1) * width] for o in old], axis=1)
                for old in parts
            ],
            axis=0,
        )
        for n in range(2)
    )
    first = first_keep * first + first_take * grad
    second = second_keep * second + second_take * grad * grad
    factor = (first / (jnp.sqrt(second) + adam_eps)).astype(bf16)
    for m in range(factor_ref.shape[0]):
        factor_ref[m] = factor
    grad_ref[...] = grad.astype(bf16)


def update_kernel(piece, basis_ref, last_ref, out_ref, done, sems):
    step, block = done.shape[1:]
    chosen = last_ref[:, :piece, :].reshape(block, RANK)
    copies = []
    for j in range(STEPS):
        at = slice(j * step, (j + 1) * step)
        update = lax.dot_general(
            basis_ref[at, :], chosen, (((1,), (1,)), ((), ())), preferred_element_type=f32
        )
        done[j] = (update * math.sqrt(FF / RANK)).astype(bf16)
        copies.append(pltpu.make_async_copy(done.at[j], out_ref.at[at, :], sems.at[j]))
        copies[-1].start()
    for copy in copies:
        copy.wait()


def update_call(basis, last, block, piece):
    rows = basis.shape[0]
    return pl.pallas_call(
        functools.partial(update_kernel, piece),
        in_specs=[VMEM, VMEM],
        out_specs=pl.BlockSpec(memory_space=pl.ANY),
        out_shape=jax.ShapeDtypeStruct((rows, block), bf16),
        scratch_shapes=[
            pltpu.VMEM((STEPS, rows // STEPS, block), bf16),
            pltpu.SemaphoreType.DMA((STEPS,)),
        ],
        compiler_params=kernel_params(),
    )(basis, last)


def owner_kernel(
    dims, me_ref, owners_ref, first_ref, second_ref, sums_ref, sums_other_ref, first_out, second_out
):
    chips, pairs, piece, per_block, slots = dims
    share = pairs * piece
    half = chips // per_block
    me = me_ref[0]
    ids_row = owners_ref[...]
    slot_row = plane_slots(ids_row)
    frags = ids_row.shape[1]
    at = iota((slots * FC, 1), 0)
    within = at % FC
    own = (ids_row == me) & (slot_row == at // FC)
    live = jnp.sum(own.astype(jnp.int32), axis=1, keepdims=True) > 0
    source = jnp.sum(jnp.where(own, iota((1, frags), 1), 0), axis=1, keepdims=True)
    b = source // per_block
    row = ((source % per_block) * half + within // piece) * share + (b // 2) * piece + within % piece
    row = jnp.where(live, row + (b % 2 != (me & 1)).astype(jnp.int32) * (chips * share), -1)
    cols = iota((1, chips * share), 1)
    hot = jnp.where(row == cols, 1.0, 0.0).astype(bf16)
    hot_other = jnp.where(row == cols + chips * share, 1.0, 0.0).astype(bf16)
    g = jnp.dot(hot, sums_ref[...], preferred_element_type=f32)
    g += jnp.dot(hot_other, sums_other_ref[...], preferred_element_type=f32)
    first, second = first_ref[...], second_ref[...]
    first_out[...] = jnp.where(live, first_keep * first + first_take * g, first)
    second_out[...] = jnp.where(live, second_keep * second + second_take * g * g, second)


def over(exchange, x, *rest):
    x, rest = lax.optimization_barrier((x, rest))
    return lax.optimization_barrier((exchange(x), rest))


def body(hidden, grad_out, basis, owners, first_moment, second_moment):
    owner_count = lax.axis_size("dp")
    planes = lax.axis_size("mp")
    chips = owner_count // 2
    tok, col = grad_out.shape
    slots = first_moment.shape[0] // FC
    frags = owners.shape[0]
    block = col * planes // owner_count
    per_block = block // FC
    piece = block // chips
    pairs = col // block // 2
    share = pairs * piece
    scale = 1.0 / math.sqrt(tok * owner_count)
    same_core = [[2 * k + c for k in range(chips)] for c in range(2)]
    swap = [(i, i ^ 1) for i in range(owner_count)]
    next_x = [(i, i ^ 2) for i in range(owner_count)]
    next_y = [(i, i ^ 8) for i in range(owner_count)]

    def other_core(x):
        return lax.ppermute(x, "dp", swap)

    def over_chips(x):
        return lax.all_to_all(x, "dp", 0, 0, axis_index_groups=same_core, tiled=True)

    def over_planes(x):
        return lax.all_to_all(x, "mp", 0, 0, tiled=True)

    me = lax.axis_index("dp").reshape(1)
    owners = owners.reshape(1, frags)

    part = coeffs_call(hidden, basis)
    part, me, grad_out, first, second = lax.optimization_barrier(
        (part, me, grad_out, first_moment, second_moment)
    )
    go_mine, go_theirs, keep, send = sort_call(me, grad_out, first, second)
    got_x = lax.ppermute(send, "dp", next_x[0::2])
    part, (me, owners, go_mine, go_theirs, keep, send, got_x) = over(
        over_planes, part, me, owners, go_mine, go_theirs, keep, send, got_x
    )
    part = part.reshape(planes, tok // planes, RANK)
    mine = jnp.sum(part.astype(f32), axis=0).astype(bf16)
    mine = jnp.broadcast_to(mine[None], part.shape).reshape(tok, RANK)
    coeffs = over_planes(mine)
    got_x = got_x + lax.ppermute(send, "dp", next_x[1::2])
    near = jnp.concatenate([keep, got_x], axis=0)
    keep, send = near[:, : RANK // 2], near[:, RANK // 2 :]
    near = jnp.concatenate([keep, lax.ppermute(send, "dp", next_y)], axis=0)
    far = other_core(near)
    go_other = other_core(go_theirs)
    coeffs, near, far, go_mine, go_other, me, owners = lax.optimization_barrier(
        (coeffs, near, far, go_mine, go_other, me, owners)
    )
    coeffs_other = other_core(coeffs)

    dims = (chips, pairs, piece, per_block, slots, scale)
    payload_shape = jax.ShapeDtypeStruct((chips, share + piece, RANK), bf16)
    payload, proj = pl.pallas_call(
        functools.partial(payload_kernel, dims),
        in_specs=[SMEM] + [VMEM] * 5,
        out_specs=[VMEM, VMEM],
        out_shape=[payload_shape, jax.ShapeDtypeStruct((pairs * block, RANK), f32)],
        compiler_params=kernel_params(),
    )(me, owners, near, far, go_mine, coeffs)
    payload = pl.pallas_call(
        functools.partial(project_kernel, dims),
        in_specs=[VMEM] * 4,
        out_specs=VMEM,
        out_shape=payload_shape,
        input_output_aliases={3: 0},
        compiler_params=kernel_params(),
    )(go_other, coeffs_other, proj, payload)
    got, (me, owners) = over(over_chips, payload, me, owners)
    factor, grad = pl.pallas_call(
        functools.partial(factor_kernel, dims),
        in_specs=[SMEM] + [VMEM] * 2,
        out_specs=[VMEM, VMEM],
        out_shape=[
            jax.ShapeDtypeStruct((planes, share, RANK), bf16),
            jax.ShapeDtypeStruct((share, RANK), bf16),
        ],
        compiler_params=kernel_params(),
    )(me, owners, got)

    spread, (grad,) = over(over_planes, factor, grad)
    spread = spread.reshape(chips, piece, RANK)
    grad = jnp.broadcast_to(grad[None], (chips, share, RANK))
    last, (me, owners, first_moment, second_moment) = over(
        over_chips,
        jnp.concatenate([spread, grad], axis=1),
        me,
        owners,
        first_moment,
        second_moment,
    )
    sums = last[:, piece:].reshape(chips * share, RANK)
    sums_other = other_core(sums)
    update = update_call(basis, last, block, piece)

    like = jax.ShapeDtypeStruct(first_moment.shape, f32)
    new_first, new_second = pl.pallas_call(
        functools.partial(owner_kernel, dims[:5]),
        in_specs=[SMEM] + [VMEM] * 5,
        out_specs=[VMEM, VMEM],
        out_shape=[like, like],
        compiler_params=kernel_params(),
    )(me, owners, first_moment, second_moment, sums, sums_other)
    return (update, new_first, new_second)


def solution(mesh):
    placed = (
        P("dp", "mp"),
        P("dp", "mp"),
        P("mp", None),
        P("mp", None),
        P(("dp", "mp"), None),
        P(("dp", "mp"), None),
    )
    return jax.shard_map(
        body,
        mesh=mesh,
        in_specs=placed,
        out_specs=(P("mp", "dp"), P(("dp", "mp"), None), P(("dp", "mp"), None)),
        check_vma=False,
    )
```

```python
import functools
import math

import jax
import jax.numpy as jnp
from jax import lax
from jax.experimental import pallas as pl
from jax.experimental.pallas import tpu as pltpu
from jax.sharding import PartitionSpec as P

FF = 28672
RANK = 512
FC = 32
STEPS = 7
SQUARE = 4

first_keep = 0.9
first_take = 0.1
second_keep = 0.95
second_take = 0.05
adam_eps = 1e-08

bf16 = jnp.bfloat16
f32 = jnp.float32
VMEM = pl.BlockSpec(memory_space=pltpu.VMEM)
SMEM = pl.BlockSpec(memory_space=pltpu.SMEM)


def iota(shape, dim):
    return lax.broadcasted_iota(jnp.int32, shape, dim)


def kernel_params(mib=16):
    return pltpu.CompilerParams(vmem_limit_bytes=mib * 2**20)


def plane_slots(ids_row):
    n = ids_row.shape[1]
    f0, f1 = iota((n, n), 0), iota((n, n), 1)
    ids_col = jnp.sum(jnp.where(f0 == f1, ids_row, 0), axis=1, keepdims=True)
    same = ids_col == ids_row
    return jnp.sum((same & (f0 < f1)).astype(jnp.int32), axis=0, keepdims=True)


def in_square(chip):
    return (chip & 1) + 2 * ((chip >> 2) & 1), ((chip >> 1) & 1) + 2 * (chip >> 3)


def coeffs_kernel(hidden_ref, basis_ref, part_ref, hidden, basis, total, sems):
    step = hidden.shape[2]

    def chunk(j):
        at = slice(j * step, (j + 1) * step)
        return (
            pltpu.make_async_copy(hidden_ref.at[:, at], hidden.at[j], sems.at[2 * j]),
            pltpu.make_async_copy(basis_ref.at[at, :], basis.at[j], sems.at[2 * j + 1]),
        )

    chunks = [chunk(j) for j in range(STEPS)]
    for pair in chunks:
        for copy in pair:
            copy.start()
    for j in range(STEPS):
        for copy in chunks[j]:
            copy.wait()
        term = jnp.dot(hidden[j], basis[j], preferred_element_type=f32)
        if j == 0:
            total[...] = term
        elif j < STEPS - 1:
            total[...] += term
        else:
            part_ref[...] = (total[...] + term).astype(bf16)


def coeffs_call(hidden, basis):
    tok, ff = hidden.shape
    step = ff // STEPS
    return pl.pallas_call(
        coeffs_kernel,
        in_specs=[pl.BlockSpec(memory_space=pl.ANY)] * 2,
        out_specs=VMEM,
        out_shape=jax.ShapeDtypeStruct((tok, RANK), bf16),
        scratch_shapes=[
            pltpu.VMEM((STEPS, tok, step), bf16),
            pltpu.VMEM((STEPS, step, RANK), bf16),
            pltpu.VMEM((tok, RANK), f32),
            pltpu.SemaphoreType.DMA((2 * STEPS,)),
        ],
        compiler_params=kernel_params(56),
    )(hidden, basis)


def sort_kernel(me_ref, go_ref, first_ref, second_ref, mine_ref, other_ref, keep_ref, send_ref):
    even = (me_ref[0] & 1) == 0
    width = go_ref.shape[1] // 4
    for p in range(2):
        low = go_ref[:, (2 * p) * width : (2 * p + 1) * width]
        high = go_ref[:, (2 * p + 1) * width : (2 * p + 2) * width]
        mine_ref[:, p * width : (p + 1) * width] = jnp.where(even, low, high)
        other_ref[:, p * width : (p + 1) * width] = jnp.where(even, high, low)
    place = in_square(me_ref[0] >> 1)[0]
    width = RANK // SQUARE
    for n, ref in enumerate((first_ref, second_ref)):
        old = [ref[:, q * width : (q + 1) * width].astype(bf16) for q in range(SQUARE)]
        for d, out in enumerate((keep_ref, send_ref)):
            for e in range(2):
                at = slice((2 * e + n) * width, (2 * e + n + 1) * width)
                q = place ^ (d + 2 * e)
                low = jnp.where((q & 1) == 0, old[0], old[1])
                high = jnp.where((q & 1) == 0, old[2], old[3])
                out[:, at] = jnp.where(q < 2, low, high)


def sort_call(me, go, first, second):
    tok, col = go.shape
    like = lambda *shape: jax.ShapeDtypeStruct(shape, bf16)
    return pl.pallas_call(
        sort_kernel,
        in_specs=[SMEM] + [VMEM] * 3,
        out_specs=[VMEM] * 4,
        out_shape=[
            like(tok, col // 2),
            like(tok, col // 2),
            like(first.shape[0], RANK),
            like(first.shape[0], RANK),
        ],
        compiler_params=kernel_params(),
        cost_estimate=pl.CostEstimate(flops=2**28, bytes_accessed=2**24, transcendentals=0),
    )(me, go, first, second)


OVER_TOKENS = (((0,), (0,)), ((), ()))


def payload_kernel(
    dims, me_ref, owners_ref, near_ref, far_ref, mine_ref, co_ref, out_ref, proj_ref
):
    chips, pairs, piece, per_block, slots, _ = dims
    share = pairs * piece
    half = chips // per_block
    held = slots * FC
    core = me_ref[0] & 1
    chip = me_ref[0] >> 1
    ids_row = owners_ref[...]
    slot_row = plane_slots(ids_row)
    frags = ids_row.shape[1]
    at = iota((chips * share, 1), 0)
    k_of, p_of, r_of = at // share, (at // piece) % pairs, at % piece
    frag = (core + 2 * p_of) * per_block + k_of // half
    base = ((ids_row & 1) != core).astype(jnp.int32) * (SQUARE * held) + slot_row * FC
    base += (in_square(ids_row >> 1)[0] ^ in_square(chip)[0]) * held
    rows = jnp.sum(jnp.where(frag == iota((1, frags), 1), base, 0), axis=1, keepdims=True)
    rows = rows + (k_of % half) * piece + r_of
    cols = iota((1, SQUARE * held), 1)
    hot = jnp.where(rows == cols, 1.0, 0.0).astype(bf16)
    hot_far = jnp.where(rows == cols + SQUARE * held, 1.0, 0.0).astype(bf16)
    old = jnp.dot(hot, near_ref[...], preferred_element_type=f32)
    old += jnp.dot(hot_far, far_ref[...], preferred_element_type=f32)
    old = old.astype(bf16).reshape(chips, pairs, piece, near_ref.shape[1])
    for p in range(pairs):
        out_ref[:, share:, p * old.shape[3] : (p + 1) * old.shape[3]] = old[:, p]
    proj_ref[...] = lax.dot_general(
        mine_ref[...], co_ref[...], OVER_TOKENS, preferred_element_type=f32
    )


def project_kernel(dims, other_ref, co_other_ref, proj_ref, part_ref, out_ref):
    chips, pairs, piece, _, _, scale = dims
    proj = proj_ref[...] + lax.dot_general(
        other_ref[...], co_other_ref[...], OVER_TOKENS, preferred_element_type=f32
    )
    proj = (proj * scale).astype(bf16).reshape(pairs, chips, piece, RANK)
    for p in range(pairs):
        out_ref[:, p * piece : (p + 1) * piece, :] = proj[p]


def factor_kernel(dims, me_ref, owners_ref, got_ref, factor_ref, grad_ref):
    chips, pairs, piece, per_block, _, _ = dims
    share = pairs * piece
    core = me_ref[0] & 1
    chip = me_ref[0] >> 1
    ids_row = owners_ref[...]
    grad = jnp.zeros((share, RANK), f32)
    for k in range(chips):
        grad += got_ref[k, :share, :].astype(f32)
    width = RANK // SQUARE
    parts = []
    for p in range(pairs):
        frag = (core + 2 * p) * per_block + chip // (chips // per_block)
        sender = jnp.where(iota(ids_row.shape, 1) == frag, ids_row, 0)
        square = in_square(jnp.sum(sender, axis=1, keepdims=True) >> 1)[1]
        old = [jnp.zeros((piece, 2 * width), f32) for _ in range(SQUARE)]
        for k in range(chips):
            place, number = in_square(k)
            sent = got_ref[k, share:, 2 * p * width : (2 * p + 2) * width].astype(f32)
            old[place] = jnp.where(square == number, sent, old[place])
        parts.append(old)
    first, second = (
        jnp.concatenate(
            [
                jnp.concatenate([o[:, n * width : (n + 1) * width] for o in old], axis=1)
                for old in parts
            ],
            axis=0,
        )
        for n in range(2)
    )
    first = first_keep * first + first_take * grad
    second = second_keep * second + second_take * grad * grad
    factor = (first / (jnp.sqrt(second) + adam_eps)).astype(bf16)
    for m in range(factor_ref.shape[0]):
        factor_ref[m] = factor
    grad_ref[...] = grad.astype(bf16)


def update_kernel(piece, basis_ref, last_ref, out_ref, done, sems):
    step, block = done.shape[1:]
    chosen = last_ref[:, :piece, :].reshape(block, RANK)
    copies = []
    for j in range(STEPS):
        at = slice(j * step, (j + 1) * step)
        update = lax.dot_general(
            basis_ref[at, :], chosen, (((1,), (1,)), ((), ())), preferred_element_type=f32
        )
        done[j] = (update * math.sqrt(FF / RANK)).astype(bf16)
        copies.append(pltpu.make_async_copy(done.at[j], out_ref.at[at, :], sems.at[j]))
        copies[-1].start()
    for copy in copies:
        copy.wait()


def update_call(basis, last, block, piece):
    rows = basis.shape[0]
    return pl.pallas_call(
        functools.partial(update_kernel, piece),
        in_specs=[VMEM, VMEM],
        out_specs=pl.BlockSpec(memory_space=pl.ANY),
        out_shape=jax.ShapeDtypeStruct((rows, block), bf16),
        scratch_shapes=[
            pltpu.VMEM((STEPS, rows // STEPS, block), bf16),
            pltpu.SemaphoreType.DMA((STEPS,)),
        ],
        compiler_params=kernel_params(),
    )(basis, last)


def owner_kernel(
    dims, me_ref, owners_ref, first_ref, second_ref, sums_ref, sums_other_ref, first_out, second_out
):
    chips, pairs, piece, per_block, slots = dims
    share = pairs * piece
    half = chips // per_block
    me = me_ref[0]
    ids_row = owners_ref[...]
    slot_row = plane_slots(ids_row)
    frags = ids_row.shape[1]
    at = iota((slots * FC, 1), 0)
    within = at % FC
    own = (ids_row == me) & (slot_row == at // FC)
    live = jnp.sum(own.astype(jnp.int32), axis=1, keepdims=True) > 0
    source = jnp.sum(jnp.where(own, iota((1, frags), 1), 0), axis=1, keepdims=True)
    b = source // per_block
    row = ((source % per_block) * half + within // piece) * share + (b // 2) * piece + within % piece
    row = jnp.where(live, row + (b % 2 != (me & 1)).astype(jnp.int32) * (chips * share), -1)
    cols = iota((1, chips * share), 1)
    hot = jnp.where(row == cols, 1.0, 0.0).astype(bf16)
    hot_other = jnp.where(row == cols + chips * share, 1.0, 0.0).astype(bf16)
    g = jnp.dot(hot, sums_ref[...], preferred_element_type=f32)
    g += jnp.dot(hot_other, sums_other_ref[...], preferred_element_type=f32)
    first, second = first_ref[...], second_ref[...]
    first_out[...] = jnp.where(live, first_keep * first + first_take * g, first)
    second_out[...] = jnp.where(live, second_keep * second + second_take * g * g, second)


def over(exchange, x, *rest):
    x, rest = lax.optimization_barrier((x, rest))
    return lax.optimization_barrier((exchange(x), rest))


def body(hidden, grad_out, basis, owners, first_moment, second_moment):
    owner_count = lax.axis_size("dp")
    planes = lax.axis_size("mp")
    chips = owner_count // 2
    tok, col = grad_out.shape
    slots = first_moment.shape[0] // FC
    frags = owners.shape[0]
    block = col * planes // owner_count
    per_block = block // FC
    piece = block // chips
    pairs = col // block // 2
    share = pairs * piece
    scale = 1.0 / math.sqrt(tok * owner_count)
    same_core = [[2 * k + c for k in range(chips)] for c in range(2)]
    swap = [(i, i ^ 1) for i in range(owner_count)]
    next_x = [(i, i ^ 2) for i in range(owner_count)]
    next_y = [(i, i ^ 8) for i in range(owner_count)]

    def other_core(x):
        return lax.ppermute(x, "dp", swap)

    def over_chips(x):
        return lax.all_to_all(x, "dp", 0, 0, axis_index_groups=same_core, tiled=True)

    def over_planes(x):
        return lax.all_to_all(x, "mp", 0, 0, tiled=True)

    me = lax.axis_index("dp").reshape(1)
    owners = owners.reshape(1, frags)

    part = coeffs_call(hidden, basis)
    part, me, grad_out, first, second = lax.optimization_barrier(
        (part, me, grad_out, first_moment, second_moment)
    )
    go_mine, go_theirs, keep, send = sort_call(me, grad_out, first, second)
    early = RANK // SQUARE
    got_x = lax.ppermute(send[:, :early], "dp", next_x[0::2])
    part, (me, owners, go_mine, go_theirs, keep, send, got_x) = over(
        over_planes, part, me, owners, go_mine, go_theirs, keep, send, got_x
    )
    part = part.reshape(planes, tok // planes, RANK)
    mine = jnp.sum(part.astype(f32), axis=0).astype(bf16)
    mine = jnp.broadcast_to(mine[None], part.shape).reshape(tok, RANK)
    coeffs = over_planes(mine)
    got_x = got_x + lax.ppermute(send[:, :early], "dp", next_x[1::2])
    got_x = jnp.concatenate([got_x, lax.ppermute(send[:, early:], "dp", next_x)], axis=1)
    near = jnp.concatenate([keep, got_x], axis=0)
    keep, send = near[:, : RANK // 2], near[:, RANK // 2 :]
    near = jnp.concatenate([keep, lax.ppermute(send, "dp", next_y)], axis=0)
    far = other_core(near)
    go_other = other_core(go_theirs)
    coeffs, near, far, go_mine, go_other, me, owners = lax.optimization_barrier(
        (coeffs, near, far, go_mine, go_other, me, owners)
    )
    coeffs_other = other_core(coeffs)

    dims = (chips, pairs, piece, per_block, slots, scale)
    payload_shape = jax.ShapeDtypeStruct((chips, share + piece, RANK), bf16)
    payload, proj = pl.pallas_call(
        functools.partial(payload_kernel, dims),
        in_specs=[SMEM] + [VMEM] * 5,
        out_specs=[VMEM, VMEM],
        out_shape=[payload_shape, jax.ShapeDtypeStruct((pairs * block, RANK), f32)],
        compiler_params=kernel_params(),
    )(me, owners, near, far, go_mine, coeffs)
    payload = pl.pallas_call(
        functools.partial(project_kernel, dims),
        in_specs=[VMEM] * 4,
        out_specs=VMEM,
        out_shape=payload_shape,
        input_output_aliases={3: 0},
        compiler_params=kernel_params(),
    )(go_other, coeffs_other, proj, payload)
    got, (me, owners) = over(over_chips, payload, me, owners)
    factor, grad = pl.pallas_call(
        functools.partial(factor_kernel, dims),
        in_specs=[SMEM] + [VMEM] * 2,
        out_specs=[VMEM, VMEM],
        out_shape=[
            jax.ShapeDtypeStruct((planes, share, RANK), bf16),
            jax.ShapeDtypeStruct((share, RANK), bf16),
        ],
        compiler_params=kernel_params(),
    )(me, owners, got)

    spread, (grad,) = over(over_planes, factor, grad)
    spread = spread.reshape(chips, piece, RANK)
    grad = jnp.broadcast_to(grad[None], (chips, share, RANK))
    last, (me, owners, first_moment, second_moment) = over(
        over_chips,
        jnp.concatenate([spread, grad], axis=1),
        me,
        owners,
        first_moment,
        second_moment,
    )
    sums = last[:, piece:].reshape(chips * share, RANK)
    sums_other = other_core(sums)
    update = update_call(basis, last, block, piece)

    like = jax.ShapeDtypeStruct(first_moment.shape, f32)
    new_first, new_second = pl.pallas_call(
        functools.partial(owner_kernel, dims[:5]),
        in_specs=[SMEM] + [VMEM] * 5,
        out_specs=[VMEM, VMEM],
        out_shape=[like, like],
        compiler_params=kernel_params(),
    )(me, owners, first_moment, second_moment, sums, sums_other)
    return (update, new_first, new_second)


def solution(mesh):
    placed = (
        P("dp", "mp"),
        P("dp", "mp"),
        P("mp", None),
        P("mp", None),
        P(("dp", "mp"), None),
        P(("dp", "mp"), None),
    )
    return jax.shard_map(
        body,
        mesh=mesh,
        in_specs=placed,
        out_specs=(P("mp", "dp"), P(("dp", "mp"), None), P(("dp", "mp"), None)),
        check_vma=False,
    )
```

```python
import functools
import math

import jax
import jax.numpy as jnp
from jax import lax
from jax.experimental import pallas as pl
from jax.experimental.pallas import tpu as pltpu
from jax.sharding import PartitionSpec as P

FF = 28672
RANK = 512
FC = 32
STEPS = 7
SQUARE = 4

first_keep = 0.9
first_take = 0.1
second_keep = 0.95
second_take = 0.05
adam_eps = 1e-08

bf16 = jnp.bfloat16
f32 = jnp.float32
VMEM = pl.BlockSpec(memory_space=pltpu.VMEM)
SMEM = pl.BlockSpec(memory_space=pltpu.SMEM)


def iota(shape, dim):
    return lax.broadcasted_iota(jnp.int32, shape, dim)


def kernel_params(mib=16):
    return pltpu.CompilerParams(vmem_limit_bytes=mib * 2**20)


def plane_slots(ids_row):
    n = ids_row.shape[1]
    f0, f1 = iota((n, n), 0), iota((n, n), 1)
    ids_col = jnp.sum(jnp.where(f0 == f1, ids_row, 0), axis=1, keepdims=True)
    same = ids_col == ids_row
    return jnp.sum((same & (f0 < f1)).astype(jnp.int32), axis=0, keepdims=True)


def in_square(chip):
    return (chip & 1) + 2 * ((chip >> 2) & 1), ((chip >> 1) & 1) + 2 * (chip >> 3)


def coeffs_kernel(hidden_ref, basis_ref, part_ref, hidden, basis, total, sems):
    step = hidden.shape[2]

    def chunk(j):
        at = slice(j * step, (j + 1) * step)
        return (
            pltpu.make_async_copy(hidden_ref.at[:, at], hidden.at[j], sems.at[2 * j]),
            pltpu.make_async_copy(basis_ref.at[at, :], basis.at[j], sems.at[2 * j + 1]),
        )

    chunks = [chunk(j) for j in range(STEPS)]
    for pair in chunks:
        for copy in pair:
            copy.start()
    for j in range(STEPS):
        for copy in chunks[j]:
            copy.wait()
        term = jnp.dot(hidden[j], basis[j], preferred_element_type=f32)
        if j == 0:
            total[...] = term
        elif j < STEPS - 1:
            total[...] += term
        else:
            part_ref[...] = (total[...] + term).astype(bf16)


def coeffs_call(hidden, basis):
    tok, ff = hidden.shape
    step = ff // STEPS
    return pl.pallas_call(
        coeffs_kernel,
        in_specs=[pl.BlockSpec(memory_space=pl.ANY)] * 2,
        out_specs=VMEM,
        out_shape=jax.ShapeDtypeStruct((tok, RANK), bf16),
        scratch_shapes=[
            pltpu.VMEM((STEPS, tok, step), bf16),
            pltpu.VMEM((STEPS, step, RANK), bf16),
            pltpu.VMEM((tok, RANK), f32),
            pltpu.SemaphoreType.DMA((2 * STEPS,)),
        ],
        compiler_params=kernel_params(56),
    )(hidden, basis)


def sort_kernel(me_ref, go_ref, first_ref, second_ref, mine_ref, other_ref, keep_ref, send_ref):
    even = (me_ref[0] & 1) == 0
    width = go_ref.shape[1] // 4
    for p in range(2):
        low = go_ref[:, (2 * p) * width : (2 * p + 1) * width]
        high = go_ref[:, (2 * p + 1) * width : (2 * p + 2) * width]
        mine_ref[:, p * width : (p + 1) * width] = jnp.where(even, low, high)
        other_ref[:, p * width : (p + 1) * width] = jnp.where(even, high, low)
    place = in_square(me_ref[0] >> 1)[0]
    width = RANK // SQUARE
    for n, ref in enumerate((first_ref, second_ref)):
        old = [ref[:, q * width : (q + 1) * width].astype(bf16) for q in range(SQUARE)]
        for d, out in enumerate((keep_ref, send_ref)):
            for e in range(2):
                at = slice((2 * e + n) * width, (2 * e + n + 1) * width)
                q = place ^ (d + 2 * e)
                low = jnp.where((q & 1) == 0, old[0], old[1])
                high = jnp.where((q & 1) == 0, old[2], old[3])
                out[:, at] = jnp.where(q < 2, low, high)


def sort_call(me, go, first, second):
    tok, col = go.shape
    like = lambda *shape: jax.ShapeDtypeStruct(shape, bf16)
    return pl.pallas_call(
        sort_kernel,
        in_specs=[SMEM] + [VMEM] * 3,
        out_specs=[VMEM] * 4,
        out_shape=[
            like(tok, col // 2),
            like(tok, col // 2),
            like(first.shape[0], RANK),
            like(first.shape[0], RANK),
        ],
        compiler_params=kernel_params(),
        cost_estimate=pl.CostEstimate(flops=2**28, bytes_accessed=2**24, transcendentals=0),
    )(me, go, first, second)


OVER_TOKENS = (((0,), (0,)), ((), ()))


def payload_kernel(
    dims, me_ref, owners_ref, near_ref, far_ref, mine_ref, co_ref, out_ref, proj_ref
):
    chips, pairs, piece, per_block, slots, _ = dims
    share = pairs * piece
    half = chips // per_block
    held = slots * FC
    core = me_ref[0] & 1
    chip = me_ref[0] >> 1
    ids_row = owners_ref[...]
    slot_row = plane_slots(ids_row)
    frags = ids_row.shape[1]
    at = iota((chips * share, 1), 0)
    k_of, p_of, r_of = at // share, (at // piece) % pairs, at % piece
    frag = (core + 2 * p_of) * per_block + k_of // half
    base = ((ids_row & 1) != core).astype(jnp.int32) * (SQUARE * held) + slot_row * FC
    base += (in_square(ids_row >> 1)[0] ^ in_square(chip)[0]) * held
    rows = jnp.sum(jnp.where(frag == iota((1, frags), 1), base, 0), axis=1, keepdims=True)
    rows = rows + (k_of % half) * piece + r_of
    cols = iota((1, SQUARE * held), 1)
    hot = jnp.where(rows == cols, 1.0, 0.0).astype(bf16)
    hot_far = jnp.where(rows == cols + SQUARE * held, 1.0, 0.0).astype(bf16)
    old = jnp.dot(hot, near_ref[...], preferred_element_type=f32)
    old += jnp.dot(hot_far, far_ref[...], preferred_element_type=f32)
    old = old.astype(bf16).reshape(chips, pairs, piece, near_ref.shape[1])
    for p in range(pairs):
        out_ref[:, share:, p * old.shape[3] : (p + 1) * old.shape[3]] = old[:, p]
    proj_ref[...] = lax.dot_general(
        mine_ref[...], co_ref[...], OVER_TOKENS, preferred_element_type=f32
    )


def project_kernel(dims, other_ref, co_other_ref, proj_ref, part_ref, out_ref):
    chips, pairs, piece, _, _, scale = dims
    proj = proj_ref[...] + lax.dot_general(
        other_ref[...], co_other_ref[...], OVER_TOKENS, preferred_element_type=f32
    )
    proj = (proj * scale).astype(bf16).reshape(pairs, chips, piece, RANK)
    for p in range(pairs):
        out_ref[:, p * piece : (p + 1) * piece, :] = proj[p]


def factor_kernel(dims, me_ref, owners_ref, got_ref, factor_ref, grad_ref):
    chips, pairs, piece, per_block, _, _ = dims
    share = pairs * piece
    core = me_ref[0] & 1
    chip = me_ref[0] >> 1
    ids_row = owners_ref[...]
    grad = jnp.zeros((share, RANK), f32)
    for k in range(chips):
        grad += got_ref[k, :share, :].astype(f32)
    width = RANK // SQUARE
    parts = []
    for p in range(pairs):
        frag = (core + 2 * p) * per_block + chip // (chips // per_block)
        sender = jnp.where(iota(ids_row.shape, 1) == frag, ids_row, 0)
        square = in_square(jnp.sum(sender, axis=1, keepdims=True) >> 1)[1]
        old = [jnp.zeros((piece, 2 * width), f32) for _ in range(SQUARE)]
        for k in range(chips):
            place, number = in_square(k)
            sent = got_ref[k, share:, 2 * p * width : (2 * p + 2) * width].astype(f32)
            old[place] = jnp.where(square == number, sent, old[place])
        parts.append(old)
    first, second = (
        jnp.concatenate(
            [
                jnp.concatenate([o[:, n * width : (n + 1) * width] for o in old], axis=1)
                for old in parts
            ],
            axis=0,
        )
        for n in range(2)
    )
    first = first_keep * first + first_take * grad
    second = second_keep * second + second_take * grad * grad
    factor = (first / (jnp.sqrt(second) + adam_eps)).astype(bf16)
    for m in range(factor_ref.shape[0]):
        factor_ref[m] = factor
    grad_ref[...] = grad.astype(bf16)


def update_kernel(piece, basis_ref, last_ref, out_ref, done, sems):
    step, block = done.shape[1:]
    chosen = last_ref[:, :piece, :].reshape(block, RANK)
    copies = []
    for j in range(STEPS):
        at = slice(j * step, (j + 1) * step)
        update = lax.dot_general(
            basis_ref[at, :], chosen, (((1,), (1,)), ((), ())), preferred_element_type=f32
        )
        done[j] = (update * math.sqrt(FF / RANK)).astype(bf16)
        copies.append(pltpu.make_async_copy(done.at[j], out_ref.at[at, :], sems.at[j]))
        copies[-1].start()
    for copy in copies:
        copy.wait()


def update_call(basis, last, block, piece):
    rows = basis.shape[0]
    return pl.pallas_call(
        functools.partial(update_kernel, piece),
        in_specs=[VMEM, VMEM],
        out_specs=pl.BlockSpec(memory_space=pl.ANY),
        out_shape=jax.ShapeDtypeStruct((rows, block), bf16),
        scratch_shapes=[
            pltpu.VMEM((STEPS, rows // STEPS, block), bf16),
            pltpu.SemaphoreType.DMA((STEPS,)),
        ],
        compiler_params=kernel_params(),
    )(basis, last)


def owner_kernel(
    dims, me_ref, owners_ref, first_ref, second_ref, sums_ref, sums_other_ref, first_out, second_out
):
    chips, pairs, piece, per_block, slots = dims
    share = pairs * piece
    half = chips // per_block
    me = me_ref[0]
    ids_row = owners_ref[...]
    slot_row = plane_slots(ids_row)
    frags = ids_row.shape[1]
    at = iota((slots * FC, 1), 0)
    within = at % FC
    own = (ids_row == me) & (slot_row == at // FC)
    live = jnp.sum(own.astype(jnp.int32), axis=1, keepdims=True) > 0
    source = jnp.sum(jnp.where(own, iota((1, frags), 1), 0), axis=1, keepdims=True)
    b = source // per_block
    row = ((source % per_block) * half + within // piece) * share + (b // 2) * piece + within % piece
    row = jnp.where(live, row + (b % 2 != (me & 1)).astype(jnp.int32) * (chips * share), -1)
    cols = iota((1, chips * share), 1)
    hot = jnp.where(row == cols, 1.0, 0.0).astype(bf16)
    hot_other = jnp.where(row == cols + chips * share, 1.0, 0.0).astype(bf16)
    g = jnp.dot(hot, sums_ref[...], preferred_element_type=f32)
    g += jnp.dot(hot_other, sums_other_ref[...], preferred_element_type=f32)
    first, second = first_ref[...], second_ref[...]
    first_out[...] = jnp.where(live, first_keep * first + first_take * g, first)
    second_out[...] = jnp.where(live, second_keep * second + second_take * g * g, second)


def over(exchange, x, *rest):
    x, rest = lax.optimization_barrier((x, rest))
    return lax.optimization_barrier((exchange(x), rest))


def body(hidden, grad_out, basis, owners, first_moment, second_moment):
    owner_count = lax.axis_size("dp")
    planes = lax.axis_size("mp")
    chips = owner_count // 2
    tok, col = grad_out.shape
    slots = first_moment.shape[0] // FC
    frags = owners.shape[0]
    block = col * planes // owner_count
    per_block = block // FC
    piece = block // chips
    pairs = col // block // 2
    share = pairs * piece
    scale = 1.0 / math.sqrt(tok * owner_count)
    same_core = [[2 * k + c for k in range(chips)] for c in range(2)]
    swap = [(i, i ^ 1) for i in range(owner_count)]
    next_x = [(i, i ^ 2) for i in range(owner_count)]
    next_y = [(i, i ^ 8) for i in range(owner_count)]

    def other_core(x):
        return lax.ppermute(x, "dp", swap)

    def over_chips(x):
        return lax.all_to_all(x, "dp", 0, 0, axis_index_groups=same_core, tiled=True)

    def over_planes(x):
        return lax.all_to_all(x, "mp", 0, 0, tiled=True)

    me = lax.axis_index("dp").reshape(1)
    owners = owners.reshape(1, frags)

    part = coeffs_call(hidden, basis)
    part, me, grad_out, first, second = lax.optimization_barrier(
        (part, me, grad_out, first_moment, second_moment)
    )
    go_mine, go_theirs, keep, send = sort_call(me, grad_out, first, second)
    got_x = lax.ppermute(send, "dp", next_x[0::2])
    part, keep, send, got_x, go_theirs = lax.optimization_barrier((part, keep, send, got_x, go_theirs))
    part = over_planes(part)
    got_x = got_x + lax.ppermute(send, "dp", next_x[1::2])
    near = jnp.concatenate([keep, got_x], axis=0)
    keep, send = near[:, : RANK // 2], near[:, RANK // 2 :]
    near = jnp.concatenate([keep, lax.ppermute(send, "dp", next_y)], axis=0)
    near, go_theirs = lax.optimization_barrier((near, go_theirs))
    far = other_core(near)
    go_other = other_core(go_theirs)
    part, near, far, go_mine, go_other, me, owners = lax.optimization_barrier(
        (part, near, far, go_mine, go_other, me, owners)
    )
    part = part.reshape(planes, tok // planes, RANK)
    mine = jnp.sum(part.astype(f32), axis=0).astype(bf16)
    mine = jnp.broadcast_to(mine[None], part.shape).reshape(tok, RANK)
    coeffs, (near, far, go_mine, go_other, me, owners) = over(
        over_planes, mine, near, far, go_mine, go_other, me, owners
    )
    coeffs_other = other_core(coeffs)

    dims = (chips, pairs, piece, per_block, slots, scale)
    payload_shape = jax.ShapeDtypeStruct((chips, share + piece, RANK), bf16)
    payload, proj = pl.pallas_call(
        functools.partial(payload_kernel, dims),
        in_specs=[SMEM] + [VMEM] * 5,
        out_specs=[VMEM, VMEM],
        out_shape=[payload_shape, jax.ShapeDtypeStruct((pairs * block, RANK), f32)],
        compiler_params=kernel_params(),
    )(me, owners, near, far, go_mine, coeffs)
    payload = pl.pallas_call(
        functools.partial(project_kernel, dims),
        in_specs=[VMEM] * 4,
        out_specs=VMEM,
        out_shape=payload_shape,
        input_output_aliases={3: 0},
        compiler_params=kernel_params(),
    )(go_other, coeffs_other, proj, payload)
    got, (me, owners) = over(over_chips, payload, me, owners)
    factor, grad = pl.pallas_call(
        functools.partial(factor_kernel, dims),
        in_specs=[SMEM] + [VMEM] * 2,
        out_specs=[VMEM, VMEM],
        out_shape=[
            jax.ShapeDtypeStruct((planes, share, RANK), bf16),
            jax.ShapeDtypeStruct((share, RANK), bf16),
        ],
        compiler_params=kernel_params(),
    )(me, owners, got)

    spread, (grad,) = over(over_planes, factor, grad)
    spread = spread.reshape(chips, piece, RANK)
    grad = jnp.broadcast_to(grad[None], (chips, share, RANK))
    last, (me, owners, first_moment, second_moment) = over(
        over_chips,
        jnp.concatenate([spread, grad], axis=1),
        me,
        owners,
        first_moment,
        second_moment,
    )
    sums = last[:, piece:].reshape(chips * share, RANK)
    sums_other = other_core(sums)
    update = update_call(basis, last, block, piece)

    like = jax.ShapeDtypeStruct(first_moment.shape, f32)
    new_first, new_second = pl.pallas_call(
        functools.partial(owner_kernel, dims[:5]),
        in_specs=[SMEM] + [VMEM] * 5,
        out_specs=[VMEM, VMEM],
        out_shape=[like, like],
        compiler_params=kernel_params(),
    )(me, owners, first_moment, second_moment, sums, sums_other)
    return (update, new_first, new_second)


def solution(mesh):
    placed = (
        P("dp", "mp"),
        P("dp", "mp"),
        P("mp", None),
        P("mp", None),
        P(("dp", "mp"), None),
        P(("dp", "mp"), None),
    )
    return jax.shard_map(
        body,
        mesh=mesh,
        in_specs=placed,
        out_specs=(P("mp", "dp"), P(("dp", "mp"), None), P(("dp", "mp"), None)),
        check_vma=False,
    )
```

```python
import functools
import math

import jax
import jax.numpy as jnp
from jax import lax
from jax.experimental import pallas as pl
from jax.experimental.pallas import tpu as pltpu
from jax.sharding import PartitionSpec as P

FF = 28672
RANK = 512
FC = 32
STEPS = 7
SQUARE = 4

first_keep = 0.9
first_take = 0.1
second_keep = 0.95
second_take = 0.05
adam_eps = 1e-08

bf16 = jnp.bfloat16
f32 = jnp.float32
VMEM = pl.BlockSpec(memory_space=pltpu.VMEM)
SMEM = pl.BlockSpec(memory_space=pltpu.SMEM)


def iota(shape, dim):
    return lax.broadcasted_iota(jnp.int32, shape, dim)


def kernel_params(mib=16):
    return pltpu.CompilerParams(vmem_limit_bytes=mib * 2**20)


def plane_slots(ids_row):
    n = ids_row.shape[1]
    f0, f1 = iota((n, n), 0), iota((n, n), 1)
    ids_col = jnp.sum(jnp.where(f0 == f1, ids_row, 0), axis=1, keepdims=True)
    same = ids_col == ids_row
    return jnp.sum((same & (f0 < f1)).astype(jnp.int32), axis=0, keepdims=True)


def in_square(chip):
    return (chip & 1) + 2 * ((chip >> 2) & 1), ((chip >> 1) & 1) + 2 * (chip >> 3)


def coeffs_kernel(hidden_ref, basis_ref, part_ref, hidden, basis, total, sems):
    step = hidden.shape[2]

    def chunk(j):
        at = slice(j * step, (j + 1) * step)
        return (
            pltpu.make_async_copy(hidden_ref.at[:, at], hidden.at[j], sems.at[2 * j]),
            pltpu.make_async_copy(basis_ref.at[at, :], basis.at[j], sems.at[2 * j + 1]),
        )

    chunks = [chunk(j) for j in range(STEPS)]
    for pair in chunks:
        for copy in pair:
            copy.start()
    for j in range(STEPS):
        for copy in chunks[j]:
            copy.wait()
        term = jnp.dot(hidden[j], basis[j], preferred_element_type=f32)
        if j == 0:
            total[...] = term
        elif j < STEPS - 1:
            total[...] += term
        else:
            part_ref[...] = (total[...] + term).astype(bf16)


def coeffs_call(hidden, basis):
    tok, ff = hidden.shape
    step = ff // STEPS
    return pl.pallas_call(
        coeffs_kernel,
        in_specs=[pl.BlockSpec(memory_space=pl.ANY)] * 2,
        out_specs=VMEM,
        out_shape=jax.ShapeDtypeStruct((tok, RANK), bf16),
        scratch_shapes=[
            pltpu.VMEM((STEPS, tok, step), bf16),
            pltpu.VMEM((STEPS, step, RANK), bf16),
            pltpu.VMEM((tok, RANK), f32),
            pltpu.SemaphoreType.DMA((2 * STEPS,)),
        ],
        compiler_params=kernel_params(56),
    )(hidden, basis)


def sort_kernel(me_ref, go_ref, first_ref, second_ref, mine_ref, other_ref, keep_ref, send_ref):
    even = (me_ref[0] & 1) == 0
    width = go_ref.shape[1] // 4
    for p in range(2):
        low = go_ref[:, (2 * p) * width : (2 * p + 1) * width]
        high = go_ref[:, (2 * p + 1) * width : (2 * p + 2) * width]
        mine_ref[:, p * width : (p + 1) * width] = jnp.where(even, low, high)
        other_ref[:, p * width : (p + 1) * width] = jnp.where(even, high, low)
    place = in_square(me_ref[0] >> 1)[0]
    width = RANK // SQUARE
    for n, ref in enumerate((first_ref, second_ref)):
        old = [ref[:, q * width : (q + 1) * width].astype(bf16) for q in range(SQUARE)]
        for d, out in enumerate((keep_ref, send_ref)):
            for e in range(2):
                at = slice((2 * e + n) * width, (2 * e + n + 1) * width)
                q = place ^ (d + 2 * e)
                low = jnp.where((q & 1) == 0, old[0], old[1])
                high = jnp.where((q & 1) == 0, old[2], old[3])
                out[:, at] = jnp.where(q < 2, low, high)


def sort_call(me, go, first, second):
    tok, col = go.shape
    like = lambda *shape: jax.ShapeDtypeStruct(shape, bf16)
    return pl.pallas_call(
        sort_kernel,
        in_specs=[SMEM] + [VMEM] * 3,
        out_specs=[VMEM] * 4,
        out_shape=[
            like(tok, col // 2),
            like(tok, col // 2),
            like(first.shape[0], RANK),
            like(first.shape[0], RANK),
        ],
        compiler_params=kernel_params(),
        cost_estimate=pl.CostEstimate(flops=2**28, bytes_accessed=2**24, transcendentals=0),
    )(me, go, first, second)


OVER_TOKENS = (((0,), (0,)), ((), ()))


def payload_kernel(
    dims, me_ref, owners_ref, near_ref, far_ref, mine_ref, co_ref, out_ref, proj_ref
):
    chips, pairs, piece, per_block, slots, _ = dims
    share = pairs * piece
    half = chips // per_block
    held = slots * FC
    core = me_ref[0] & 1
    chip = me_ref[0] >> 1
    ids_row = owners_ref[...]
    slot_row = plane_slots(ids_row)
    frags = ids_row.shape[1]
    at = iota((chips * share, 1), 0)
    k_of, p_of, r_of = at // share, (at // piece) % pairs, at % piece
    frag = (core + 2 * p_of) * per_block + k_of // half
    base = ((ids_row & 1) != core).astype(jnp.int32) * (SQUARE * held) + slot_row * FC
    base += (in_square(ids_row >> 1)[0] ^ in_square(chip)[0]) * held
    rows = jnp.sum(jnp.where(frag == iota((1, frags), 1), base, 0), axis=1, keepdims=True)
    rows = rows + (k_of % half) * piece + r_of
    cols = iota((1, SQUARE * held), 1)
    hot = jnp.where(rows == cols, 1.0, 0.0).astype(bf16)
    hot_far = jnp.where(rows == cols + SQUARE * held, 1.0, 0.0).astype(bf16)
    old = jnp.dot(hot, near_ref[...], preferred_element_type=f32)
    old += jnp.dot(hot_far, far_ref[...], preferred_element_type=f32)
    old = old.astype(bf16).reshape(chips, pairs, piece, near_ref.shape[1])
    for p in range(pairs):
        out_ref[:, share:, p * old.shape[3] : (p + 1) * old.shape[3]] = old[:, p]
    proj_ref[...] = lax.dot_general(
        mine_ref[...], co_ref[...], OVER_TOKENS, preferred_element_type=f32
    )


def project_kernel(dims, other_ref, co_other_ref, proj_ref, part_ref, out_ref):
    chips, pairs, piece, _, _, scale = dims
    proj = proj_ref[...] + lax.dot_general(
        other_ref[...], co_other_ref[...], OVER_TOKENS, preferred_element_type=f32
    )
    proj = (proj * scale).astype(bf16).reshape(pairs, chips, piece, RANK)
    for p in range(pairs):
        out_ref[:, p * piece : (p + 1) * piece, :] = proj[p]


def factor_kernel(dims, me_ref, owners_ref, got_ref, factor_ref, grad_ref):
    chips, pairs, piece, per_block, _, _ = dims
    share = pairs * piece
    core = me_ref[0] & 1
    chip = me_ref[0] >> 1
    ids_row = owners_ref[...]
    grad = jnp.zeros((share, RANK), f32)
    for k in range(chips):
        grad += got_ref[k, :share, :].astype(f32)
    width = RANK // SQUARE
    parts = []
    for p in range(pairs):
        frag = (core + 2 * p) * per_block + chip // (chips // per_block)
        sender = jnp.where(iota(ids_row.shape, 1) == frag, ids_row, 0)
        square = in_square(jnp.sum(sender, axis=1, keepdims=True) >> 1)[1]
        old = [jnp.zeros((piece, 2 * width), f32) for _ in range(SQUARE)]
        for k in range(chips):
            place, number = in_square(k)
            sent = got_ref[k, share:, 2 * p * width : (2 * p + 2) * width].astype(f32)
            old[place] = jnp.where(square == number, sent, old[place])
        parts.append(old)
    first, second = (
        jnp.concatenate(
            [
                jnp.concatenate([o[:, n * width : (n + 1) * width] for o in old], axis=1)
                for old in parts
            ],
            axis=0,
        )
        for n in range(2)
    )
    first = first_keep * first + first_take * grad
    second = second_keep * second + second_take * grad * grad
    factor = (first / (jnp.sqrt(second) + adam_eps)).astype(bf16)
    for m in range(factor_ref.shape[0]):
        factor_ref[m] = factor
    grad_ref[...] = grad.astype(bf16)


def update_kernel(piece, basis_ref, last_ref, out_ref, done, sems):
    step, block = done.shape[1:]
    chosen = last_ref[:, :piece, :].reshape(block, RANK)
    copies = []
    for j in range(STEPS):
        at = slice(j * step, (j + 1) * step)
        update = lax.dot_general(
            basis_ref[at, :], chosen, (((1,), (1,)), ((), ())), preferred_element_type=f32
        )
        done[j] = (update * math.sqrt(FF / RANK)).astype(bf16)
        copies.append(pltpu.make_async_copy(done.at[j], out_ref.at[at, :], sems.at[j]))
        copies[-1].start()
    for copy in copies:
        copy.wait()


def update_call(basis, last, block, piece):
    rows = basis.shape[0]
    return pl.pallas_call(
        functools.partial(update_kernel, piece),
        in_specs=[VMEM, VMEM],
        out_specs=pl.BlockSpec(memory_space=pl.ANY),
        out_shape=jax.ShapeDtypeStruct((rows, block), bf16),
        scratch_shapes=[
            pltpu.VMEM((STEPS, rows // STEPS, block), bf16),
            pltpu.SemaphoreType.DMA((STEPS,)),
        ],
        compiler_params=kernel_params(),
    )(basis, last)


def owner_kernel(
    dims, me_ref, owners_ref, first_ref, second_ref, sums_ref, sums_other_ref, first_out, second_out
):
    chips, pairs, piece, per_block, slots = dims
    share = pairs * piece
    half = chips // per_block
    me = me_ref[0]
    ids_row = owners_ref[...]
    slot_row = plane_slots(ids_row)
    frags = ids_row.shape[1]
    at = iota((slots * FC, 1), 0)
    within = at % FC
    own = (ids_row == me) & (slot_row == at // FC)
    live = jnp.sum(own.astype(jnp.int32), axis=1, keepdims=True) > 0
    source = jnp.sum(jnp.where(own, iota((1, frags), 1), 0), axis=1, keepdims=True)
    b = source // per_block
    row = ((source % per_block) * half + within // piece) * share + (b // 2) * piece + within % piece
    row = jnp.where(live, row + (b % 2 != (me & 1)).astype(jnp.int32) * (chips * share), -1)
    cols = iota((1, chips * share), 1)
    hot = jnp.where(row == cols, 1.0, 0.0).astype(bf16)
    hot_other = jnp.where(row == cols + chips * share, 1.0, 0.0).astype(bf16)
    g = jnp.dot(hot, sums_ref[...], preferred_element_type=f32)
    g += jnp.dot(hot_other, sums_other_ref[...], preferred_element_type=f32)
    first, second = first_ref[...], second_ref[...]
    first_out[...] = jnp.where(live, first_keep * first + first_take * g, first)
    second_out[...] = jnp.where(live, second_keep * second + second_take * g * g, second)


def over(exchange, x, *rest):
    x, rest = lax.optimization_barrier((x, rest))
    return lax.optimization_barrier((exchange(x), rest))


def body(hidden, grad_out, basis, owners, first_moment, second_moment):
    owner_count = lax.axis_size("dp")
    planes = lax.axis_size("mp")
    chips = owner_count // 2
    tok, col = grad_out.shape
    slots = first_moment.shape[0] // FC
    frags = owners.shape[0]
    block = col * planes // owner_count
    per_block = block // FC
    piece = block // chips
    pairs = col // block // 2
    share = pairs * piece
    scale = 1.0 / math.sqrt(tok * owner_count)
    same_core = [[2 * k + c for k in range(chips)] for c in range(2)]
    swap = [(i, i ^ 1) for i in range(owner_count)]
    next_x = [(i, i ^ 2) for i in range(owner_count)]
    next_y = [(i, i ^ 8) for i in range(owner_count)]

    def other_core(x):
        return lax.ppermute(x, "dp", swap)

    def over_chips(x):
        return lax.all_to_all(x, "dp", 0, 0, axis_index_groups=same_core, tiled=True)

    def over_planes(x):
        return lax.all_to_all(x, "mp", 0, 0, tiled=True)

    me = lax.axis_index("dp").reshape(1)
    owners = owners.reshape(1, frags)

    even, odd = slice(0, None, 2), slice(1, None, 2)
    early, half = RANK // SQUARE, RANK // 2
    part = coeffs_call(hidden, basis)
    part, me, grad_out, first, second = lax.optimization_barrier(
        (part, me, grad_out, first_moment, second_moment)
    )
    go_mine, go_theirs, keep, send = sort_call(me, grad_out, first, second)
    got_x = lax.ppermute(send[:, :early], "dp", next_x[even])
    part, keep, send, got_x = lax.optimization_barrier((part, keep, send, got_x))
    part = over_planes(part)
    got_x = jnp.concatenate([got_x, lax.ppermute(send[:, early:], "dp", next_x[even])], axis=1)
    near = jnp.concatenate([keep, got_x], axis=0)
    got_y = lax.ppermute(near[:, half:], "dp", next_y[even])
    part, keep, send, got_x, got_y, go_mine, go_theirs, me, owners = lax.optimization_barrier(
        (part, keep, send, got_x, got_y, go_mine, go_theirs, me, owners)
    )
    part = part.reshape(planes, tok // planes, RANK)
    mine = jnp.sum(part.astype(f32), axis=0).astype(bf16)
    mine = jnp.broadcast_to(mine[None], part.shape).reshape(tok, RANK)
    coeffs = over_planes(mine)
    got_x = got_x + lax.ppermute(send, "dp", next_x[odd])
    near = jnp.concatenate([keep, got_x], axis=0)
    got_y = got_y + lax.ppermute(near[:, half:], "dp", next_y[odd])
    near = jnp.concatenate([near[:, :half], got_y], axis=0)
    near, go_theirs = lax.optimization_barrier((near, go_theirs))
    far = other_core(near)
    go_other = other_core(go_theirs)
    coeffs, near, far, go_mine, go_other, me, owners = lax.optimization_barrier(
        (coeffs, near, far, go_mine, go_other, me, owners)
    )
    coeffs_other = other_core(coeffs)

    dims = (chips, pairs, piece, per_block, slots, scale)
    payload_shape = jax.ShapeDtypeStruct((chips, share + piece, RANK), bf16)
    payload, proj = pl.pallas_call(
        functools.partial(payload_kernel, dims),
        in_specs=[SMEM] + [VMEM] * 5,
        out_specs=[VMEM, VMEM],
        out_shape=[payload_shape, jax.ShapeDtypeStruct((pairs * block, RANK), f32)],
        compiler_params=kernel_params(),
    )(me, owners, near, far, go_mine, coeffs)
    payload = pl.pallas_call(
        functools.partial(project_kernel, dims),
        in_specs=[VMEM] * 4,
        out_specs=VMEM,
        out_shape=payload_shape,
        input_output_aliases={3: 0},
        compiler_params=kernel_params(),
    )(go_other, coeffs_other, proj, payload)
    got, (me, owners) = over(over_chips, payload, me, owners)
    factor, grad = pl.pallas_call(
        functools.partial(factor_kernel, dims),
        in_specs=[SMEM] + [VMEM] * 2,
        out_specs=[VMEM, VMEM],
        out_shape=[
            jax.ShapeDtypeStruct((planes, share, RANK), bf16),
            jax.ShapeDtypeStruct((share, RANK), bf16),
        ],
        compiler_params=kernel_params(),
    )(me, owners, got)

    spread, (grad,) = over(over_planes, factor, grad)
    spread = spread.reshape(chips, piece, RANK)
    grad = jnp.broadcast_to(grad[None], (chips, share, RANK))
    last, (me, owners, first_moment, second_moment) = over(
        over_chips,
        jnp.concatenate([spread, grad], axis=1),
        me,
        owners,
        first_moment,
        second_moment,
    )
    sums = last[:, piece:].reshape(chips * share, RANK)
    sums_other = other_core(sums)
    update = update_call(basis, last, block, piece)

    like = jax.ShapeDtypeStruct(first_moment.shape, f32)
    new_first, new_second = pl.pallas_call(
        functools.partial(owner_kernel, dims[:5]),
        in_specs=[SMEM] + [VMEM] * 5,
        out_specs=[VMEM, VMEM],
        out_shape=[like, like],
        compiler_params=kernel_params(),
    )(me, owners, first_moment, second_moment, sums, sums_other)
    return (update, new_first, new_second)


def solution(mesh):
    placed = (
        P("dp", "mp"),
        P("dp", "mp"),
        P("mp", None),
        P("mp", None),
        P(("dp", "mp"), None),
        P(("dp", "mp"), None),
    )
    return jax.shard_map(
        body,
        mesh=mesh,
        in_specs=placed,
        out_specs=(P("mp", "dp"), P(("dp", "mp"), None), P(("dp", "mp"), None)),
        check_vma=False,
    )
```

```python
import functools
import math

import jax
import jax.numpy as jnp
from jax import lax
from jax.experimental import pallas as pl
from jax.experimental.pallas import tpu as pltpu
from jax.sharding import PartitionSpec as P

FF = 28672
RANK = 512
FC = 32
STEPS = 7
SQUARE = 4

first_keep = 0.9
first_take = 0.1
second_keep = 0.95
second_take = 0.05
adam_eps = 1e-08

bf16 = jnp.bfloat16
f32 = jnp.float32
VMEM = pl.BlockSpec(memory_space=pltpu.VMEM)
SMEM = pl.BlockSpec(memory_space=pltpu.SMEM)


def iota(shape, dim):
    return lax.broadcasted_iota(jnp.int32, shape, dim)


def kernel_params(mib=16):
    return pltpu.CompilerParams(vmem_limit_bytes=mib * 2**20)


def plane_slots(ids_row):
    n = ids_row.shape[1]
    f0, f1 = iota((n, n), 0), iota((n, n), 1)
    ids_col = jnp.sum(jnp.where(f0 == f1, ids_row, 0), axis=1, keepdims=True)
    same = ids_col == ids_row
    return jnp.sum((same & (f0 < f1)).astype(jnp.int32), axis=0, keepdims=True)


def in_square(chip):
    return (chip & 1) + 2 * ((chip >> 2) & 1), ((chip >> 1) & 1) + 2 * (chip >> 3)


def coeffs_kernel(hidden_ref, basis_ref, part_ref, hidden, basis, total, sems):
    step = hidden.shape[2]

    def chunk(j):
        at = slice(j * step, (j + 1) * step)
        return (
            pltpu.make_async_copy(hidden_ref.at[:, at], hidden.at[j], sems.at[2 * j]),
            pltpu.make_async_copy(basis_ref.at[at, :], basis.at[j], sems.at[2 * j + 1]),
        )

    chunks = [chunk(j) for j in range(STEPS)]
    for pair in chunks:
        for copy in pair:
            copy.start()
    for j in range(STEPS):
        for copy in chunks[j]:
            copy.wait()
        term = jnp.dot(hidden[j], basis[j], preferred_element_type=f32)
        if j == 0:
            total[...] = term
        elif j < STEPS - 1:
            total[...] += term
        else:
            part_ref[...] = (total[...] + term).astype(bf16)


def coeffs_call(hidden, basis):
    tok, ff = hidden.shape
    step = ff // STEPS
    return pl.pallas_call(
        coeffs_kernel,
        in_specs=[pl.BlockSpec(memory_space=pl.ANY)] * 2,
        out_specs=VMEM,
        out_shape=jax.ShapeDtypeStruct((tok, RANK), bf16),
        scratch_shapes=[
            pltpu.VMEM((STEPS, tok, step), bf16),
            pltpu.VMEM((STEPS, step, RANK), bf16),
            pltpu.VMEM((tok, RANK), f32),
            pltpu.SemaphoreType.DMA((2 * STEPS,)),
        ],
        compiler_params=kernel_params(56),
    )(hidden, basis)


def sort_kernel(me_ref, go_ref, first_ref, second_ref, mine_ref, other_ref, keep_ref, send_ref):
    even = (me_ref[0] & 1) == 0
    width = go_ref.shape[1] // 4
    for p in range(2):
        low = go_ref[:, (2 * p) * width : (2 * p + 1) * width]
        high = go_ref[:, (2 * p + 1) * width : (2 * p + 2) * width]
        mine_ref[:, p * width : (p + 1) * width] = jnp.where(even, low, high)
        other_ref[:, p * width : (p + 1) * width] = jnp.where(even, high, low)
    place = in_square(me_ref[0] >> 1)[0]
    width = RANK // SQUARE
    for n, ref in enumerate((first_ref, second_ref)):
        old = [ref[:, q * width : (q + 1) * width].astype(bf16) for q in range(SQUARE)]
        for d, out in enumerate((keep_ref, send_ref)):
            for e in range(2):
                at = slice((2 * e + n) * width, (2 * e + n + 1) * width)
                q = place ^ (d + 2 * e)
                low = jnp.where((q & 1) == 0, old[0], old[1])
                high = jnp.where((q & 1) == 0, old[2], old[3])
                out[:, at] = jnp.where(q < 2, low, high)


def sort_call(me, go, first, second):
    tok, col = go.shape
    like = lambda *shape: jax.ShapeDtypeStruct(shape, bf16)
    return pl.pallas_call(
        sort_kernel,
        in_specs=[SMEM] + [VMEM] * 3,
        out_specs=[VMEM] * 4,
        out_shape=[
            like(tok, col // 2),
            like(tok, col // 2),
            like(first.shape[0], RANK),
            like(first.shape[0], RANK),
        ],
        compiler_params=kernel_params(),
        cost_estimate=pl.CostEstimate(flops=2**28, bytes_accessed=2**24, transcendentals=0),
    )(me, go, first, second)


OVER_TOKENS = (((0,), (0,)), ((), ()))


def payload_kernel(
    dims, me_ref, owners_ref, near_ref, far_ref, mine_ref, co_ref, out_ref, proj_ref
):
    chips, pairs, piece, per_block, slots, _ = dims
    share = pairs * piece
    half = chips // per_block
    held = slots * FC
    core = me_ref[0] & 1
    chip = me_ref[0] >> 1
    ids_row = owners_ref[...]
    slot_row = plane_slots(ids_row)
    frags = ids_row.shape[1]
    at = iota((chips * share, 1), 0)
    k_of, p_of, r_of = at // share, (at // piece) % pairs, at % piece
    frag = (core + 2 * p_of) * per_block + k_of // half
    base = ((ids_row & 1) != core).astype(jnp.int32) * (SQUARE * held) + slot_row * FC
    base += (in_square(ids_row >> 1)[0] ^ in_square(chip)[0]) * held
    rows = jnp.sum(jnp.where(frag == iota((1, frags), 1), base, 0), axis=1, keepdims=True)
    rows = rows + (k_of % half) * piece + r_of
    cols = iota((1, SQUARE * held), 1)
    hot = jnp.where(rows == cols, 1.0, 0.0).astype(bf16)
    hot_far = jnp.where(rows == cols + SQUARE * held, 1.0, 0.0).astype(bf16)
    old = jnp.dot(hot, near_ref[...], preferred_element_type=f32)
    old += jnp.dot(hot_far, far_ref[...], preferred_element_type=f32)
    old = old.astype(bf16).reshape(chips, pairs, piece, near_ref.shape[1])
    for p in range(pairs):
        out_ref[:, share:, p * old.shape[3] : (p + 1) * old.shape[3]] = old[:, p]
    proj_ref[...] = lax.dot_general(
        mine_ref[...], co_ref[...], OVER_TOKENS, preferred_element_type=f32
    )


def project_kernel(dims, other_ref, co_other_ref, proj_ref, part_ref, out_ref):
    chips, pairs, piece, _, _, scale = dims
    proj = proj_ref[...] + lax.dot_general(
        other_ref[...], co_other_ref[...], OVER_TOKENS, preferred_element_type=f32
    )
    proj = (proj * scale).astype(bf16).reshape(pairs, chips, piece, RANK)
    for p in range(pairs):
        out_ref[:, p * piece : (p + 1) * piece, :] = proj[p]


def factor_kernel(dims, me_ref, owners_ref, got_ref, factor_ref, grad_ref):
    chips, pairs, piece, per_block, _, _ = dims
    share = pairs * piece
    core = me_ref[0] & 1
    chip = me_ref[0] >> 1
    ids_row = owners_ref[...]
    grad = jnp.zeros((share, RANK), f32)
    for k in range(chips):
        grad += got_ref[k, :share, :].astype(f32)
    width = RANK // SQUARE
    parts = []
    for p in range(pairs):
        frag = (core + 2 * p) * per_block + chip // (chips // per_block)
        sender = jnp.where(iota(ids_row.shape, 1) == frag, ids_row, 0)
        square = in_square(jnp.sum(sender, axis=1, keepdims=True) >> 1)[1]
        old = [jnp.zeros((piece, 2 * width), f32) for _ in range(SQUARE)]
        for k in range(chips):
            place, number = in_square(k)
            sent = got_ref[k, share:, 2 * p * width : (2 * p + 2) * width].astype(f32)
            old[place] = jnp.where(square == number, sent, old[place])
        parts.append(old)
    first, second = (
        jnp.concatenate(
            [
                jnp.concatenate([o[:, n * width : (n + 1) * width] for o in old], axis=1)
                for old in parts
            ],
            axis=0,
        )
        for n in range(2)
    )
    first = first_keep * first + first_take * grad
    second = second_keep * second + second_take * grad * grad
    factor = (first / (jnp.sqrt(second) + adam_eps)).astype(bf16)
    for m in range(factor_ref.shape[0]):
        factor_ref[m] = factor
    grad_ref[...] = grad.astype(bf16)


def update_kernel(piece, basis_ref, last_ref, out_ref, done, sems):
    step, block = done.shape[1:]
    chosen = last_ref[:, :piece, :].reshape(block, RANK)
    copies = []
    for j in range(STEPS):
        at = slice(j * step, (j + 1) * step)
        update = lax.dot_general(
            basis_ref[at, :], chosen, (((1,), (1,)), ((), ())), preferred_element_type=f32
        )
        done[j] = (update * math.sqrt(FF / RANK)).astype(bf16)
        copies.append(pltpu.make_async_copy(done.at[j], out_ref.at[at, :], sems.at[j]))
        copies[-1].start()
    for copy in copies:
        copy.wait()


def update_call(basis, last, block, piece):
    rows = basis.shape[0]
    return pl.pallas_call(
        functools.partial(update_kernel, piece),
        in_specs=[VMEM, VMEM],
        out_specs=pl.BlockSpec(memory_space=pl.ANY),
        out_shape=jax.ShapeDtypeStruct((rows, block), bf16),
        scratch_shapes=[
            pltpu.VMEM((STEPS, rows // STEPS, block), bf16),
            pltpu.SemaphoreType.DMA((STEPS,)),
        ],
        compiler_params=kernel_params(),
    )(basis, last)


def owner_kernel(
    dims, me_ref, owners_ref, first_ref, second_ref, sums_ref, sums_other_ref, first_out, second_out
):
    chips, pairs, piece, per_block, slots = dims
    share = pairs * piece
    half = chips // per_block
    me = me_ref[0]
    ids_row = owners_ref[...]
    slot_row = plane_slots(ids_row)
    frags = ids_row.shape[1]
    at = iota((slots * FC, 1), 0)
    within = at % FC
    own = (ids_row == me) & (slot_row == at // FC)
    live = jnp.sum(own.astype(jnp.int32), axis=1, keepdims=True) > 0
    source = jnp.sum(jnp.where(own, iota((1, frags), 1), 0), axis=1, keepdims=True)
    b = source // per_block
    row = ((source % per_block) * half + within // piece) * share + (b // 2) * piece + within % piece
    row = jnp.where(live, row + (b % 2 != (me & 1)).astype(jnp.int32) * (chips * share), -1)
    cols = iota((1, chips * share), 1)
    hot = jnp.where(row == cols, 1.0, 0.0).astype(bf16)
    hot_other = jnp.where(row == cols + chips * share, 1.0, 0.0).astype(bf16)
    g = jnp.dot(hot, sums_ref[...], preferred_element_type=f32)
    g += jnp.dot(hot_other, sums_other_ref[...], preferred_element_type=f32)
    first, second = first_ref[...], second_ref[...]
    first_out[...] = jnp.where(live, first_keep * first + first_take * g, first)
    second_out[...] = jnp.where(live, second_keep * second + second_take * g * g, second)


def over(exchange, x, *rest):
    x, rest = lax.optimization_barrier((x, rest))
    return lax.optimization_barrier((exchange(x), rest))


def body(hidden, grad_out, basis, owners, first_moment, second_moment):
    owner_count = lax.axis_size("dp")
    planes = lax.axis_size("mp")
    chips = owner_count // 2
    tok, col = grad_out.shape
    slots = first_moment.shape[0] // FC
    frags = owners.shape[0]
    block = col * planes // owner_count
    per_block = block // FC
    piece = block // chips
    pairs = col // block // 2
    share = pairs * piece
    scale = 1.0 / math.sqrt(tok * owner_count)
    same_core = [[2 * k + c for k in range(chips)] for c in range(2)]
    swap = [(i, i ^ 1) for i in range(owner_count)]
    next_x = [(i, i ^ 2) for i in range(owner_count)]
    next_y = [(i, i ^ 8) for i in range(owner_count)]

    def other_core(x):
        return lax.ppermute(x, "dp", swap)

    def over_chips(x):
        return lax.all_to_all(x, "dp", 0, 0, axis_index_groups=same_core, tiled=True)

    def over_planes(x):
        return lax.all_to_all(x, "mp", 0, 0, tiled=True)

    me = lax.axis_index("dp").reshape(1)
    owners = owners.reshape(1, frags)

    even, odd = slice(0, None, 2), slice(1, None, 2)
    early, half = RANK // SQUARE, RANK // 2
    part = coeffs_call(hidden, basis)
    part, me, grad_out, first, second = lax.optimization_barrier(
        (part, me, grad_out, first_moment, second_moment)
    )
    go_mine, go_theirs, keep, send = sort_call(me, grad_out, first, second)
    got_x = lax.ppermute(send[:, :early], "dp", next_x[even])
    part, keep, send, got_x = lax.optimization_barrier((part, keep, send, got_x))
    part = over_planes(part)
    got_x = jnp.concatenate([got_x, lax.ppermute(send[:, early:], "dp", next_x[even])], axis=1)
    part, keep, send, got_x, go_mine, go_theirs, me, owners = lax.optimization_barrier(
        (part, keep, send, got_x, go_mine, go_theirs, me, owners)
    )
    part = part.reshape(planes, tok // planes, RANK)
    mine = jnp.sum(part.astype(f32), axis=0).astype(bf16)
    mine = jnp.broadcast_to(mine[None], part.shape).reshape(tok, RANK)
    mine, send = lax.optimization_barrier((mine, send))
    coeffs = over_planes(mine)
    got_x = got_x + lax.ppermute(send, "dp", next_x[odd])
    near = jnp.concatenate([keep, got_x], axis=0)
    got_y = lax.ppermute(near[:, half:], "dp", next_y)
    near = jnp.concatenate([near[:, :half], got_y], axis=0)
    near, go_theirs = lax.optimization_barrier((near, go_theirs))
    far = other_core(near)
    go_other = other_core(go_theirs)
    coeffs, near, far, go_mine, go_other, me, owners = lax.optimization_barrier(
        (coeffs, near, far, go_mine, go_other, me, owners)
    )
    coeffs_other = other_core(coeffs)

    dims = (chips, pairs, piece, per_block, slots, scale)
    payload_shape = jax.ShapeDtypeStruct((chips, share + piece, RANK), bf16)
    payload, proj = pl.pallas_call(
        functools.partial(payload_kernel, dims),
        in_specs=[SMEM] + [VMEM] * 5,
        out_specs=[VMEM, VMEM],
        out_shape=[payload_shape, jax.ShapeDtypeStruct((pairs * block, RANK), f32)],
        compiler_params=kernel_params(),
    )(me, owners, near, far, go_mine, coeffs)
    payload = pl.pallas_call(
        functools.partial(project_kernel, dims),
        in_specs=[VMEM] * 4,
        out_specs=VMEM,
        out_shape=payload_shape,
        input_output_aliases={3: 0},
        compiler_params=kernel_params(),
    )(go_other, coeffs_other, proj, payload)
    got, (me, owners) = over(over_chips, payload, me, owners)
    factor, grad = pl.pallas_call(
        functools.partial(factor_kernel, dims),
        in_specs=[SMEM] + [VMEM] * 2,
        out_specs=[VMEM, VMEM],
        out_shape=[
            jax.ShapeDtypeStruct((planes, share, RANK), bf16),
            jax.ShapeDtypeStruct((share, RANK), bf16),
        ],
        compiler_params=kernel_params(),
    )(me, owners, got)

    spread, (grad,) = over(over_planes, factor, grad)
    spread = spread.reshape(chips, piece, RANK)
    grad = jnp.broadcast_to(grad[None], (chips, share, RANK))
    last, (me, owners, first_moment, second_moment) = over(
        over_chips,
        jnp.concatenate([spread, grad], axis=1),
        me,
        owners,
        first_moment,
        second_moment,
    )
    sums = last[:, piece:].reshape(chips * share, RANK)
    sums_other = other_core(sums)
    update = update_call(basis, last, block, piece)

    like = jax.ShapeDtypeStruct(first_moment.shape, f32)
    new_first, new_second = pl.pallas_call(
        functools.partial(owner_kernel, dims[:5]),
        in_specs=[SMEM] + [VMEM] * 5,
        out_specs=[VMEM, VMEM],
        out_shape=[like, like],
        compiler_params=kernel_params(),
    )(me, owners, first_moment, second_moment, sums, sums_other)
    return (update, new_first, new_second)


def solution(mesh):
    placed = (
        P("dp", "mp"),
        P("dp", "mp"),
        P("mp", None),
        P("mp", None),
        P(("dp", "mp"), None),
        P(("dp", "mp"), None),
    )
    return jax.shard_map(
        body,
        mesh=mesh,
        in_specs=placed,
        out_specs=(P("mp", "dp"), P(("dp", "mp"), None), P(("dp", "mp"), None)),
        check_vma=False,
    )
```

```python
import functools
import math

import jax
import jax.numpy as jnp
from jax import lax
from jax.experimental import pallas as pl
from jax.experimental.pallas import tpu as pltpu
from jax.sharding import PartitionSpec as P

FF = 28672
RANK = 512
FC = 32
STEPS = 7
SQUARE = 4

first_keep = 0.9
first_take = 0.1
second_keep = 0.95
second_take = 0.05
adam_eps = 1e-08

bf16 = jnp.bfloat16
f32 = jnp.float32
VMEM = pl.BlockSpec(memory_space=pltpu.VMEM)
SMEM = pl.BlockSpec(memory_space=pltpu.SMEM)


def iota(shape, dim):
    return lax.broadcasted_iota(jnp.int32, shape, dim)


def kernel_params(mib=16):
    return pltpu.CompilerParams(vmem_limit_bytes=mib * 2**20)


def plane_slots(ids_row):
    n = ids_row.shape[1]
    f0, f1 = iota((n, n), 0), iota((n, n), 1)
    ids_col = jnp.sum(jnp.where(f0 == f1, ids_row, 0), axis=1, keepdims=True)
    same = ids_col == ids_row
    return jnp.sum((same & (f0 < f1)).astype(jnp.int32), axis=0, keepdims=True)


def in_square(chip):
    return (chip & 1) + 2 * ((chip >> 2) & 1), ((chip >> 1) & 1) + 2 * (chip >> 3)


def coeffs_kernel(hidden_ref, basis_ref, part_ref, hidden, basis, total, sems):
    step = hidden.shape[2]

    def chunk(j):
        at = slice(j * step, (j + 1) * step)
        return (
            pltpu.make_async_copy(hidden_ref.at[:, at], hidden.at[j], sems.at[2 * j]),
            pltpu.make_async_copy(basis_ref.at[at, :], basis.at[j], sems.at[2 * j + 1]),
        )

    chunks = [chunk(j) for j in range(STEPS)]
    for pair in chunks:
        for copy in pair:
            copy.start()
    for j in range(STEPS):
        for copy in chunks[j]:
            copy.wait()
        term = jnp.dot(hidden[j], basis[j], preferred_element_type=f32)
        if j == 0:
            total[...] = term
        elif j < STEPS - 1:
            total[...] += term
        else:
            part_ref[...] = (total[...] + term).astype(bf16)


def coeffs_call(hidden, basis):
    tok, ff = hidden.shape
    step = ff // STEPS
    return pl.pallas_call(
        coeffs_kernel,
        in_specs=[pl.BlockSpec(memory_space=pl.ANY)] * 2,
        out_specs=VMEM,
        out_shape=jax.ShapeDtypeStruct((tok, RANK), bf16),
        scratch_shapes=[
            pltpu.VMEM((STEPS, tok, step), bf16),
            pltpu.VMEM((STEPS, step, RANK), bf16),
            pltpu.VMEM((tok, RANK), f32),
            pltpu.SemaphoreType.DMA((2 * STEPS,)),
        ],
        compiler_params=kernel_params(56),
    )(hidden, basis)


def sort_kernel(me_ref, go_ref, first_ref, second_ref, mine_ref, other_ref, keep_ref, send_ref):
    even = (me_ref[0] & 1) == 0
    width = go_ref.shape[1] // 4
    for p in range(2):
        low = go_ref[:, (2 * p) * width : (2 * p + 1) * width]
        high = go_ref[:, (2 * p + 1) * width : (2 * p + 2) * width]
        mine_ref[:, p * width : (p + 1) * width] = jnp.where(even, low, high)
        other_ref[:, p * width : (p + 1) * width] = jnp.where(even, high, low)
    place = in_square(me_ref[0] >> 1)[0]
    width = RANK // SQUARE
    for n, ref in enumerate((first_ref, second_ref)):
        old = [ref[:, q * width : (q + 1) * width].astype(bf16) for q in range(SQUARE)]
        for d, out in enumerate((keep_ref, send_ref)):
            for e in range(2):
                at = slice((2 * e + n) * width, (2 * e + n + 1) * width)
                q = place ^ (d + 2 * e)
                low = jnp.where((q & 1) == 0, old[0], old[1])
                high = jnp.where((q & 1) == 0, old[2], old[3])
                out[:, at] = jnp.where(q < 2, low, high)


def sort_call(me, go, first, second):
    tok, col = go.shape
    like = lambda *shape: jax.ShapeDtypeStruct(shape, bf16)
    return pl.pallas_call(
        sort_kernel,
        in_specs=[SMEM] + [VMEM] * 3,
        out_specs=[VMEM] * 4,
        out_shape=[
            like(tok, col // 2),
            like(tok, col // 2),
            like(first.shape[0], RANK),
            like(first.shape[0], RANK),
        ],
        compiler_params=kernel_params(),
        cost_estimate=pl.CostEstimate(flops=2**28, bytes_accessed=2**24, transcendentals=0),
    )(me, go, first, second)


OVER_TOKENS = (((0,), (0,)), ((), ()))


def payload_kernel(
    dims, me_ref, owners_ref, near_ref, far_ref, mine_ref, co_ref, out_ref, proj_ref
):
    chips, pairs, piece, per_block, slots, _ = dims
    share = pairs * piece
    half = chips // per_block
    held = slots * FC
    core = me_ref[0] & 1
    chip = me_ref[0] >> 1
    ids_row = owners_ref[...]
    slot_row = plane_slots(ids_row)
    frags = ids_row.shape[1]
    at = iota((chips * share, 1), 0)
    k_of, p_of, r_of = at // share, (at // piece) % pairs, at % piece
    frag = (core + 2 * p_of) * per_block + k_of // half
    base = ((ids_row & 1) != core).astype(jnp.int32) * (SQUARE * held) + slot_row * FC
    base += (in_square(ids_row >> 1)[0] ^ in_square(chip)[0]) * held
    rows = jnp.sum(jnp.where(frag == iota((1, frags), 1), base, 0), axis=1, keepdims=True)
    rows = rows + (k_of % half) * piece + r_of
    cols = iota((1, SQUARE * held), 1)
    hot = jnp.where(rows == cols, 1.0, 0.0).astype(bf16)
    hot_far = jnp.where(rows == cols + SQUARE * held, 1.0, 0.0).astype(bf16)
    old = jnp.dot(hot, near_ref[...], preferred_element_type=f32)
    old += jnp.dot(hot_far, far_ref[...], preferred_element_type=f32)
    old = old.astype(bf16).reshape(chips, pairs, piece, near_ref.shape[1])
    for p in range(pairs):
        out_ref[:, share:, p * old.shape[3] : (p + 1) * old.shape[3]] = old[:, p]
    proj_ref[...] = lax.dot_general(
        mine_ref[...], co_ref[...], OVER_TOKENS, preferred_element_type=f32
    )


def project_kernel(dims, other_ref, co_other_ref, proj_ref, part_ref, out_ref):
    chips, pairs, piece, _, _, scale = dims
    proj = proj_ref[...] + lax.dot_general(
        other_ref[...], co_other_ref[...], OVER_TOKENS, preferred_element_type=f32
    )
    proj = (proj * scale).astype(bf16).reshape(pairs, chips, piece, RANK)
    for p in range(pairs):
        out_ref[:, p * piece : (p + 1) * piece, :] = proj[p]


def factor_kernel(dims, me_ref, owners_ref, got_ref, factor_ref, grad_ref):
    chips, pairs, piece, per_block, _, _ = dims
    share = pairs * piece
    core = me_ref[0] & 1
    chip = me_ref[0] >> 1
    ids_row = owners_ref[...]
    grad = jnp.zeros((share, RANK), f32)
    for k in range(chips):
        grad += got_ref[k, :share, :].astype(f32)
    width = RANK // SQUARE
    parts = []
    for p in range(pairs):
        frag = (core + 2 * p) * per_block + chip // (chips // per_block)
        sender = jnp.where(iota(ids_row.shape, 1) == frag, ids_row, 0)
        square = in_square(jnp.sum(sender, axis=1, keepdims=True) >> 1)[1]
        old = [jnp.zeros((piece, 2 * width), f32) for _ in range(SQUARE)]
        for k in range(chips):
            place, number = in_square(k)
            sent = got_ref[k, share:, 2 * p * width : (2 * p + 2) * width].astype(f32)
            old[place] = jnp.where(square == number, sent, old[place])
        parts.append(old)
    first, second = (
        jnp.concatenate(
            [
                jnp.concatenate([o[:, n * width : (n + 1) * width] for o in old], axis=1)
                for old in parts
            ],
            axis=0,
        )
        for n in range(2)
    )
    first = first_keep * first + first_take * grad
    second = second_keep * second + second_take * grad * grad
    factor = (first / (jnp.sqrt(second) + adam_eps)).astype(bf16)
    for m in range(factor_ref.shape[0]):
        factor_ref[m] = factor
    grad_ref[...] = grad.astype(bf16)


def update_kernel(piece, basis_ref, last_ref, out_ref, done, sems):
    step, block = done.shape[1:]
    chosen = last_ref[:, :piece, :].reshape(block, RANK)
    copies = []
    for j in range(STEPS):
        at = slice(j * step, (j + 1) * step)
        update = lax.dot_general(
            basis_ref[at, :], chosen, (((1,), (1,)), ((), ())), preferred_element_type=f32
        )
        done[j] = (update * math.sqrt(FF / RANK)).astype(bf16)
        copies.append(pltpu.make_async_copy(done.at[j], out_ref.at[at, :], sems.at[j]))
        copies[-1].start()
    for copy in copies:
        copy.wait()


def update_call(basis, last, block, piece):
    rows = basis.shape[0]
    return pl.pallas_call(
        functools.partial(update_kernel, piece),
        in_specs=[VMEM, VMEM],
        out_specs=pl.BlockSpec(memory_space=pl.ANY),
        out_shape=jax.ShapeDtypeStruct((rows, block), bf16),
        scratch_shapes=[
            pltpu.VMEM((STEPS, rows // STEPS, block), bf16),
            pltpu.SemaphoreType.DMA((STEPS,)),
        ],
        compiler_params=kernel_params(),
    )(basis, last)


def owner_kernel(
    dims, me_ref, owners_ref, first_ref, second_ref, sums_ref, sums_other_ref, first_out, second_out
):
    chips, pairs, piece, per_block, slots = dims
    share = pairs * piece
    half = chips // per_block
    me = me_ref[0]
    ids_row = owners_ref[...]
    slot_row = plane_slots(ids_row)
    frags = ids_row.shape[1]
    at = iota((slots * FC, 1), 0)
    within = at % FC
    own = (ids_row == me) & (slot_row == at // FC)
    live = jnp.sum(own.astype(jnp.int32), axis=1, keepdims=True) > 0
    source = jnp.sum(jnp.where(own, iota((1, frags), 1), 0), axis=1, keepdims=True)
    b = source // per_block
    row = ((source % per_block) * half + within // piece) * share + (b // 2) * piece + within % piece
    row = jnp.where(live, row + (b % 2 != (me & 1)).astype(jnp.int32) * (chips * share), -1)
    cols = iota((1, chips * share), 1)
    hot = jnp.where(row == cols, 1.0, 0.0).astype(bf16)
    hot_other = jnp.where(row == cols + chips * share, 1.0, 0.0).astype(bf16)
    g = jnp.dot(hot, sums_ref[...], preferred_element_type=f32)
    g += jnp.dot(hot_other, sums_other_ref[...], preferred_element_type=f32)
    first, second = first_ref[...], second_ref[...]
    first_out[...] = jnp.where(live, first_keep * first + first_take * g, first)
    second_out[...] = jnp.where(live, second_keep * second + second_take * g * g, second)


def over(exchange, x, *rest):
    x, rest = lax.optimization_barrier((x, rest))
    return lax.optimization_barrier((exchange(x), rest))


def body(hidden, grad_out, basis, owners, first_moment, second_moment):
    owner_count = lax.axis_size("dp")
    planes = lax.axis_size("mp")
    chips = owner_count // 2
    tok, col = grad_out.shape
    slots = first_moment.shape[0] // FC
    frags = owners.shape[0]
    block = col * planes // owner_count
    per_block = block // FC
    piece = block // chips
    pairs = col // block // 2
    share = pairs * piece
    scale = 1.0 / math.sqrt(tok * owner_count)
    same_core = [[2 * k + c for k in range(chips)] for c in range(2)]
    swap = [(i, i ^ 1) for i in range(owner_count)]
    next_x = [(i, i ^ 2) for i in range(owner_count)]
    next_y = [(i, i ^ 8) for i in range(owner_count)]

    def other_core(x):
        return lax.ppermute(x, "dp", swap)

    def over_chips(x):
        return lax.all_to_all(x, "dp", 0, 0, axis_index_groups=same_core, tiled=True)

    def over_planes(x):
        return lax.all_to_all(x, "mp", 0, 0, tiled=True)

    me = lax.axis_index("dp").reshape(1)
    owners = owners.reshape(1, frags)

    even, odd = slice(0, None, 2), slice(1, None, 2)
    early, half = RANK // SQUARE, RANK // 2
    part = coeffs_call(hidden, basis)
    part, me, grad_out, first, second = lax.optimization_barrier(
        (part, me, grad_out, first_moment, second_moment)
    )
    go_mine, go_theirs, keep, send = sort_call(me, grad_out, first, second)
    got_x = lax.ppermute(send[:, :early], "dp", next_x[even])
    part, keep, send, got_x = lax.optimization_barrier((part, keep, send, got_x))
    part = over_planes(part)
    got_x = jnp.concatenate([got_x, lax.ppermute(send[:, early:], "dp", next_x[even])], axis=1)
    part, keep, got_x, go_mine, go_theirs, me, owners = lax.optimization_barrier(
        (part, keep, got_x, go_mine, go_theirs, me, owners)
    )
    part = part.reshape(planes, tok // planes, RANK)
    mine = jnp.sum(part.astype(f32), axis=0).astype(bf16)
    mine = jnp.broadcast_to(mine[None], part.shape).reshape(tok, RANK)
    coeffs = over_planes(mine)
    got_x = got_x + lax.ppermute(send, "dp", next_x[odd])
    near = jnp.concatenate([keep, got_x], axis=0)
    got_y = lax.ppermute(near[:, half:], "dp", next_y)
    near = jnp.concatenate([near[:, :half], got_y], axis=0)
    near, go_theirs = lax.optimization_barrier((near, go_theirs))
    far = other_core(near)
    go_other = other_core(go_theirs)
    coeffs, near, far, go_mine, go_other, me, owners = lax.optimization_barrier(
        (coeffs, near, far, go_mine, go_other, me, owners)
    )
    coeffs_other = other_core(coeffs)

    dims = (chips, pairs, piece, per_block, slots, scale)
    payload_shape = jax.ShapeDtypeStruct((chips, share + piece, RANK), bf16)
    payload, proj = pl.pallas_call(
        functools.partial(payload_kernel, dims),
        in_specs=[SMEM] + [VMEM] * 5,
        out_specs=[VMEM, VMEM],
        out_shape=[payload_shape, jax.ShapeDtypeStruct((pairs * block, RANK), f32)],
        compiler_params=kernel_params(),
    )(me, owners, near, far, go_mine, coeffs)
    payload = pl.pallas_call(
        functools.partial(project_kernel, dims),
        in_specs=[VMEM] * 4,
        out_specs=VMEM,
        out_shape=payload_shape,
        input_output_aliases={3: 0},
        compiler_params=kernel_params(),
    )(go_other, coeffs_other, proj, payload)
    got, (me, owners) = over(over_chips, payload, me, owners)
    factor, grad = pl.pallas_call(
        functools.partial(factor_kernel, dims),
        in_specs=[SMEM] + [VMEM] * 2,
        out_specs=[VMEM, VMEM],
        out_shape=[
            jax.ShapeDtypeStruct((planes, share, RANK), bf16),
            jax.ShapeDtypeStruct((share, RANK), bf16),
        ],
        compiler_params=kernel_params(),
    )(me, owners, got)

    spread, (grad,) = over(over_planes, factor, grad)
    spread = spread.reshape(chips, piece, RANK)
    grad = jnp.broadcast_to(grad[None], (chips, share, RANK))
    last, (me, owners, first_moment, second_moment) = over(
        over_chips,
        jnp.concatenate([spread, grad], axis=1),
        me,
        owners,
        first_moment,
        second_moment,
    )
    sums = last[:, piece:].reshape(chips * share, RANK)
    sums_other = other_core(sums)
    update = update_call(basis, last, block, piece)

    like = jax.ShapeDtypeStruct(first_moment.shape, f32)
    new_first, new_second = pl.pallas_call(
        functools.partial(owner_kernel, dims[:5]),
        in_specs=[SMEM] + [VMEM] * 5,
        out_specs=[VMEM, VMEM],
        out_shape=[like, like],
        compiler_params=kernel_params(),
    )(me, owners, first_moment, second_moment, sums, sums_other)
    return (update, new_first, new_second)


def solution(mesh):
    placed = (
        P("dp", "mp"),
        P("dp", "mp"),
        P("mp", None),
        P("mp", None),
        P(("dp", "mp"), None),
        P(("dp", "mp"), None),
    )
    return jax.shard_map(
        body,
        mesh=mesh,
        in_specs=placed,
        out_specs=(P("mp", "dp"), P(("dp", "mp"), None), P(("dp", "mp"), None)),
        check_vma=False,
    )
```

```python
import functools
import math

import jax
import jax.numpy as jnp
from jax import lax
from jax.experimental import pallas as pl
from jax.experimental.pallas import tpu as pltpu
from jax.sharding import PartitionSpec as P

FF = 28672
RANK = 512
FC = 32
STEPS = 7
SQUARE = 4

first_keep = 0.9
first_take = 0.1
second_keep = 0.95
second_take = 0.05
adam_eps = 1e-08

bf16 = jnp.bfloat16
f32 = jnp.float32
VMEM = pl.BlockSpec(memory_space=pltpu.VMEM)
SMEM = pl.BlockSpec(memory_space=pltpu.SMEM)


def iota(shape, dim):
    return lax.broadcasted_iota(jnp.int32, shape, dim)


def kernel_params(mib=16):
    return pltpu.CompilerParams(vmem_limit_bytes=mib * 2**20)


def plane_slots(ids_row):
    n = ids_row.shape[1]
    f0, f1 = iota((n, n), 0), iota((n, n), 1)
    ids_col = jnp.sum(jnp.where(f0 == f1, ids_row, 0), axis=1, keepdims=True)
    same = ids_col == ids_row
    return jnp.sum((same & (f0 < f1)).astype(jnp.int32), axis=0, keepdims=True)


def in_square(chip):
    return (chip & 1) + 2 * ((chip >> 2) & 1), ((chip >> 1) & 1) + 2 * (chip >> 3)


def coeffs_kernel(hidden_ref, basis_ref, part_ref, hidden, basis, total, sems):
    step = hidden.shape[2]

    def chunk(j):
        at = slice(j * step, (j + 1) * step)
        return (
            pltpu.make_async_copy(hidden_ref.at[:, at], hidden.at[j], sems.at[2 * j]),
            pltpu.make_async_copy(basis_ref.at[at, :], basis.at[j], sems.at[2 * j + 1]),
        )

    chunks = [chunk(j) for j in range(STEPS)]
    for pair in chunks:
        for copy in pair:
            copy.start()
    for j in range(STEPS):
        for copy in chunks[j]:
            copy.wait()
        term = jnp.dot(hidden[j], basis[j], preferred_element_type=f32)
        if j == 0:
            total[...] = term
        elif j < STEPS - 1:
            total[...] += term
        else:
            part_ref[...] = (total[...] + term).astype(bf16)


def coeffs_call(hidden, basis):
    tok, ff = hidden.shape
    step = ff // STEPS
    return pl.pallas_call(
        coeffs_kernel,
        in_specs=[pl.BlockSpec(memory_space=pl.ANY)] * 2,
        out_specs=VMEM,
        out_shape=jax.ShapeDtypeStruct((tok, RANK), bf16),
        scratch_shapes=[
            pltpu.VMEM((STEPS, tok, step), bf16),
            pltpu.VMEM((STEPS, step, RANK), bf16),
            pltpu.VMEM((tok, RANK), f32),
            pltpu.SemaphoreType.DMA((2 * STEPS,)),
        ],
        compiler_params=kernel_params(56),
    )(hidden, basis)


def sort_kernel(me_ref, go_ref, first_ref, second_ref, mine_ref, other_ref, keep_ref, send_ref):
    even = (me_ref[0] & 1) == 0
    width = go_ref.shape[1] // 4
    for p in range(2):
        low = go_ref[:, (2 * p) * width : (2 * p + 1) * width]
        high = go_ref[:, (2 * p + 1) * width : (2 * p + 2) * width]
        mine_ref[:, p * width : (p + 1) * width] = jnp.where(even, low, high)
        other_ref[:, p * width : (p + 1) * width] = jnp.where(even, high, low)
    place = in_square(me_ref[0] >> 1)[0]
    width = RANK // SQUARE
    for n, ref in enumerate((first_ref, second_ref)):
        old = [ref[:, q * width : (q + 1) * width].astype(bf16) for q in range(SQUARE)]
        for d, out in enumerate((keep_ref, send_ref)):
            for e in range(2):
                at = slice((2 * e + n) * width, (2 * e + n + 1) * width)
                q = place ^ (d + 2 * e)
                low = jnp.where((q & 1) == 0, old[0], old[1])
                high = jnp.where((q & 1) == 0, old[2], old[3])
                out[:, at] = jnp.where(q < 2, low, high)


def sort_call(me, go, first, second):
    tok, col = go.shape
    like = lambda *shape: jax.ShapeDtypeStruct(shape, bf16)
    return pl.pallas_call(
        sort_kernel,
        in_specs=[SMEM] + [VMEM] * 3,
        out_specs=[VMEM] * 4,
        out_shape=[
            like(tok, col // 2),
            like(tok, col // 2),
            like(first.shape[0], RANK),
            like(first.shape[0], RANK),
        ],
        compiler_params=kernel_params(),
        cost_estimate=pl.CostEstimate(flops=2**28, bytes_accessed=2**24, transcendentals=0),
    )(me, go, first, second)


OVER_TOKENS = (((0,), (0,)), ((), ()))


def payload_kernel(
    dims, me_ref, owners_ref, near_ref, far_ref, mine_ref, co_ref, out_ref, proj_ref
):
    chips, pairs, piece, per_block, slots, _ = dims
    share = pairs * piece
    half = chips // per_block
    held = slots * FC
    core = me_ref[0] & 1
    chip = me_ref[0] >> 1
    ids_row = owners_ref[...]
    slot_row = plane_slots(ids_row)
    frags = ids_row.shape[1]
    at = iota((chips * share, 1), 0)
    k_of, p_of, r_of = at // share, (at // piece) % pairs, at % piece
    frag = (core + 2 * p_of) * per_block + k_of // half
    base = ((ids_row & 1) != core).astype(jnp.int32) * (SQUARE * held) + slot_row * FC
    base += (in_square(ids_row >> 1)[0] ^ in_square(chip)[0]) * held
    rows = jnp.sum(jnp.where(frag == iota((1, frags), 1), base, 0), axis=1, keepdims=True)
    rows = rows + (k_of % half) * piece + r_of
    cols = iota((1, SQUARE * held), 1)
    hot = jnp.where(rows == cols, 1.0, 0.0).astype(bf16)
    hot_far = jnp.where(rows == cols + SQUARE * held, 1.0, 0.0).astype(bf16)
    old = jnp.dot(hot, near_ref[...], preferred_element_type=f32)
    old += jnp.dot(hot_far, far_ref[...], preferred_element_type=f32)
    old = old.astype(bf16).reshape(chips, pairs, piece, near_ref.shape[1])
    for p in range(pairs):
        out_ref[:, share:, p * old.shape[3] : (p + 1) * old.shape[3]] = old[:, p]
    proj_ref[...] = lax.dot_general(
        mine_ref[...], co_ref[...], OVER_TOKENS, preferred_element_type=f32
    )


def project_kernel(dims, other_ref, co_other_ref, proj_ref, part_ref, out_ref):
    chips, pairs, piece, _, _, scale = dims
    proj = proj_ref[...] + lax.dot_general(
        other_ref[...], co_other_ref[...], OVER_TOKENS, preferred_element_type=f32
    )
    proj = (proj * scale).astype(bf16).reshape(pairs, chips, piece, RANK)
    for p in range(pairs):
        out_ref[:, p * piece : (p + 1) * piece, :] = proj[p]


def factor_kernel(dims, me_ref, owners_ref, got_ref, factor_ref, grad_ref):
    chips, pairs, piece, per_block, _, _ = dims
    share = pairs * piece
    core = me_ref[0] & 1
    chip = me_ref[0] >> 1
    ids_row = owners_ref[...]
    grad = jnp.zeros((share, RANK), f32)
    for k in range(chips):
        grad += got_ref[k, :share, :].astype(f32)
    width = RANK // SQUARE
    parts = []
    for p in range(pairs):
        frag = (core + 2 * p) * per_block + chip // (chips // per_block)
        sender = jnp.where(iota(ids_row.shape, 1) == frag, ids_row, 0)
        square = in_square(jnp.sum(sender, axis=1, keepdims=True) >> 1)[1]
        old = [jnp.zeros((piece, 2 * width), f32) for _ in range(SQUARE)]
        for k in range(chips):
            place, number = in_square(k)
            sent = got_ref[k, share:, 2 * p * width : (2 * p + 2) * width].astype(f32)
            old[place] = jnp.where(square == number, sent, old[place])
        parts.append(old)
    first, second = (
        jnp.concatenate(
            [
                jnp.concatenate([o[:, n * width : (n + 1) * width] for o in old], axis=1)
                for old in parts
            ],
            axis=0,
        )
        for n in range(2)
    )
    first = first_keep * first + first_take * grad
    second = second_keep * second + second_take * grad * grad
    factor = (first / (jnp.sqrt(second) + adam_eps)).astype(bf16)
    for m in range(factor_ref.shape[0]):
        factor_ref[m] = factor
    grad_ref[...] = grad.astype(bf16)


def update_kernel(piece, basis_ref, last_ref, out_ref, done, sems):
    step, block = done.shape[1:]
    chosen = last_ref[:, :piece, :].reshape(block, RANK)
    copies = []
    for j in range(STEPS):
        at = slice(j * step, (j + 1) * step)
        update = lax.dot_general(
            basis_ref[at, :], chosen, (((1,), (1,)), ((), ())), preferred_element_type=f32
        )
        done[j] = (update * math.sqrt(FF / RANK)).astype(bf16)
        copies.append(pltpu.make_async_copy(done.at[j], out_ref.at[at, :], sems.at[j]))
        copies[-1].start()
    for copy in copies:
        copy.wait()


def update_call(basis, last, block, piece):
    rows = basis.shape[0]
    return pl.pallas_call(
        functools.partial(update_kernel, piece),
        in_specs=[VMEM, VMEM],
        out_specs=pl.BlockSpec(memory_space=pl.ANY),
        out_shape=jax.ShapeDtypeStruct((rows, block), bf16),
        scratch_shapes=[
            pltpu.VMEM((STEPS, rows // STEPS, block), bf16),
            pltpu.SemaphoreType.DMA((STEPS,)),
        ],
        compiler_params=kernel_params(),
    )(basis, last)


def owner_kernel(
    dims, me_ref, owners_ref, first_ref, second_ref, sums_ref, sums_other_ref, first_out, second_out
):
    chips, pairs, piece, per_block, slots = dims
    share = pairs * piece
    half = chips // per_block
    me = me_ref[0]
    ids_row = owners_ref[...]
    slot_row = plane_slots(ids_row)
    frags = ids_row.shape[1]
    at = iota((slots * FC, 1), 0)
    within = at % FC
    own = (ids_row == me) & (slot_row == at // FC)
    live = jnp.sum(own.astype(jnp.int32), axis=1, keepdims=True) > 0
    source = jnp.sum(jnp.where(own, iota((1, frags), 1), 0), axis=1, keepdims=True)
    b = source // per_block
    row = ((source % per_block) * half + within // piece) * share + (b // 2) * piece + within % piece
    row = jnp.where(live, row + (b % 2 != (me & 1)).astype(jnp.int32) * (chips * share), -1)
    cols = iota((1, chips * share), 1)
    hot = jnp.where(row == cols, 1.0, 0.0).astype(bf16)
    hot_other = jnp.where(row == cols + chips * share, 1.0, 0.0).astype(bf16)
    g = jnp.dot(hot, sums_ref[...], preferred_element_type=f32)
    g += jnp.dot(hot_other, sums_other_ref[...], preferred_element_type=f32)
    first, second = first_ref[...], second_ref[...]
    first_out[...] = jnp.where(live, first_keep * first + first_take * g, first)
    second_out[...] = jnp.where(live, second_keep * second + second_take * g * g, second)


def over(exchange, x, *rest):
    x, rest = lax.optimization_barrier((x, rest))
    return lax.optimization_barrier((exchange(x), rest))


def body(hidden, grad_out, basis, owners, first_moment, second_moment):
    owner_count = lax.axis_size("dp")
    planes = lax.axis_size("mp")
    chips = owner_count // 2
    tok, col = grad_out.shape
    slots = first_moment.shape[0] // FC
    frags = owners.shape[0]
    block = col * planes // owner_count
    per_block = block // FC
    piece = block // chips
    pairs = col // block // 2
    share = pairs * piece
    scale = 1.0 / math.sqrt(tok * owner_count)
    same_core = [[2 * k + c for k in range(chips)] for c in range(2)]
    swap = [(i, i ^ 1) for i in range(owner_count)]
    next_x = [(i, i ^ 2) for i in range(owner_count)]
    next_y = [(i, i ^ 8) for i in range(owner_count)]

    def other_core(x):
        return lax.ppermute(x, "dp", swap)

    def over_chips(x):
        return lax.all_to_all(x, "dp", 0, 0, axis_index_groups=same_core, tiled=True)

    def over_planes(x):
        return lax.all_to_all(x, "mp", 0, 0, tiled=True)

    me = lax.axis_index("dp").reshape(1)
    owners = owners.reshape(1, frags)

    even, odd = slice(0, None, 2), slice(1, None, 2)
    early, half = RANK // SQUARE, RANK // 2
    part = coeffs_call(hidden, basis)
    part, me, grad_out, first, second = lax.optimization_barrier(
        (part, me, grad_out, first_moment, second_moment)
    )
    go_mine, go_theirs, keep, send = sort_call(me, grad_out, first, second)
    got_x = lax.ppermute(send[:, :early], "dp", next_x[even])
    part, keep, send, got_x, go_theirs = lax.optimization_barrier((part, keep, send, got_x, go_theirs))
    part = over_planes(part)
    go_other = other_core(go_theirs)
    got_x = jnp.concatenate([got_x, lax.ppermute(send[:, early:], "dp", next_x[even])], axis=1)
    got_x = got_x + lax.ppermute(send, "dp", next_x[odd])
    part, keep, got_x, go_mine, go_other, me, owners = lax.optimization_barrier(
        (part, keep, got_x, go_mine, go_other, me, owners)
    )
    part = part.reshape(planes, tok // planes, RANK)
    mine = jnp.sum(part.astype(f32), axis=0).astype(bf16)
    mine = jnp.broadcast_to(mine[None], part.shape).reshape(tok, RANK)
    coeffs = over_planes(mine)
    near = jnp.concatenate([keep, got_x], axis=0)
    got_y = lax.ppermute(near[:, half:], "dp", next_y)
    near = jnp.concatenate([near[:, :half], got_y], axis=0)
    far = other_core(near)
    coeffs, near, far, go_mine, go_other, me, owners = lax.optimization_barrier(
        (coeffs, near, far, go_mine, go_other, me, owners)
    )
    coeffs_other = other_core(coeffs)

    dims = (chips, pairs, piece, per_block, slots, scale)
    payload_shape = jax.ShapeDtypeStruct((chips, share + piece, RANK), bf16)
    payload, proj = pl.pallas_call(
        functools.partial(payload_kernel, dims),
        in_specs=[SMEM] + [VMEM] * 5,
        out_specs=[VMEM, VMEM],
        out_shape=[payload_shape, jax.ShapeDtypeStruct((pairs * block, RANK), f32)],
        compiler_params=kernel_params(),
    )(me, owners, near, far, go_mine, coeffs)
    payload = pl.pallas_call(
        functools.partial(project_kernel, dims),
        in_specs=[VMEM] * 4,
        out_specs=VMEM,
        out_shape=payload_shape,
        input_output_aliases={3: 0},
        compiler_params=kernel_params(),
    )(go_other, coeffs_other, proj, payload)
    got, (me, owners) = over(over_chips, payload, me, owners)
    factor, grad = pl.pallas_call(
        functools.partial(factor_kernel, dims),
        in_specs=[SMEM] + [VMEM] * 2,
        out_specs=[VMEM, VMEM],
        out_shape=[
            jax.ShapeDtypeStruct((planes, share, RANK), bf16),
            jax.ShapeDtypeStruct((share, RANK), bf16),
        ],
        compiler_params=kernel_params(),
    )(me, owners, got)

    spread, (grad,) = over(over_planes, factor, grad)
    spread = spread.reshape(chips, piece, RANK)
    grad = jnp.broadcast_to(grad[None], (chips, share, RANK))
    last, (me, owners, first_moment, second_moment) = over(
        over_chips,
        jnp.concatenate([spread, grad], axis=1),
        me,
        owners,
        first_moment,
        second_moment,
    )
    sums = last[:, piece:].reshape(chips * share, RANK)
    sums_other = other_core(sums)
    update = update_call(basis, last, block, piece)

    like = jax.ShapeDtypeStruct(first_moment.shape, f32)
    new_first, new_second = pl.pallas_call(
        functools.partial(owner_kernel, dims[:5]),
        in_specs=[SMEM] + [VMEM] * 5,
        out_specs=[VMEM, VMEM],
        out_shape=[like, like],
        compiler_params=kernel_params(),
    )(me, owners, first_moment, second_moment, sums, sums_other)
    return (update, new_first, new_second)


def solution(mesh):
    placed = (
        P("dp", "mp"),
        P("dp", "mp"),
        P("mp", None),
        P("mp", None),
        P(("dp", "mp"), None),
        P(("dp", "mp"), None),
    )
    return jax.shard_map(
        body,
        mesh=mesh,
        in_specs=placed,
        out_specs=(P("mp", "dp"), P(("dp", "mp"), None), P(("dp", "mp"), None)),
        check_vma=False,
    )
```

```python
import functools
import math

import jax
import jax.numpy as jnp
from jax import lax
from jax.experimental import pallas as pl
from jax.experimental.pallas import tpu as pltpu
from jax.sharding import PartitionSpec as P

FF = 28672
RANK = 512
FC = 32
STEPS = 7
SQUARE = 4

first_keep = 0.9
first_take = 0.1
second_keep = 0.95
second_take = 0.05
adam_eps = 1e-08

bf16 = jnp.bfloat16
f32 = jnp.float32
VMEM = pl.BlockSpec(memory_space=pltpu.VMEM)
SMEM = pl.BlockSpec(memory_space=pltpu.SMEM)


def iota(shape, dim):
    return lax.broadcasted_iota(jnp.int32, shape, dim)


def kernel_params(mib=16):
    return pltpu.CompilerParams(vmem_limit_bytes=mib * 2**20)


def plane_slots(ids_row):
    n = ids_row.shape[1]
    f0, f1 = iota((n, n), 0), iota((n, n), 1)
    ids_col = jnp.sum(jnp.where(f0 == f1, ids_row, 0), axis=1, keepdims=True)
    same = ids_col == ids_row
    return jnp.sum((same & (f0 < f1)).astype(jnp.int32), axis=0, keepdims=True)


def in_square(chip):
    return (chip & 1) + 2 * ((chip >> 2) & 1), ((chip >> 1) & 1) + 2 * (chip >> 3)


def coeffs_kernel(hidden_ref, basis_ref, part_ref, hidden, basis, total, sems):
    step = hidden.shape[2]

    def chunk(j):
        at = slice(j * step, (j + 1) * step)
        return (
            pltpu.make_async_copy(hidden_ref.at[:, at], hidden.at[j], sems.at[2 * j]),
            pltpu.make_async_copy(basis_ref.at[at, :], basis.at[j], sems.at[2 * j + 1]),
        )

    chunks = [chunk(j) for j in range(STEPS)]
    for pair in chunks:
        for copy in pair:
            copy.start()
    for j in range(STEPS):
        for copy in chunks[j]:
            copy.wait()
        term = jnp.dot(hidden[j], basis[j], preferred_element_type=f32)
        if j == 0:
            total[...] = term
        elif j < STEPS - 1:
            total[...] += term
        else:
            part_ref[...] = (total[...] + term).astype(bf16)


def coeffs_call(hidden, basis):
    tok, ff = hidden.shape
    step = ff // STEPS
    return pl.pallas_call(
        coeffs_kernel,
        in_specs=[pl.BlockSpec(memory_space=pl.ANY)] * 2,
        out_specs=VMEM,
        out_shape=jax.ShapeDtypeStruct((tok, RANK), bf16),
        scratch_shapes=[
            pltpu.VMEM((STEPS, tok, step), bf16),
            pltpu.VMEM((STEPS, step, RANK), bf16),
            pltpu.VMEM((tok, RANK), f32),
            pltpu.SemaphoreType.DMA((2 * STEPS,)),
        ],
        compiler_params=kernel_params(56),
    )(hidden, basis)


def sort_kernel(me_ref, go_ref, first_ref, second_ref, mine_ref, other_ref, keep_ref, send_ref):
    even = (me_ref[0] & 1) == 0
    width = go_ref.shape[1] // 4
    for p in range(2):
        low = go_ref[:, (2 * p) * width : (2 * p + 1) * width]
        high = go_ref[:, (2 * p + 1) * width : (2 * p + 2) * width]
        mine_ref[:, p * width : (p + 1) * width] = jnp.where(even, low, high)
        other_ref[:, p * width : (p + 1) * width] = jnp.where(even, high, low)
    place = in_square(me_ref[0] >> 1)[0]
    width = RANK // SQUARE
    for n, ref in enumerate((first_ref, second_ref)):
        old = [ref[:, q * width : (q + 1) * width].astype(bf16) for q in range(SQUARE)]
        for d, out in enumerate((keep_ref, send_ref)):
            for e in range(2):
                at = slice((2 * e + n) * width, (2 * e + n + 1) * width)
                q = place ^ (d + 2 * e)
                low = jnp.where((q & 1) == 0, old[0], old[1])
                high = jnp.where((q & 1) == 0, old[2], old[3])
                out[:, at] = jnp.where(q < 2, low, high)


def sort_call(me, go, first, second):
    tok, col = go.shape
    like = lambda *shape: jax.ShapeDtypeStruct(shape, bf16)
    return pl.pallas_call(
        sort_kernel,
        in_specs=[SMEM] + [VMEM] * 3,
        out_specs=[VMEM] * 4,
        out_shape=[
            like(tok, col // 2),
            like(tok, col // 2),
            like(first.shape[0], RANK),
            like(first.shape[0], RANK),
        ],
        compiler_params=kernel_params(),
        cost_estimate=pl.CostEstimate(flops=2**28, bytes_accessed=2**24, transcendentals=0),
    )(me, go, first, second)


def spread_kernel(part_ref, out_ref, total, sems):
    total[...] = jnp.sum(part_ref[...].astype(f32), axis=0).astype(bf16)
    copies = [
        pltpu.make_async_copy(total, out_ref.at[m], sems.at[m]) for m in range(out_ref.shape[0])
    ]
    for copy in copies:
        copy.start()
    for copy in copies:
        copy.wait()


def spread_call(part):
    return pl.pallas_call(
        spread_kernel,
        in_specs=[VMEM],
        out_specs=pl.BlockSpec(memory_space=pl.ANY),
        out_shape=jax.ShapeDtypeStruct(part.shape, bf16),
        scratch_shapes=[
            pltpu.VMEM(part.shape[1:], bf16),
            pltpu.SemaphoreType.DMA((part.shape[0],)),
        ],
        compiler_params=kernel_params(),
    )(part)


OVER_TOKENS = (((0,), (0,)), ((), ()))


def payload_kernel(
    dims, me_ref, owners_ref, near_ref, far_ref, mine_ref, co_ref, out_ref, proj_ref
):
    chips, pairs, piece, per_block, slots, _ = dims
    share = pairs * piece
    half = chips // per_block
    held = slots * FC
    core = me_ref[0] & 1
    chip = me_ref[0] >> 1
    ids_row = owners_ref[...]
    slot_row = plane_slots(ids_row)
    frags = ids_row.shape[1]
    at = iota((chips * share, 1), 0)
    k_of, p_of, r_of = at // share, (at // piece) % pairs, at % piece
    frag = (core + 2 * p_of) * per_block + k_of // half
    base = ((ids_row & 1) != core).astype(jnp.int32) * (SQUARE * held) + slot_row * FC
    base += (in_square(ids_row >> 1)[0] ^ in_square(chip)[0]) * held
    rows = jnp.sum(jnp.where(frag == iota((1, frags), 1), base, 0), axis=1, keepdims=True)
    rows = rows + (k_of % half) * piece + r_of
    cols = iota((1, SQUARE * held), 1)
    hot = jnp.where(rows == cols, 1.0, 0.0).astype(bf16)
    hot_far = jnp.where(rows == cols + SQUARE * held, 1.0, 0.0).astype(bf16)
    old = jnp.dot(hot, near_ref[...], preferred_element_type=f32)
    old += jnp.dot(hot_far, far_ref[...], preferred_element_type=f32)
    old = old.astype(bf16).reshape(chips, pairs, piece, near_ref.shape[1])
    for p in range(pairs):
        out_ref[:, share:, p * old.shape[3] : (p + 1) * old.shape[3]] = old[:, p]
    proj_ref[...] = lax.dot_general(
        mine_ref[...], co_ref[...], OVER_TOKENS, preferred_element_type=f32
    )


def project_kernel(dims, other_ref, co_other_ref, proj_ref, part_ref, out_ref):
    chips, pairs, piece, _, _, scale = dims
    proj = proj_ref[...] + lax.dot_general(
        other_ref[...], co_other_ref[...], OVER_TOKENS, preferred_element_type=f32
    )
    proj = (proj * scale).astype(bf16).reshape(pairs, chips, piece, RANK)
    for p in range(pairs):
        out_ref[:, p * piece : (p + 1) * piece, :] = proj[p]


def factor_kernel(dims, me_ref, owners_ref, got_ref, factor_ref, grad_ref):
    chips, pairs, piece, per_block, _, _ = dims
    share = pairs * piece
    core = me_ref[0] & 1
    chip = me_ref[0] >> 1
    ids_row = owners_ref[...]
    grad = jnp.zeros((share, RANK), f32)
    for k in range(chips):
        grad += got_ref[k, :share, :].astype(f32)
    width = RANK // SQUARE
    parts = []
    for p in range(pairs):
        frag = (core + 2 * p) * per_block + chip // (chips // per_block)
        sender = jnp.where(iota(ids_row.shape, 1) == frag, ids_row, 0)
        square = in_square(jnp.sum(sender, axis=1, keepdims=True) >> 1)[1]
        old = [jnp.zeros((piece, 2 * width), f32) for _ in range(SQUARE)]
        for k in range(chips):
            place, number = in_square(k)
            sent = got_ref[k, share:, 2 * p * width : (2 * p + 2) * width].astype(f32)
            old[place] = jnp.where(square == number, sent, old[place])
        parts.append(old)
    first, second = (
        jnp.concatenate(
            [
                jnp.concatenate([o[:, n * width : (n + 1) * width] for o in old], axis=1)
                for old in parts
            ],
            axis=0,
        )
        for n in range(2)
    )
    first = first_keep * first + first_take * grad
    second = second_keep * second + second_take * grad * grad
    factor = (first / (jnp.sqrt(second) + adam_eps)).astype(bf16)
    for m in range(factor_ref.shape[0]):
        factor_ref[m] = factor
    grad_ref[...] = grad.astype(bf16)


def update_kernel(piece, basis_ref, last_ref, out_ref, done, sems):
    step, block = done.shape[1:]
    chosen = last_ref[:, :piece, :].reshape(block, RANK)
    copies = []
    for j in range(STEPS):
        at = slice(j * step, (j + 1) * step)
        update = lax.dot_general(
            basis_ref[at, :], chosen, (((1,), (1,)), ((), ())), preferred_element_type=f32
        )
        done[j] = (update * math.sqrt(FF / RANK)).astype(bf16)
        copies.append(pltpu.make_async_copy(done.at[j], out_ref.at[at, :], sems.at[j]))
        copies[-1].start()
    for copy in copies:
        copy.wait()


def update_call(basis, last, block, piece):
    rows = basis.shape[0]
    return pl.pallas_call(
        functools.partial(update_kernel, piece),
        in_specs=[VMEM, VMEM],
        out_specs=pl.BlockSpec(memory_space=pl.ANY),
        out_shape=jax.ShapeDtypeStruct((rows, block), bf16),
        scratch_shapes=[
            pltpu.VMEM((STEPS, rows // STEPS, block), bf16),
            pltpu.SemaphoreType.DMA((STEPS,)),
        ],
        compiler_params=kernel_params(),
    )(basis, last)


def owner_kernel(
    dims, me_ref, owners_ref, first_ref, second_ref, sums_ref, sums_other_ref, first_out, second_out
):
    chips, pairs, piece, per_block, slots = dims
    share = pairs * piece
    half = chips // per_block
    me = me_ref[0]
    ids_row = owners_ref[...]
    slot_row = plane_slots(ids_row)
    frags = ids_row.shape[1]
    at = iota((slots * FC, 1), 0)
    within = at % FC
    own = (ids_row == me) & (slot_row == at // FC)
    live = jnp.sum(own.astype(jnp.int32), axis=1, keepdims=True) > 0
    source = jnp.sum(jnp.where(own, iota((1, frags), 1), 0), axis=1, keepdims=True)
    b = source // per_block
    row = ((source % per_block) * half + within // piece) * share + (b // 2) * piece + within % piece
    row = jnp.where(live, row + (b % 2 != (me & 1)).astype(jnp.int32) * (chips * share), -1)
    cols = iota((1, chips * share), 1)
    hot = jnp.where(row == cols, 1.0, 0.0).astype(bf16)
    hot_other = jnp.where(row == cols + chips * share, 1.0, 0.0).astype(bf16)
    g = jnp.dot(hot, sums_ref[...], preferred_element_type=f32)
    g += jnp.dot(hot_other, sums_other_ref[...], preferred_element_type=f32)
    first, second = first_ref[...], second_ref[...]
    first_out[...] = jnp.where(live, first_keep * first + first_take * g, first)
    second_out[...] = jnp.where(live, second_keep * second + second_take * g * g, second)


def over(exchange, x, *rest):
    x, rest = lax.optimization_barrier((x, rest))
    return lax.optimization_barrier((exchange(x), rest))


def body(hidden, grad_out, basis, owners, first_moment, second_moment):
    owner_count = lax.axis_size("dp")
    planes = lax.axis_size("mp")
    chips = owner_count // 2
    tok, col = grad_out.shape
    slots = first_moment.shape[0] // FC
    frags = owners.shape[0]
    block = col * planes // owner_count
    per_block = block // FC
    piece = block // chips
    pairs = col // block // 2
    share = pairs * piece
    scale = 1.0 / math.sqrt(tok * owner_count)
    same_core = [[2 * k + c for k in range(chips)] for c in range(2)]
    swap = [(i, i ^ 1) for i in range(owner_count)]
    next_x = [(i, i ^ 2) for i in range(owner_count)]
    next_y = [(i, i ^ 8) for i in range(owner_count)]

    def other_core(x):
        return lax.ppermute(x, "dp", swap)

    def over_chips(x):
        return lax.all_to_all(x, "dp", 0, 0, axis_index_groups=same_core, tiled=True)

    def over_planes(x):
        return lax.all_to_all(x, "mp", 0, 0, tiled=True)

    me = lax.axis_index("dp").reshape(1)
    owners = owners.reshape(1, frags)

    even, odd = slice(0, None, 2), slice(1, None, 2)
    early, half = RANK // SQUARE, RANK // 2
    part = coeffs_call(hidden, basis)
    part, me, grad_out, first, second = lax.optimization_barrier(
        (part, me, grad_out, first_moment, second_moment)
    )
    go_mine, go_theirs, keep, send = sort_call(me, grad_out, first, second)
    got_x = lax.ppermute(send[:, :early], "dp", next_x[even])
    part, keep, send, got_x = lax.optimization_barrier((part, keep, send, got_x))
    part = over_planes(part)
    got_x = jnp.concatenate([got_x, lax.ppermute(send[:, early:], "dp", next_x[even])], axis=1)
    part, keep, got_x, go_mine, go_theirs, me, owners = lax.optimization_barrier(
        (part, keep, got_x, go_mine, go_theirs, me, owners)
    )
    mine = spread_call(part.reshape(planes, tok // planes, RANK)).reshape(tok, RANK)
    coeffs = over_planes(mine)
    got_x = got_x + lax.ppermute(send, "dp", next_x[odd])
    near = jnp.concatenate([keep, got_x], axis=0)
    got_y = lax.ppermute(near[:, half:], "dp", next_y)
    near = jnp.concatenate([near[:, :half], got_y], axis=0)
    near, go_theirs = lax.optimization_barrier((near, go_theirs))
    far = other_core(near)
    go_other = other_core(go_theirs)
    coeffs, near, far, go_mine, go_other, me, owners = lax.optimization_barrier(
        (coeffs, near, far, go_mine, go_other, me, owners)
    )
    coeffs_other = other_core(coeffs)

    dims = (chips, pairs, piece, per_block, slots, scale)
    payload_shape = jax.ShapeDtypeStruct((chips, share + piece, RANK), bf16)
    payload, proj = pl.pallas_call(
        functools.partial(payload_kernel, dims),
        in_specs=[SMEM] + [VMEM] * 5,
        out_specs=[VMEM, VMEM],
        out_shape=[payload_shape, jax.ShapeDtypeStruct((pairs * block, RANK), f32)],
        compiler_params=kernel_params(),
    )(me, owners, near, far, go_mine, coeffs)
    payload = pl.pallas_call(
        functools.partial(project_kernel, dims),
        in_specs=[VMEM] * 4,
        out_specs=VMEM,
        out_shape=payload_shape,
        input_output_aliases={3: 0},
        compiler_params=kernel_params(),
    )(go_other, coeffs_other, proj, payload)
    got, (me, owners) = over(over_chips, payload, me, owners)
    factor, grad = pl.pallas_call(
        functools.partial(factor_kernel, dims),
        in_specs=[SMEM] + [VMEM] * 2,
        out_specs=[VMEM, VMEM],
        out_shape=[
            jax.ShapeDtypeStruct((planes, share, RANK), bf16),
            jax.ShapeDtypeStruct((share, RANK), bf16),
        ],
        compiler_params=kernel_params(),
    )(me, owners, got)

    spread, (grad,) = over(over_planes, factor, grad)
    spread = spread.reshape(chips, piece, RANK)
    grad = jnp.broadcast_to(grad[None], (chips, share, RANK))
    last, (me, owners, first_moment, second_moment) = over(
        over_chips,
        jnp.concatenate([spread, grad], axis=1),
        me,
        owners,
        first_moment,
        second_moment,
    )
    sums = last[:, piece:].reshape(chips * share, RANK)
    sums_other = other_core(sums)
    update = update_call(basis, last, block, piece)

    like = jax.ShapeDtypeStruct(first_moment.shape, f32)
    new_first, new_second = pl.pallas_call(
        functools.partial(owner_kernel, dims[:5]),
        in_specs=[SMEM] + [VMEM] * 5,
        out_specs=[VMEM, VMEM],
        out_shape=[like, like],
        compiler_params=kernel_params(),
    )(me, owners, first_moment, second_moment, sums, sums_other)
    return (update, new_first, new_second)


def solution(mesh):
    placed = (
        P("dp", "mp"),
        P("dp", "mp"),
        P("mp", None),
        P("mp", None),
        P(("dp", "mp"), None),
        P(("dp", "mp"), None),
    )
    return jax.shard_map(
        body,
        mesh=mesh,
        in_specs=placed,
        out_specs=(P("mp", "dp"), P(("dp", "mp"), None), P(("dp", "mp"), None)),
        check_vma=False,
    )
```
